128 devices in a mesh: dp: 16 (over y, x_hi, core), mp: 8 (over z, x_lo).
Axes of the slice: x: 4 (x_hi: 2, x_lo: 2; x = x_hi * 2 + x_lo), y: 4, z: 4, core: 2. Of those that a mesh axis runs over, the one named last changes fastest.
Arguments:
- tokens: bfloat16 [2, 8192, 1024], P(None, ('dp', 'mp')), may hold values from -6 to 6
- segment_ids: int32 [2, 8192], P(None, 'dp'), may hold values from 0 to 3, as said below
- cotangent: bfloat16 [2, 8192, 1024], P(None, ('dp', 'mp')), may hold values from -6 to 6
- w_query: bfloat16 [1024, 1024], P('dp', 'mp'), may hold values from -0.1875 to 0.1875
- w_key: bfloat16 [1024, 512], P('dp', 'mp'), may hold values from -0.1875 to 0.1875
- w_value: bfloat16 [1024, 512], P('dp', 'mp'), may hold values from -0.1875 to 0.1875
- w_out: bfloat16 [1024, 1024], P('mp', 'dp'), may hold values from -1.5 to 1.5
- w_gate: bfloat16 [1024, 4608], P('dp', 'mp'), may hold values from -0.1875 to 0.1875
- w_up: bfloat16 [1024, 4608], P('dp', 'mp'), may hold values from -0.1875 to 0.1875
- w_down: bfloat16 [4608, 1024], P('mp', 'dp'), may hold values from -0.09375 to 0.09375
- norm_gain: float32 [1024], replicated, may hold values from 0.5 to 1.5
- ffn_gain: float32 [1024], replicated, may hold values from 0.5 to 1.5
- query_gain: float32 [64], replicated, may hold values from 0.1 to 1.9
- key_gain: float32 [64], replicated, may hold values from 0.1 to 1.9
Outputs:
- output: bfloat16 [2, 8192, 1024], P(None, ('dp', 'mp'))
- input_grad: bfloat16 [2, 8192, 1024], P(None, ('dp', 'mp'))
- grad_query: float32 [1024, 1024], P('dp', 'mp')
- grad_key: float32 [1024, 512], P('dp', 'mp')
- grad_value: float32 [1024, 512], P('dp', 'mp')
- grad_out: float32 [1024, 1024], P('mp', 'dp')
- grad_gate: float32 [1024, 4608], P('dp', 'mp')
- grad_up: float32 [1024, 4608], P('dp', 'mp')
- grad_down: float32 [4608, 1024], P('mp', 'dp')
- grad_norm: float32 [1024], replicated
- grad_ffn_norm: float32 [1024], replicated
- grad_query_gain: float32 [64], replicated
- grad_key_gain: float32 [64], replicated
The draws below stay inside these ranges and needn't reach their ends.
Inputs may be any that keep to these rules, and one draw needn't show every extreme that they name: `segment_ids`: in each micro-batch each data group's 512 tokens hold 1 to 4 whole sequences, numbered 0, 1, ... in order; in each micro-batch some group holds a single sequence and some group holds four.
All inputs are finite; a program needn't handle non-finite values.
Results may differ from the reference program's by a relative error of at most 0.025.
Values may be sent and summed in bfloat16 or wider, within the bound.
No kernel may reach another device: no remote copies, remote signals or barrier semaphores. Data moves between devices by JAX's collectives and lax.ppermute only.
A program may use at most 128 MiB of HBM per device.

```python
import jax
import jax.numpy as jnp
from jax import lax

D = 1024
HQ = 16
KV = 8
HD = 64
FF = 4608
TOK_MB = 64
MICRO = 2
TOKENS_MB = 8192
N_DP = 16
N_MP = 8


def draw_segment_ids(key, part):
    key = jax.random.fold_in(key, 7)
    group = TOK_MB * N_MP
    first, second, third, fourth = jax.random.split(key, 4)
    counts = jax.random.randint(first, (MICRO, N_DP), 0, 4)
    single = jax.random.randint(second, (MICRO,), 0, N_DP)
    offset = jax.random.randint(third, (MICRO,), 1, N_DP)
    fullest = (single + offset) % N_DP
    column = jnp.arange(N_DP)[None, :]
    counts = jnp.where(column == fullest[:, None], 3, counts)
    counts = jnp.where(column == single[:, None], 0, counts)
    keys = jax.random.split(fourth, MICRO * N_DP)
    cuts = jax.vmap(lambda one: jax.random.permutation(one, group - 1)[:3] + 1)(keys).reshape(MICRO, N_DP, 3)
    active = jnp.arange(3)[None, None, :] < counts[:, :, None]
    cuts = jnp.where(active, cuts, group)
    place = jnp.arange(group)[None, None, None, :]
    segment = jnp.sum((place >= cuts[..., None]).astype(jnp.int32), axis=2)
    return segment.reshape(MICRO, N_DP * group).astype(jnp.int32)


def block_levels(own_key, extent, pieces, smallest, largest):
    factor_of, own = 1.0, jax.random.fold_in(own_key, 6)
    for dim, parts in pieces:
        draws = jnp.exp(jax.random.uniform(jax.random.fold_in(own, dim), (parts,), jnp.float32, smallest / len(pieces), largest / len(pieces)))
        factor_of = factor_of * jnp.repeat(draws, extent[dim] // parts).reshape([-1 if axis == dim else 1 for axis in range(len(extent))])
    return factor_of


def noise(own_key, dims, scale, reach, pieces=(), held_as=jnp.bfloat16):
    values = scale * jax.random.normal(own_key, dims, jnp.float32)
    if pieces:
        values = values * block_levels(own_key, dims, pieces, -0.22, 0.18)
    return jnp.clip(values, -reach, reach).astype(held_as)


def setup_inputs(seed: int = 0) -> dict:
    arg_keys = jax.random.split(jax.random.key(seed), 15)
    return {
        "tokens": noise(arg_keys[0], (MICRO, TOKENS_MB, D), 1.0, 6.0, ((1, 128),)),
        "segment_ids": draw_segment_ids(jax.random.fold_in(arg_keys[14], 71), 0),
        "cotangent": noise(arg_keys[2], (MICRO, TOKENS_MB, D), 1.0, 6.0, ((1, 128),)),
        "w_query": noise(arg_keys[3], (D, HQ * HD), D ** -0.5, 0.1875, ((0, 16), (1, 8))),
        "w_key": noise(arg_keys[4], (D, KV * HD), D ** -0.5, 0.1875, ((0, 16), (1, 8))),
        "w_value": noise(arg_keys[5], (D, KV * HD), D ** -0.5, 0.1875, ((0, 16), (1, 8))),
        "w_out": noise(arg_keys[6], (HQ * HD, D), (HQ * HD // 64) ** -0.5, 1.5, ((0, 8), (1, 16))),
        "w_gate": noise(arg_keys[7], (D, FF), D ** -0.5, 0.1875, ((0, 16), (1, 8))),
        "w_up": noise(arg_keys[8], (D, FF), D ** -0.5, 0.1875, ((0, 16), (1, 8))),
        "w_down": noise(arg_keys[9], (FF, D), FF ** -0.5, 0.09375, ((0, 8), (1, 16))),
        "norm_gain": jnp.clip(1.0 + 0.1 * jax.random.normal(arg_keys[10], (D,), jnp.float32), 0.5, 1.5),
        "ffn_gain": jnp.clip(1.0 + 0.1 * jax.random.normal(arg_keys[11], (D,), jnp.float32), 0.5, 1.5),
        "query_gain": jnp.clip(1.0 + 0.18 * jax.random.normal(arg_keys[12], (HD,), jnp.float32), 0.1, 1.9),
        "key_gain": jnp.clip(1.0 + 0.18 * jax.random.normal(arg_keys[13], (HD,), jnp.float32), 0.1, 1.9),
    }


eps = 1e-05
rope_base = 1000000.0

@jax.custom_vjp
def low(v):
    return lax.optimization_barrier(v.astype(jnp.bfloat16)).astype(jnp.float32)

@jax.custom_vjp
def low_back(v):
    return v

def low_keep(v):
    return (low(v), None)

def low_pass(kept, grad):
    return (grad,)

def back_keep(v):
    return (v, None)

def back_low(kept, grad):
    return (low(grad),)
low.defvjp(low_keep, low_pass)
low_back.defvjp(back_keep, back_low)

def product(left, right):
    return jnp.dot(left, right, precision=lax.Precision.HIGHEST, preferred_element_type=jnp.float32)

def rms_rows(value, gain):
    return value * lax.rsqrt(lax.optimization_barrier(jnp.mean(value * value, axis=-1, keepdims=True)) + eps) * gain

def rotate(value, cosine, sine):
    half = value.shape[-1] // 2
    turned = jnp.concatenate([-value[..., half:], value[..., :half]], axis=-1)
    return value * cosine + turned * sine

def rope_tables(segment):
    count = segment.shape[0]
    index = jnp.arange(count, dtype=jnp.int32)
    change = jnp.concatenate([jnp.ones((1,), dtype=bool), segment[1:] != segment[:-1]])
    start = lax.cummax(jnp.where(change, index, 0).astype(jnp.int32), axis=0)
    place = (index - start).astype(jnp.float32)
    freq = rope_base ** (-(jnp.arange(HD // 2, dtype=jnp.float32) * 2.0 / HD))
    angle = place[:, None] * freq[None, :]
    angle = jnp.concatenate([angle, angle], axis=-1)
    return (jnp.cos(angle)[:, None, :], jnp.sin(angle)[:, None, :])

def layer(resid, w_query, w_key, w_value, w_out, w_gate, w_up, w_down, norm_gain, ffn_gain, query_gain, key_gain, cosine, sine, allowed):
    group = resid.shape[0]
    normed = low(rms_rows(resid, norm_gain))
    query_raw = low_back(product(normed, w_query)).reshape(group, HQ, HD)
    key_raw = low_back(product(normed, w_key)).reshape(group, KV, HD)
    values = low(low_back(product(normed, w_value))).reshape(group, KV, HD)
    queries = low(rotate(rms_rows(query_raw, query_gain), cosine, sine))
    keys = low(rotate(rms_rows(key_raw, key_gain), cosine, sine))
    repeat = HQ // KV
    block = min(512, group)
    blocks = group // block
    scale = HD ** (-0.5)

    def one_block(item):
        query_block, mask_block = item
        scores = low_back(jnp.einsum('bgrd,kgd->grbk', query_block, keys, precision=lax.Precision.HIGHEST) * scale)
        scores = jnp.where(mask_block[None, None], scores, -1e+30)
        top = lax.optimization_barrier(jnp.max(scores, axis=-1, keepdims=True))
        expo = jnp.exp(scores - top)
        weights = low(expo / lax.optimization_barrier(jnp.sum(expo, axis=-1, keepdims=True)))
        return jnp.einsum('grbk,kgd->bgrd', weights, values, precision=lax.Precision.HIGHEST)
    mixed = lax.map(jax.checkpoint(one_block), (queries.reshape(blocks, block, KV, repeat, HD), allowed.reshape(blocks, block, group)))
    mixed = low(low_back(mixed.reshape(group, HQ * HD)))
    hidden_state = resid + low_back(product(mixed, w_out))
    second = low(rms_rows(hidden_state, ffn_gain))
    gate = low_back(product(second, w_gate))
    up_act = low_back(product(second, w_up))
    inner = low(jax.nn.silu(gate) * up_act)
    return hidden_state + product(inner, w_down)

def reference(tokens, segment_ids, cotangent, w_query, w_key, w_value, w_out, w_gate, w_up, w_down, norm_gain, ffn_gain, query_gain, key_gain):
    group = TOK_MB * N_MP
    count = MICRO * N_DP
    inputs = tokens.astype(jnp.float32).reshape(count, group, D)
    segments = segment_ids.astype(jnp.int32).reshape(count, group)
    upstream = cotangent.astype(jnp.float32).reshape(count, group, D)
    params = tuple((w.astype(jnp.float32) for w in (w_query, w_key, w_value, w_out, w_gate, w_up, w_down, norm_gain, ffn_gain, query_gain, key_gain)))

    def step(totals, item):
        resid, segment, grad_in = item
        cosine, sine = rope_tables(segment)
        index = jnp.arange(group, dtype=jnp.int32)
        allowed = (segment[:, None] == segment[None, :]) & (index[:, None] >= index[None, :])

        def forward(resid, *weights):
            return layer(resid, *weights, cosine, sine, allowed)
        result, pull = jax.vjp(forward, resid, *params)
        grads = pull(grad_in)
        totals = tuple((a + b for a, b in zip(totals, grads[1:])))
        return (totals, (result.astype(jnp.bfloat16), grads[0].astype(jnp.bfloat16)))
    zeros = tuple((jnp.zeros(w.shape, jnp.float32) for w in params))
    totals, (results, input_grads) = lax.scan(step, zeros, (inputs, segments, upstream))
    output = results.reshape(MICRO, TOKENS_MB, D)
    input_grad = input_grads.reshape(MICRO, TOKENS_MB, D)
    return (output, input_grad, totals[0], totals[1], totals[2], totals[3], totals[4], totals[5], totals[6], totals[7], totals[8], totals[9], totals[10])
```

```python
import jax
import jax.numpy as jnp
from jax import lax
from jax.sharding import Mesh, PartitionSpec as P

eps = 1e-05
rope_base = 1000000.0
axes = ("y", "xh", "core", "z", "xl")
plane = ("y", "xh", "xl")
CORE = [(0, 1), (1, 0)]
bf16 = jnp.bfloat16
f32 = jnp.float32


def product(left, right):
    return jnp.dot(left, right, preferred_element_type=jnp.float32)


def product_nt(left, right):
    return lax.dot_general(
        left, right, (((1,), (1,)), ((), ())), preferred_element_type=jnp.float32
    )


def product_tn(left, right):
    return lax.dot_general(
        left, right, (((0,), (0,)), ((), ())), preferred_element_type=jnp.float32
    )


def rms_scale(value):
    return lax.rsqrt(jnp.mean(value * value, axis=-1, keepdims=True) + eps)


def rms_rows(value, gain):
    return value * rms_scale(value) * gain


def rotate(value, cosine, sine):
    half = value.shape[-1] // 2
    turned = jnp.concatenate([-value[..., half:], value[..., :half]], axis=-1)
    return value * cosine + turned * sine


def head_prepare(raw, gain, cosine, sine):
    return rotate(rms_rows(raw, gain), cosine, sine)


def swap(value):
    return lax.ppermute(
        value, ("core", "xl"), [(a * 2 + b, b * 2 + a) for a in range(2) for b in range(2)]
    )


def from_z(value, k):
    return lax.ppermute(value, "z", [(z, (z - k) % 4) for z in range(4)])


def swap_from_z(value, k):
    perm = [
        (a * 8 + z * 2 + b, b * 8 + ((z - k) % 4) * 2 + a)
        for a in range(2)
        for z in range(4)
        for b in range(2)
    ]
    return lax.ppermute(value, ("core", "z", "xl"), perm)


def other_core(value):
    return lax.ppermute(value, "core", CORE)


def gather_swapped(value):
    chain = jnp.concatenate([swap_from_z(value, k) for k in range(4)], axis=1)
    return jnp.concatenate([chain, other_core(chain)], axis=1)


def gather(value):
    chain = jnp.concatenate([value] + [from_z(value, k) for k in (1, 2, 3)], axis=1)
    return jnp.concatenate([chain, other_core(chain)], axis=1)


def scatter_sum(partial):
    half = partial.shape[1] // 2
    block = half // 4
    chain = partial[:, :half] + other_core(partial[:, half:].astype(bf16)).astype(f32)
    total = chain[:, :block]
    low = chain.astype(bf16)
    for k in (1, 2, 3):
        total = total + from_z(low[:, k * block : (k + 1) * block], -k).astype(f32)
    return total


def ordered(value, z, core, axis):
    shape = value.shape
    block = shape[axis] // 8
    v = value.reshape(shape[:axis] + (4, 2, block) + shape[axis + 1 :])
    v = lax.dynamic_slice_in_dim(jnp.concatenate([v, v], axis), z, 4, axis)
    v = lax.dynamic_slice_in_dim(jnp.concatenate([v, v], axis + 1), core, 2, axis + 1)
    return jnp.swapaxes(v, axis, axis + 1).reshape(shape)


def gather_heads(mixed):
    micro, group, cols = mixed.shape
    block = group // 8
    pieces = [mixed] + [from_z(mixed, k) for k in (1, 2, 3)]
    other = [other_core(p) for p in pieces]

    def roll(piece, k, flip):
        p = piece.reshape(micro, 2, 4, block, cols)
        if flip:
            p = p[:, ::-1]
        if k:
            p = jnp.concatenate([p[:, :, 4 - k :], p[:, :, : 4 - k]], axis=2)
        return p.reshape(micro, group, cols)

    return jnp.concatenate(
        [roll(p, k, False) for k, p in enumerate(pieces)]
        + [roll(p, k, True) for k, p in enumerate(other)],
        axis=2,
    )


def all_sum(value):
    value = value + other_core(value)
    for axis in ("z", ("xh", "xl"), "y"):
        value = value + sum(
            lax.ppermute(value, axis, [(i, (i + k) % 4) for i in range(4)]) for k in (1, 2, 3)
        )
    return value


def local(
    tokens,
    segment_ids,
    cotangent,
    w_query,
    w_key,
    w_value,
    w_out,
    w_gate,
    w_up,
    w_down,
    norm_gain,
    ffn_gain,
    query_gain,
    key_gain,
):
    micro, own, width = tokens.shape
    head_size = query_gain.shape[0]
    nq = w_query.shape[1]
    nk = w_key.shape[1]
    heads = nq // head_size
    group = segment_ids.shape[1]
    hidden = w_gate.shape[1]
    scale = head_size ** (-0.5)
    z = lax.axis_index("z")
    core = lax.axis_index("core")

    x_low = gather_swapped(tokens)
    segment = swap(segment_ids)
    w_att = lax.all_gather(
        swap(jnp.concatenate([w_query, w_key, w_value, w_out.T], axis=1)), plane, axis=0, tiled=True
    )
    w_qkv = w_att[:, : nq + 2 * nk]
    w_own = w_att[:, nq + 2 * nk :]
    w_out_t = jnp.concatenate([w_own] + [from_z(w_own, k) for k in (1, 2, 3)], axis=1)
    w_out_t = jnp.concatenate([w_out_t, other_core(w_out_t)], axis=1)
    upstream = gather_swapped(cotangent).reshape(micro * group, width)
    w_ffn = lax.all_gather(
        swap(jnp.concatenate([w_gate, w_up, w_down.T], axis=1)), plane, axis=0, tiled=True
    )
    w_gu = w_ffn[:, : 2 * hidden]
    w_down_t = w_ffn[:, 2 * hidden :]

    index = jnp.arange(group, dtype=jnp.int32)
    change = jnp.concatenate(
        [jnp.ones((micro, 1), dtype=bool), segment[:, 1:] != segment[:, :-1]], axis=1
    )
    start = lax.cummax(jnp.where(change, index, 0), axis=1)
    start = ordered(start, z, core, 1)
    index = ordered(index[None], z, core, 1)
    place = (index - start).astype(f32)
    freq = rope_base ** (-(jnp.arange(head_size // 2, dtype=f32) * 2.0 / head_size))
    angle = place[:, :, None] * freq
    angle = jnp.concatenate([angle, angle], axis=-1)
    cosine, sine = jnp.cos(angle)[:, :, None], jnp.sin(angle)[:, :, None]
    allowed = (start[:, :, None] == start[:, None, :]) & (index[:, :, None] >= index[:, None, :])

    x = x_low.astype(f32).reshape(micro * group, width)
    x_scale = rms_scale(x)
    normed = (x * x_scale * norm_gain).astype(bf16)
    qkv = product(normed, w_qkv).reshape(micro, group, heads + 2, head_size)
    query_raw, key_raw = qkv[:, :, :heads], qkv[:, :, heads : heads + 1]
    values = qkv[:, :, heads + 1].astype(bf16)
    prepare_q = lambda raw, gain: head_prepare(raw, gain, cosine, sine)
    queries, query_pull = jax.vjp(prepare_q, query_raw, query_gain)
    keys, key_pull = jax.vjp(prepare_q, key_raw, key_gain)
    queries = queries.astype(bf16)
    keys = keys[:, :, 0].astype(bf16)
    scores = jnp.einsum("mbrd,mkd->mrbk", queries, keys, preferred_element_type=f32) * scale
    scores = jnp.where(allowed[:, None], scores, -1e30)
    top = jnp.max(scores, axis=-1, keepdims=True)
    expo = jnp.exp(scores - top)
    total = jnp.sum(expo, axis=-1, keepdims=True)
    soft = expo / total
    soft_low = soft.astype(bf16)
    mixed = jnp.einsum("mrbk,mkd->mbrd", soft_low, values, preferred_element_type=f32)
    mixed = mixed.astype(bf16).reshape(micro, group, nq)
    mixed_full = gather_heads(mixed).reshape(micro * group, 8 * nq)
    mixed = mixed.reshape(micro * group, nq)
    state = x + product_nt(mixed_full, w_out_t)
    second = rms_rows(state, ffn_gain).astype(bf16)

    gate_up = product(second, w_gu)
    gate, up = gate_up[:, :hidden], gate_up[:, hidden:]
    sig = 1.0 / (1.0 + jnp.exp(-gate))
    silu = gate * sig
    inner = (silu * up).astype(bf16)
    grad_inner = product(upstream, w_down_t)
    grad_gate_low = (grad_inner * up * sig * (1.0 + gate * (1.0 - sig))).astype(bf16)
    grad_up_low = (grad_inner * silu).astype(bf16)
    grad_gu_low = jnp.concatenate([grad_gate_low, grad_up_low], axis=1)
    grad_second = product_nt(grad_gu_low, w_gu)
    grad_second = scatter_sum(grad_second.reshape(micro, group, width))
    state_own = state.reshape(micro, group, width)[:, :own]
    down = product_nt(inner, w_down_t)
    output = state_own + scatter_sum(down.reshape(micro, group, width))
    output = swap(output.astype(bf16))
    grad_ffn = jnp.concatenate(
        [product_tn(second, grad_gu_low), product_tn(upstream, inner)], axis=1
    ).astype(bf16)
    grad_ffn = lax.psum_scatter(grad_ffn, plane, scatter_dimension=0, tiled=True)
    grad_ffn = swap(grad_ffn).astype(f32)

    _, norm_pull = jax.vjp(rms_rows, state_own, ffn_gain)
    grad_state_norm, grad_ffn_gain = norm_pull(grad_second)
    cotangent_own = upstream.reshape(micro, group, width)[:, :own].astype(f32)
    grad_state = cotangent_own + grad_state_norm
    state_full = gather(grad_state.astype(bf16)).reshape(micro * group, width)

    grad_out = product_tn(state_full, mixed)
    grad_mixed = product(state_full, w_own).astype(bf16).reshape(micro, group, heads, head_size)
    grad_weights = jnp.einsum("mbrd,mkd->mrbk", grad_mixed, values, preferred_element_type=f32)
    center = jnp.sum(soft * grad_weights, axis=-1, keepdims=True)
    grad_scores = (soft * (grad_weights - center)).astype(bf16)
    grad_queries = (
        jnp.einsum("mrbk,mkd->mbrd", grad_scores, keys, preferred_element_type=f32) * scale
    )
    grad_keys = (
        jnp.einsum("mrbk,mbrd->mkd", grad_scores, queries, preferred_element_type=f32) * scale
    )
    grad_values = jnp.einsum("mrbk,mbrd->mkd", soft_low, grad_mixed, preferred_element_type=f32)
    grad_query_raw, grad_qgain = query_pull(grad_queries)
    grad_key_raw, grad_kgain = key_pull(grad_keys[:, :, None])
    qkv_low = jnp.concatenate(
        [
            grad_query_raw.reshape(micro * group, nq).astype(bf16),
            grad_key_raw.reshape(micro * group, nk).astype(bf16),
            grad_values.reshape(micro * group, nk).astype(bf16),
        ],
        axis=1,
    )
    grad_normed = product_nt(qkv_low, w_qkv)
    grad_norm_gain = jnp.sum(grad_normed * x * x_scale, axis=0)
    gains = all_sum(jnp.concatenate([grad_norm_gain, grad_ffn_gain, grad_qgain, grad_kgain]))
    grad_normed = scatter_sum(grad_normed.reshape(micro, group, width))
    grad_att = jnp.concatenate([product_tn(normed, qkv_low), grad_out], axis=1).astype(bf16)
    grad_att = lax.all_to_all(grad_att, plane, 0, 0, tiled=True)
    grad_att = jnp.sum(grad_att.reshape(16, width // 16, -1).astype(f32), axis=0)
    grad_att = swap(grad_att)
    x_own = x.reshape(micro, group, width)[:, :own]
    _, first_pull = jax.vjp(rms_rows, x_own, norm_gain)
    grad_resid_norm, _ = first_pull(grad_normed)
    input_grad = swap((grad_state + grad_resid_norm).astype(bf16))
    split = nq + nk
    return (
        output,
        input_grad,
        grad_att[:, :nq],
        grad_att[:, nq:split],
        grad_att[:, split : split + nk],
        grad_att[:, split + nk :].T,
        grad_ffn[:, :hidden],
        grad_ffn[:, hidden : 2 * hidden],
        grad_ffn[:, 2 * hidden :].T,
        gains[:width],
        gains[width : 2 * width],
        gains[2 * width : 2 * width + head_size],
        gains[2 * width + head_size :],
    )


def solution(mesh):
    inner = Mesh(mesh.devices.reshape(4, 2, 2, 4, 2), axes)
    dp, mp = ("y", "xh", "core"), ("z", "xl")
    rows = P(None, dp + mp, None)
    weight_in = [P(dp, mp)] * 3 + [P(mp, dp)] + [P(dp, mp)] * 2 + [P(mp, dp)]
    return jax.shard_map(
        local,
        mesh=inner,
        in_specs=tuple([rows, P(None, dp), rows] + weight_in + [P()] * 4),
        out_specs=tuple([rows, rows] + weight_in + [P()] * 4),
        check_vma=False,
    )
```

```python
import jax
import jax.numpy as jnp
from jax import lax
from jax.experimental import pallas as pl
from jax.experimental.pallas import tpu as pltpu
from jax.sharding import Mesh, PartitionSpec as P

eps = 1e-05
rope_base = 1000000.0
axes = ("y", "xh", "core", "z", "xl")
plane = ("y", "xh", "xl")
CORE = [(0, 1), (1, 0)]
bf16 = jnp.bfloat16
f32 = jnp.float32


def product(left, right):
    return jnp.dot(left, right, preferred_element_type=jnp.float32)


def product_nt(left, right):
    return lax.dot_general(
        left, right, (((1,), (1,)), ((), ())), preferred_element_type=jnp.float32
    )


def product_tn(left, right):
    return lax.dot_general(
        left, right, (((0,), (0,)), ((), ())), preferred_element_type=jnp.float32
    )


def rms_scale(value):
    return lax.rsqrt(jnp.mean(value * value, axis=-1, keepdims=True) + eps)


def rms_rows(value, gain):
    return value * rms_scale(value) * gain


def swap(value):
    return lax.ppermute(
        value, ("core", "xl"), [(a * 2 + b, b * 2 + a) for a in range(2) for b in range(2)]
    )


def from_z(value, k):
    return lax.ppermute(value, "z", [(z, (z - k) % 4) for z in range(4)])


def swap_from_z(value, k):
    perm = [
        (a * 8 + z * 2 + b, b * 8 + ((z - k) % 4) * 2 + a)
        for a in range(2)
        for z in range(4)
        for b in range(2)
    ]
    return lax.ppermute(value, ("core", "z", "xl"), perm)


def swap_from_x(value, k):
    perm = []
    for xh in range(2):
        for a in range(2):
            for b in range(2):
                x = (xh * 2 + a - k) % 4
                perm.append((xh * 4 + a * 2 + b, (x // 2) * 4 + b * 2 + x % 2))
    return lax.ppermute(value, ("xh", "core", "xl"), perm)


def from_y(value, k):
    return lax.ppermute(value, "y", [(y, (y - k) % 4) for y in range(4)])


def other_core(value):
    return lax.ppermute(value, "core", CORE)


def gather_swapped(value):
    chain = [swap_from_z(value, k) for k in range(4)]
    return chain + [other_core(v) for v in chain]


def gather(value):
    chain = [value] + [from_z(value, k) for k in (1, 2, 3)]
    return chain + [other_core(v) for v in chain]


def ordered(value, z, core, axis):
    shape = value.shape
    block = shape[axis] // 8
    v = value.reshape(shape[:axis] + (4, 2, block) + shape[axis + 1 :])
    v = lax.dynamic_slice_in_dim(jnp.concatenate([v, v], axis), z, 4, axis)
    v = lax.dynamic_slice_in_dim(jnp.concatenate([v, v], axis + 1), core, 2, axis + 1)
    return jnp.swapaxes(v, axis, axis + 1).reshape(shape)


def all_sum(value):
    value = value + other_core(value)
    for axis in ("z", ("xh", "xl"), "y"):
        value = value + sum(
            lax.ppermute(value, axis, [(i, (i + k) % 4) for i in range(4)]) for k in (1, 2, 3)
        )
    return value


def halves(value):
    lane = lax.broadcasted_iota(jnp.int32, value.shape, value.ndim - 1)
    return lane < 64


def quarter(value):
    lane = lax.broadcasted_iota(jnp.int32, value.shape, value.ndim - 1)
    return (lane & 32) == 0


def turn(value):
    return jnp.where(quarter(value), -pltpu.roll(value, 96, 1), pltpu.roll(value, 32, 1))


def turn_back(value):
    return jnp.where(quarter(value), pltpu.roll(value, 96, 1), -pltpu.roll(value, 32, 1))


def head_mean(value):
    low = halves(value)
    first = jnp.sum(jnp.where(low, value, 0.0), axis=-1, keepdims=True)
    second = jnp.sum(jnp.where(low, 0.0, value), axis=-1, keepdims=True)
    return jnp.where(low, first, second) * (1.0 / 64)


def attend_kernel(at_ref, *refs):
    x_refs, w_refs = refs[:8], refs[8:12]
    gain_ref, qk_gain_ref, cos_ref, sin_ref, bias_ref = refs[12:17]
    mixed_ref, x_ref, normed_ref, w_ref, raw_ref, q_ref, kk_ref, vv_ref, stat_ref = refs[17:]

    @pl.when(pl.program_id(0) == 0)
    def _():
        for ky in range(4):
            for kx in range(4):
                row = lax.rem(at_ref[0] + ky, 4) * 256 + lax.rem(at_ref[1] + kx, 4) * 64
                row = pl.multiple_of(row, 64)
                w_ref[pl.ds(row, 64), :] = w_refs[ky][kx * 64 : kx * 64 + 64, :]

    for i, ref in enumerate(x_refs):
        block = ref[0]
        x_ref[i * 64 : i * 64 + 64, :] = block
        block = block.astype(f32)
        normed_ref[i * 64 : i * 64 + 64, :] = (
            block * rms_scale(block) * gain_ref[0:1, :]
        ).astype(bf16)
    raw = product(normed_ref[...], w_ref[:, :256])
    raw_ref[...] = raw
    cosine, sine = cos_ref[0], sin_ref[0]
    query, kv = raw[:, :128], raw[:, 128:]
    low = halves(kv)
    query = query * lax.rsqrt(head_mean(query * query) + eps) * qk_gain_ref[0:1, :]
    q_ref[...] = (query * cosine + turn(query) * sine).astype(bf16)
    key = kv * lax.rsqrt(head_mean(kv * kv) + eps) * qk_gain_ref[1:2, :]
    key = key * cosine + turn(key) * sine
    kk_ref[...] = jnp.where(low, key, pltpu.roll(key, 64, 1)).astype(bf16)
    vv_ref[...] = jnp.where(low, pltpu.roll(kv, 64, 1), kv).astype(bf16)
    keys, values = kk_ref[...], vv_ref[...]
    for rows in (slice(0, 256), slice(256, 512)):
        queries = q_ref[rows, :]
        low = halves(queries)
        bias = bias_ref[0, rows, :].astype(f32)
        parts = []
        for head in range(2):
            one = jnp.where(low == (head == 0), queries, jnp.zeros_like(queries))
            scores = product_nt(one, keys) * 0.125 + bias
            top = jnp.max(scores, axis=-1, keepdims=True)
            expo = jnp.exp(scores - top)
            total = jnp.sum(expo, axis=-1, keepdims=True)
            weights = (expo * (1.0 / total)).astype(bf16)
            parts.append((product(weights, values), top + jnp.log(total)))
        first = halves(parts[0][0])
        mixed_ref[rows, :] = jnp.where(first, parts[0][0], parts[1][0]).astype(bf16)
        stat_ref[rows, :] = jnp.where(first, parts[0][1], parts[1][1])


def attend(at, pieces, weights, gain, qk_gain, cosine, sine, bias):
    width = pieces[0].shape[2]
    micro = pieces[0].shape[0]
    group = 512
    whole = lambda a: pl.BlockSpec(a.shape, lambda m, at: (0,) * a.ndim)
    part = lambda a: pl.BlockSpec((1,) + a.shape[1:], lambda m, at: (m, 0, 0))
    rows = lambda cols: pl.BlockSpec((group, cols), lambda m, at: (m, 0))
    out = lambda cols, kind: jax.ShapeDtypeStruct((micro * group, cols), kind)
    return pl.pallas_call(
        attend_kernel,
        grid_spec=pltpu.PrefetchScalarGridSpec(
            num_scalar_prefetch=1,
            grid=(micro,),
            in_specs=[part(p) for p in pieces]
            + [whole(w) for w in weights]
            + [whole(gain), whole(qk_gain), part(cosine), part(sine), part(bias)],
            out_specs=[
                rows(128),
                rows(width),
                rows(width),
                pl.BlockSpec((width, 384), lambda m, at: (0, 0)),
                rows(256),
                rows(128),
                rows(128),
                rows(128),
                rows(128),
            ],
        ),
        out_shape=[
            out(128, bf16),
            out(width, bf16),
            out(width, bf16),
            jax.ShapeDtypeStruct((width, 384), bf16),
            out(256, f32),
            out(128, bf16),
            out(128, bf16),
            out(128, bf16),
            out(128, f32),
        ],
        compiler_params=pltpu.CompilerParams(vmem_limit_bytes=48 * 2**20),
        cost_estimate=pl.CostEstimate(flops=2 * 10**9, bytes_accessed=10**7, transcendentals=10**6),
        name="attend",
    )(at, *pieces, *weights, gain, qk_gain, cosine, sine, bias)


def feed_kernel(at_ref, *refs):
    mixed_refs, w_refs = refs[:8], refs[8:16]
    x_ref, up_ref, gain_ref, wf_ref = refs[16:20]
    state_ref, second_ref, inner_ref, low_ref, own_ref, other_ref = refs[20:26]
    w_out, mixed = refs[26:]
    step = pl.program_id(0)
    micro, side = step // 2, lax.rem(step, 2)

    @pl.when(step == 0)
    def _():
        for i, ref in enumerate(w_refs):
            for ky in range(4):
                for kx in range(4):
                    row = lax.rem(at_ref[0] + ky, 4) * 256 + lax.rem(at_ref[1] + kx, 4) * 64
                    row = pl.multiple_of(row, 64)
                    w_out[pl.ds(row, 64), i * 128 : i * 128 + 128] = ref[
                        ky * 256 + kx * 64 : ky * 256 + kx * 64 + 64, :
                    ]

    for i, ref in enumerate(mixed_refs):
        flip, k = i // 4, i % 4
        base = micro * 512 + lax.rem(side + flip, 2) * 256
        for j in range(4):
            row = pl.multiple_of(base + (j - k) % 4 * 64, 64)
            mixed[j * 64 : j * 64 + 64, i * 128 : i * 128 + 128] = ref[pl.ds(row, 64), :]
    state = x_ref[...].astype(f32) + product_nt(mixed[...], w_out[...])
    state_ref[...] = state[:64]
    second = (state * rms_scale(state) * gain_ref[0:1, :]).astype(bf16)
    second_ref[...] = second
    both = product(second, wf_ref[:, :1152])
    grad_inner = product(up_ref[...], wf_ref[:, 1152:1728])

    def glu(gate, up, grad):
        sig = 1.0 / (1.0 + jnp.exp(-gate))
        silu = gate * sig
        inner = (silu * up).astype(bf16)
        grad_gate = (grad * up * sig * (1.0 + gate * (1.0 - sig))).astype(bf16)
        return inner, grad_gate, (grad * silu).astype(bf16)

    inner, grad_gate, grad_up = glu(both[:, :512], both[:, 512:1024], grad_inner[:, :512])
    inner_ref[:, :512] = inner
    low_ref[:, :512] = grad_gate
    low_ref[:, 512:1024] = grad_up
    tail = both[:, 1024:]
    up_tail = pltpu.roll(tail, 64, 1)
    inner, grad_gate, grad_up = glu(tail[:, :64], up_tail[:, :64], grad_inner[:, 512:])
    inner_ref[:, 512:] = inner
    low_ref[:, 1024:1088] = grad_gate
    low_ref[:, 1088:] = grad_up
    grad = product_nt(low_ref[...], wf_ref[:, :1152]).astype(bf16)

    @pl.when(side == 0)
    def _():
        own_ref[0] = grad

    @pl.when(side == 1)
    def _():
        other_ref[0] = grad


def feed(at, mixed, w_out, x, upstream, gain, w_ffn):
    count, width = x.shape
    steps = count // 256
    whole = lambda a: pl.BlockSpec(a.shape, lambda b, at: (0,) * a.ndim)
    rows = lambda cols, block=256: pl.BlockSpec((block, cols), lambda b, at: (b, 0))
    half = pl.BlockSpec((1, 256, width), lambda b, at: (b // 2, 0, 0))
    out = lambda shape, kind: jax.ShapeDtypeStruct(shape, kind)
    return pl.pallas_call(
        feed_kernel,
        grid_spec=pltpu.PrefetchScalarGridSpec(
            num_scalar_prefetch=1,
            grid=(steps,),
            in_specs=[whole(p) for p in mixed]
            + [whole(w) for w in w_out]
            + [rows(width), rows(width), whole(gain), whole(w_ffn)],
            out_specs=[rows(width, 64), rows(width), rows(576), rows(1152), half, half],
            scratch_shapes=[pltpu.VMEM((width, 1024), bf16), pltpu.VMEM((256, 1024), bf16)],
        ),
        out_shape=[
            out((steps * 64, width), f32),
            out((count, width), bf16),
            out((count, 576), bf16),
            out((count, 1152), bf16),
            out((steps // 2, 256, width), bf16),
            out((steps // 2, 256, width), bf16),
        ],
        compiler_params=pltpu.CompilerParams(vmem_limit_bytes=56 * 2**20),
        cost_estimate=pl.CostEstimate(flops=9 * 10**9, bytes_accessed=10**7, transcendentals=10**6),
        name="feed",
    )(at, *mixed, *w_out, x, upstream, gain, w_ffn)


def back_kernel(*refs):
    state_refs = refs[:8]
    normed_ref, w_ref, raw_ref, q_ref, kk_ref, vv_ref, stat_ref, mixed_ref = refs[8:16]
    qk_gain_ref, cos_ref, sin_ref, bias_ref = refs[16:20]
    own_ref, other_ref, grad_ref, gain_ref, qk_grad_ref = refs[20:25]
    state, low_ref, total = refs[25:]
    step = pl.program_id(0)
    for i, ref in enumerate(state_refs):
        state[i * 64 : i * 64 + 64, :] = ref[0]
    grad_mixed = product(state[...], w_ref[:, 256:]).astype(bf16)
    keys, values = kk_ref[...], vv_ref[...]
    grad_key = jnp.zeros((512, 128), f32)
    grad_value = jnp.zeros((512, 128), f32)
    grad_query = []
    for rows in (slice(0, 256), slice(256, 512)):
        queries, grads = q_ref[rows, :], grad_mixed[rows, :]
        low = halves(queries)
        bias = bias_ref[0, rows, :].astype(f32)
        parts = []
        for head in range(2):
            keep = low == (head == 0)
            one = jnp.where(keep, queries, jnp.zeros_like(queries))
            grad_one = jnp.where(keep, grads, jnp.zeros_like(grads))
            scores = product_nt(one, keys) * 0.125 + bias
            soft = jnp.exp(scores - stat_ref[rows, head * 64 : head * 64 + 1])
            grad_weights = product_nt(grad_one, values)
            center = jnp.sum(soft * grad_weights, axis=-1, keepdims=True)
            grad_scores = (soft * (grad_weights - center)).astype(bf16)
            parts.append(product(grad_scores, keys))
            grad_key = grad_key + product_tn(grad_scores, one)
            grad_value = grad_value + product_tn(soft.astype(bf16), grad_one)
        grad_query.append(jnp.where(halves(parts[0]), parts[0], parts[1]))
    cosine, sine = cos_ref[0], sin_ref[0]

    def prepare_back(grad, raw, gain):
        grad = grad * cosine + turn_back(grad * sine)
        scale = lax.rsqrt(head_mean(raw * raw) + eps)
        unit = raw * scale
        grad_gain = jnp.sum(grad * unit, axis=0, keepdims=True)
        scaled = grad * gain
        return scale * (scaled - unit * head_mean(scaled * unit)), grad_gain

    raw = raw_ref[...]
    grad_q = jnp.concatenate(grad_query, axis=0) * 0.125
    grad_q, gain_q = prepare_back(grad_q, raw[:, :128], qk_gain_ref[0:1, :])
    grad_key = (grad_key + pltpu.roll(grad_key, 64, 1)) * 0.125
    grad_value = grad_value + pltpu.roll(grad_value, 64, 1)
    low = halves(grad_value)
    raw_k = jnp.where(low, raw[:, 128:], 0.0)
    grad_k, gain_k = prepare_back(jnp.where(low, grad_key, 0.0), raw_k, qk_gain_ref[1:2, :])
    low_ref[:, :128] = grad_q.astype(bf16)
    low_ref[:, 128:] = jnp.where(low, grad_k, grad_value).astype(bf16)

    @pl.when(step == 0)
    def _():
        total[...] = jnp.zeros_like(total)
        gain_ref[...] = jnp.zeros_like(gain_ref)
        qk_grad_ref[...] = jnp.zeros_like(qk_grad_ref)

    qk_grad_ref[0:1, :] += gain_q
    qk_grad_ref[1:2, :] += gain_k
    for rows, ref in ((slice(0, 256), own_ref), (slice(256, 512), other_ref)):
        grad = product_nt(low_ref[rows, :], w_ref[:, :256])
        ref[0] = grad.astype(bf16)
        gain_ref[0:1, :] += jnp.sum(grad * normed_ref[rows, :].astype(f32), axis=0, keepdims=True)
    total[:, :256] += product_tn(normed_ref[...], low_ref[...])
    total[:, 256:] += product_tn(state[...], mixed_ref[...])
    grad_ref[...] = total[...].astype(bf16)


def back(state, normed, w_att, raw, query, keys, values, stat, mixed, qk_gain, cosine, sine, bias):
    width = state[0].shape[2]
    micro = state[0].shape[0]
    whole = lambda a: pl.BlockSpec(a.shape, lambda m: (0,) * a.ndim)
    part = lambda a: pl.BlockSpec((1,) + a.shape[1:], lambda m: (m, 0, 0))
    rows = lambda a: pl.BlockSpec((512, a.shape[1]), lambda m: (m, 0))
    half = pl.BlockSpec((1, 256, width), lambda m: (m, 0, 0))
    fixed = lambda a, b: pl.BlockSpec((a, b), lambda m: (0, 0))
    out = jax.ShapeDtypeStruct
    return pl.pallas_call(
        back_kernel,
        grid=(micro,),
        in_specs=[part(p) for p in state]
        + [rows(normed), whole(w_att), rows(raw), rows(query), rows(keys), rows(values)]
        + [rows(stat), rows(mixed), whole(qk_gain), part(cosine), part(sine), part(bias)],
        out_specs=[half, half, fixed(width, 384), fixed(8, width), fixed(8, 128)],
        scratch_shapes=[
            pltpu.VMEM((512, width), bf16),
            pltpu.VMEM((512, 256), bf16),
            pltpu.VMEM((width, 384), f32),
        ],
        out_shape=[
            out((micro, 256, width), bf16),
            out((micro, 256, width), bf16),
            out((width, 384), bf16),
            out((8, width), f32),
            out((8, 128), f32),
        ],
        compiler_params=pltpu.CompilerParams(vmem_limit_bytes=48 * 2**20),
        cost_estimate=pl.CostEstimate(flops=4 * 10**9, bytes_accessed=10**7, transcendentals=10**6),
        name="back",
    )(*state, normed, w_att, raw, query, keys, values, stat, mixed, qk_gain, cosine, sine, bias)


def split_kernel(own_ref, got_ref, total_ref, *low_refs):
    total_ref[...] = own_ref[:, :64].astype(f32) + got_ref[:, :64].astype(f32)
    for k, ref in enumerate(low_refs, 1):
        rows = slice(k * 64, k * 64 + 64)
        ref[...] = (own_ref[:, rows].astype(f32) + got_ref[:, rows].astype(f32)).astype(bf16)


def scatter_sum(own, other):
    got = other_core(other)
    micro, _, width = own.shape
    out = lambda kind: jax.ShapeDtypeStruct((micro, 64, width), kind)
    parts = pl.pallas_call(
        split_kernel,
        out_shape=[out(f32), out(bf16), out(bf16), out(bf16)],
        name="split",
    )(own, got)
    total = parts[0]
    for k in (1, 2, 3):
        total = total + from_z(parts[k], -k).astype(f32)
    return total


def local(
    tokens,
    segment_ids,
    cotangent,
    w_query,
    w_key,
    w_value,
    w_out,
    w_gate,
    w_up,
    w_down,
    norm_gain,
    ffn_gain,
    query_gain,
    key_gain,
):
    micro, own, width = tokens.shape
    head_size = query_gain.shape[0]
    nq = w_query.shape[1]
    nk = w_key.shape[1]
    group = segment_ids.shape[1]
    hidden = w_gate.shape[1]
    main = hidden - hidden % 128
    z = lax.axis_index("z")
    core = lax.axis_index("core")
    at = jnp.stack([lax.axis_index("y"), lax.axis_index("xh") * 2 + lax.axis_index("xl")])
    at = at.astype(jnp.int32)

    x_pieces = gather_swapped(tokens)
    w_att = jnp.concatenate([w_query, w_key, w_value, w_out.T], axis=1)
    w_att = jnp.concatenate([swap_from_x(w_att, k) for k in range(4)], axis=0)
    w_att = [w_att] + [from_y(w_att, k) for k in (1, 2, 3)]
    segment = swap(segment_ids)
    w_ffn = [w_gate[:, :main], w_up[:, :main], w_gate[:, main:], w_up[:, main:], w_down.T]
    w_ffn = lax.all_gather(swap(jnp.concatenate(w_ffn, axis=1)), plane, axis=0, tiled=True)
    upstream = jnp.concatenate(gather_swapped(cotangent), axis=1).reshape(micro * group, width)
    w_out_all = jnp.concatenate([w[:, nq + 2 * nk :] for w in w_att], axis=0)
    w_out_all = [w_out_all] + [from_z(w_out_all, k) for k in (1, 2, 3)]
    w_out_all = w_out_all + [other_core(w) for w in w_out_all]

    index = jnp.arange(group, dtype=jnp.int32)
    change = jnp.concatenate(
        [jnp.ones((micro, 1), dtype=bool), segment[:, 1:] != segment[:, :-1]], axis=1
    )
    start = lax.cummax(jnp.where(change, index, 0), axis=1)
    start = ordered(start, z, core, 1)
    index = ordered(index[None], z, core, 1)
    place = (index - start).astype(f32)
    freq = rope_base ** (-(jnp.arange(head_size // 2, dtype=f32) * 2.0 / head_size))
    angle = place[:, :, None] * jnp.tile(freq, 4)
    cosine, sine = jnp.cos(angle), jnp.sin(angle)
    allowed = (start[:, :, None] == start[:, None, :]) & (index[:, :, None] >= index[:, None, :])
    bias = jnp.where(allowed, 0.0, -1e30).astype(bf16)
    qk_gain = jnp.stack([jnp.tile(query_gain, 2), jnp.tile(key_gain, 2)])
    qk_gain = jnp.concatenate([qk_gain, jnp.zeros((6, 128), f32)])
    gain_rows = lambda gain: jnp.broadcast_to(gain, (8, width))

    mixed, x, normed, w_abs, raw, query, keys, values, stat = attend(
        at, x_pieces, w_att, gain_rows(norm_gain), qk_gain, cosine, sine, bias
    )
    state, second, inner, gu_low, grad_own, grad_other = feed(
        at, gather(mixed), w_out_all, x, upstream, gain_rows(ffn_gain), w_ffn
    )
    grad_second = scatter_sum(grad_own, grad_other)
    state_own = state.reshape(micro, 2, own, width)[:, 0]
    _, norm_pull = jax.vjp(rms_rows, state_own, ffn_gain)
    grad_state_norm, grad_ffn_gain = norm_pull(grad_second)
    upstream_blocks = upstream.reshape(micro, group, width)
    grad_state = upstream_blocks[:, :own].astype(f32) + grad_state_norm
    state_pieces = gather(grad_state.astype(bf16))

    grad_gu = product_tn(second, gu_low).astype(bf16)
    grad_gu = lax.psum_scatter(grad_gu, plane, scatter_dimension=0, tiled=True)
    grad_down = product_tn(upstream, inner).astype(bf16)
    grad_down = lax.psum_scatter(grad_down, plane, scatter_dimension=0, tiled=True)
    grad_ffn = swap(jnp.concatenate([grad_gu, grad_down], axis=1)).astype(f32)
    down = product_nt(inner, w_ffn[:, 2 * hidden :]).astype(bf16).reshape(micro, group, width)
    output = state_own + scatter_sum(down[:, : group // 2], down[:, group // 2 :])
    output = swap(output.astype(bf16))

    grad_own, grad_other, grad_att, grad_norm_gain, grad_qk_gain = back(
        state_pieces, normed, w_abs, raw, query, keys, values, stat, mixed, qk_gain, cosine, sine, bias
    )
    grad_normed = scatter_sum(grad_own, grad_other)
    grad_att = lax.all_to_all(grad_att, plane, 0, 0, tiled=True)
    grad_att = jnp.sum(grad_att.reshape(16, width // 16, -1).astype(f32), axis=0)
    grad_att = swap(grad_att)
    gains = all_sum(
        jnp.concatenate(
            [grad_norm_gain[0] / norm_gain, grad_ffn_gain, grad_qk_gain[0], grad_qk_gain[1]]
        )
    )
    x_own = x.reshape(micro, group, width)[:, :own].astype(f32)
    _, first_pull = jax.vjp(rms_rows, x_own, norm_gain)
    grad_resid_norm, _ = first_pull(grad_normed)
    input_grad = swap((grad_state + grad_resid_norm).astype(bf16))
    split = nq + nk
    q_gains = gains[2 * width :]
    return (
        output,
        input_grad,
        grad_att[:, :nq],
        grad_att[:, nq:split],
        grad_att[:, split : split + nk],
        grad_att[:, split + nk :].T,
        jnp.concatenate([grad_ffn[:, :main], grad_ffn[:, 2 * main : main + hidden]], axis=1),
        jnp.concatenate([grad_ffn[:, main : 2 * main], grad_ffn[:, main + hidden : 2 * hidden]], axis=1),
        grad_ffn[:, 2 * hidden :].T,
        gains[:width],
        gains[width : 2 * width],
        q_gains[:head_size] + q_gains[head_size : 2 * head_size],
        q_gains[2 * head_size : 3 * head_size],
    )


def solution(mesh):
    inner = Mesh(mesh.devices.reshape(4, 2, 2, 4, 2), axes)
    dp, mp = ("y", "xh", "core"), ("z", "xl")
    rows = P(None, dp + mp, None)
    weight_in = [P(dp, mp)] * 3 + [P(mp, dp)] + [P(dp, mp)] * 2 + [P(mp, dp)]
    return jax.shard_map(
        local,
        mesh=inner,
        in_specs=tuple([rows, P(None, dp), rows] + weight_in + [P()] * 4),
        out_specs=tuple([rows, rows] + weight_in + [P()] * 4),
        check_vma=False,
    )
```

```python
import jax
import jax.numpy as jnp
from jax import lax
from jax.experimental import pallas as pl
from jax.experimental.pallas import tpu as pltpu
from jax.sharding import Mesh, PartitionSpec as P

eps = 1e-05
rope_base = 1000000.0
axes = ("y", "xh", "core", "z", "xl")
plane = ("y", "xh", "xl")
CORE = [(0, 1), (1, 0)]
bf16 = jnp.bfloat16
f32 = jnp.float32
VMEM = 60 * 2**20


def product(left, right):
    return jnp.dot(left, right, preferred_element_type=jnp.float32)


def product_nt(left, right):
    return lax.dot_general(
        left, right, (((1,), (1,)), ((), ())), preferred_element_type=jnp.float32
    )


def product_tn(left, right):
    return lax.dot_general(
        left, right, (((0,), (0,)), ((), ())), preferred_element_type=jnp.float32
    )


def rms_scale(value):
    return lax.rsqrt(jnp.mean(value * value, axis=-1, keepdims=True) + eps)


def rms_rows(value, gain):
    return value * rms_scale(value) * gain


def swap(value):
    return lax.ppermute(
        value, ("core", "xl"), [(a * 2 + b, b * 2 + a) for a in range(2) for b in range(2)]
    )


def from_z(value, k):
    return lax.ppermute(value, "z", [(z, (z - k) % 4) for z in range(4)])


def swap_from_z(value, k):
    perm = [
        (a * 8 + z * 2 + b, b * 8 + ((z - k) % 4) * 2 + a)
        for a in range(2)
        for z in range(4)
        for b in range(2)
    ]
    return lax.ppermute(value, ("core", "z", "xl"), perm)


def swap_from_x(value, k):
    perm = []
    for xh in range(2):
        for a in range(2):
            for b in range(2):
                x = (xh * 2 + a - k) % 4
                perm.append((xh * 4 + a * 2 + b, (x // 2) * 4 + b * 2 + x % 2))
    return lax.ppermute(value, ("xh", "core", "xl"), perm)


def from_y(value, k):
    return lax.ppermute(value, "y", [(y, (y - k) % 4) for y in range(4)])


def other_core(value):
    return lax.ppermute(value, "core", CORE)


def from_chain(value):
    return [value] + [from_z(value, k) for k in (1, 2, 3)]


def gather_chains(pieces):
    chain = jnp.stack(pieces)
    return chain, other_core(chain)


def gather(value):
    chain = [value] + [from_z(value, k) for k in (1, 2, 3)]
    return chain + [other_core(v) for v in chain]


def ordered(value, z, core, axis):
    shape = value.shape
    block = shape[axis] // 8
    v = value.reshape(shape[:axis] + (4, 2, block) + shape[axis + 1 :])
    v = lax.dynamic_slice_in_dim(jnp.concatenate([v, v], axis), z, 4, axis)
    v = lax.dynamic_slice_in_dim(jnp.concatenate([v, v], axis + 1), core, 2, axis + 1)
    return jnp.swapaxes(v, axis, axis + 1).reshape(shape)


def group_sum(value):
    value = value + other_core(value)
    return value + sum(from_z(value, k) for k in (1, 2, 3))


def tie(*values):
    return lax.optimization_barrier(values)


def halves(value):
    lane = lax.broadcasted_iota(jnp.int32, value.shape, value.ndim - 1)
    return lane < 64


def quarter(value):
    lane = lax.broadcasted_iota(jnp.int32, value.shape, value.ndim - 1)
    return (lane & 32) == 0


def turn(value):
    return jnp.where(quarter(value), -pltpu.roll(value, 96, 1), pltpu.roll(value, 32, 1))


def turn_back(value):
    return jnp.where(quarter(value), pltpu.roll(value, 96, 1), -pltpu.roll(value, 32, 1))


def head_mean(value):
    low = halves(value)
    first = jnp.sum(jnp.where(low, value, 0.0), axis=-1, keepdims=True)
    second = jnp.sum(jnp.where(low, 0.0, value), axis=-1, keepdims=True)
    return jnp.where(low, first, second) * (1.0 / 64)


def attend_kernel(at_ref, *refs):
    x_refs, w_refs = refs[:2], refs[2:6]
    gain_ref, qk_gain_ref, cos_ref, sin_ref, bias_ref = refs[6:11]
    mixed_ref, x_ref, normed_ref, w_ref, raw_ref, q_ref, kk_ref, vv_ref, stat_ref = refs[11:]

    @pl.when(pl.program_id(0) == 0)
    def _():
        for ky in range(4):
            for kx in range(4):
                row = lax.rem(at_ref[0] + ky, 4) * 256 + lax.rem(at_ref[1] + kx, 4) * 64
                row = pl.multiple_of(row, 64)
                w_ref[pl.ds(row, 64), :] = w_refs[ky][kx * 64 : kx * 64 + 64, :]

    for i in range(8):
        block = x_refs[i // 4][i % 4, 0]
        x_ref[i * 64 : i * 64 + 64, :] = block
        block = block.astype(f32)
        normed_ref[i * 64 : i * 64 + 64, :] = (
            block * rms_scale(block) * gain_ref[0:1, :]
        ).astype(bf16)
    raw = product(normed_ref[...], w_ref[:, :256])
    raw_ref[...] = raw
    cosine, sine = cos_ref[0], sin_ref[0]
    query, kv = raw[:, :128], raw[:, 128:]
    low = halves(kv)
    query = query * lax.rsqrt(head_mean(query * query) + eps) * qk_gain_ref[0:1, :]
    q_ref[...] = (query * cosine + turn(query) * sine).astype(bf16)
    key = kv * lax.rsqrt(head_mean(kv * kv) + eps) * qk_gain_ref[1:2, :]
    key = key * cosine + turn(key) * sine
    kk_ref[...] = jnp.where(low, key, pltpu.roll(key, 64, 1)).astype(bf16)
    vv_ref[...] = jnp.where(low, pltpu.roll(kv, 64, 1), kv).astype(bf16)
    keys, values = kk_ref[...], vv_ref[...]
    for rows in (slice(0, 256), slice(256, 512)):
        queries = q_ref[rows, :]
        low = halves(queries)
        bias = bias_ref[0, rows, :].astype(f32)
        parts = []
        for head in range(2):
            one = jnp.where(low == (head == 0), queries, jnp.zeros_like(queries))
            scores = product_nt(one, keys) * 0.125 + bias
            top = jnp.max(scores, axis=-1, keepdims=True)
            expo = jnp.exp(scores - top)
            total = jnp.sum(expo, axis=-1, keepdims=True)
            weights = (expo * (1.0 / total)).astype(bf16)
            parts.append((product(weights, values), top + jnp.log(total)))
        first = halves(parts[0][0])
        mixed_ref[rows, :] = jnp.where(first, parts[0][0], parts[1][0]).astype(bf16)
        stat_ref[rows, :] = jnp.where(first, parts[0][1], parts[1][1])


def attend(at, pieces, weights, gain, qk_gain, cosine, sine, bias):
    width = pieces[0].shape[3]
    micro = pieces[0].shape[1]
    group = 512
    chain = pl.BlockSpec((4, 1, 64, width), lambda m, at: (0, m, 0, 0))
    whole = lambda a: pl.BlockSpec(a.shape, lambda m, at: (0,) * a.ndim)
    part = lambda a: pl.BlockSpec((1,) + a.shape[1:], lambda m, at: (m, 0, 0))
    rows = lambda cols: pl.BlockSpec((group, cols), lambda m, at: (m, 0))
    out = lambda cols, kind: jax.ShapeDtypeStruct((micro * group, cols), kind)
    return pl.pallas_call(
        attend_kernel,
        grid_spec=pltpu.PrefetchScalarGridSpec(
            num_scalar_prefetch=1,
            grid=(micro,),
            in_specs=[chain, chain]
            + [whole(w) for w in weights]
            + [whole(gain), whole(qk_gain), part(cosine), part(sine), part(bias)],
            out_specs=[
                rows(128),
                rows(width),
                rows(width),
                pl.BlockSpec((width, 384), lambda m, at: (0, 0)),
                rows(256),
                rows(128),
                rows(128),
                rows(128),
                rows(128),
            ],
        ),
        out_shape=[
            out(128, bf16),
            out(width, bf16),
            out(width, bf16),
            jax.ShapeDtypeStruct((width, 384), bf16),
            out(256, f32),
            out(128, bf16),
            out(128, bf16),
            out(128, bf16),
            out(128, f32),
        ],
        compiler_params=pltpu.CompilerParams(vmem_limit_bytes=VMEM),
        cost_estimate=pl.CostEstimate(flops=2 * 10**9, bytes_accessed=10**7, transcendentals=10**6),
        name="attend",
    )(at, *pieces, *weights, gain, qk_gain, cosine, sine, bias)


def feed_kernel(at_ref, *refs):
    mixed_refs, w_refs = refs[:8], refs[8:10]
    x_ref, gain_ref, wf_ref = refs[10:13]
    up_refs = refs[13:15]
    state_ref, second_ref, inner_ref, low_ref, own_ref, other_ref = refs[15:21]
    up_ref, down_own_ref, down_other_ref = refs[21:24]
    w_out, mixed, w_gu = refs[24:]
    step = pl.program_id(0)
    micro, side = step // 2, lax.rem(step, 2)

    @pl.when(step == 0)
    def _():
        for i in range(8):
            for ky in range(4):
                for kx in range(4):
                    row = lax.rem(at_ref[0] + ky, 4) * 256 + lax.rem(at_ref[1] + kx, 4) * 64
                    row = pl.multiple_of(row, 64)
                    w_out[pl.ds(row, 64), i * 128 : i * 128 + 128] = w_refs[i // 4][
                        i % 4, ky * 256 + kx * 64 : ky * 256 + kx * 64 + 64, :
                    ]
        for rows in (slice(i, i + 128) for i in range(0, w_gu.shape[0], 128)):
            w_gu[rows, :512] = wf_ref[rows, :512]
            rest = wf_ref[rows, 512:1152].astype(f32)
            w_gu[rows, 512:] = pltpu.roll(rest, 576, 1).astype(bf16)

    for i, ref in enumerate(up_refs):

        @pl.when(side == i)
        def _():
            for j in range(4):
                up_ref[j * 64 : j * 64 + 64, :] = ref[j, 0]

    for i, ref in enumerate(mixed_refs):
        flip, k = i // 4, i % 4
        base = micro * 512 + lax.rem(side + flip, 2) * 256
        for j in range(4):
            row = pl.multiple_of(base + (j - k) % 4 * 64, 64)
            mixed[j * 64 : j * 64 + 64, i * 128 : i * 128 + 128] = ref[pl.ds(row, 64), :]
    state = x_ref[...].astype(f32) + product_nt(mixed[...], w_out[...])
    state_ref[...] = state[:64]
    second = (state * rms_scale(state) * gain_ref[0:1, :]).astype(bf16)
    second_ref[...] = second
    both = product(second, w_gu[...])
    grad_inner = product(up_ref[...], wf_ref[:, 1152:1728])

    def glu(gate, up, grad):
        sig = 1.0 / (1.0 + jnp.exp(-gate))
        silu = gate * sig
        inner = (silu * up).astype(bf16)
        grad_gate = (grad * up * sig * (1.0 + gate * (1.0 - sig))).astype(bf16)
        return inner, grad_gate, (grad * silu).astype(bf16)

    inner, grad_gate, grad_up = glu(both[:, :512], both[:, 512:1024], grad_inner[:, :512])
    inner_ref[:, :512] = inner
    low_ref[:, :512] = grad_gate
    low_ref[:, 512:1024] = grad_up
    tail = both[:, 1024:]
    gate_tail = pltpu.roll(tail, 64, 1)
    inner, grad_gate, grad_up = glu(gate_tail[:, :64], tail[:, :64], grad_inner[:, 512:])
    inner_ref[:, 512:] = inner
    low_ref[:, 1024:1088] = grad_up
    low_ref[:, 1088:] = grad_gate
    grad = product_nt(low_ref[...], w_gu[...]).astype(bf16)
    down = product_nt(inner_ref[...], wf_ref[:, 1152:]).astype(bf16)

    @pl.when(side == 0)
    def _():
        own_ref[0] = grad
        down_own_ref[0] = down

    @pl.when(side == 1)
    def _():
        other_ref[0] = grad
        down_other_ref[0] = down


def feed(at, mixed, w_out, x, cotangent, gain, w_ffn):
    count, width = x.shape
    steps = count // 256
    whole = lambda a: pl.BlockSpec(a.shape, lambda b, at: (0,) * a.ndim)
    rows = lambda cols, block=256: pl.BlockSpec((block, cols), lambda b, at: (b, 0))
    half = pl.BlockSpec((1, 256, width), lambda b, at: (b // 2, 0, 0))
    out = lambda shape, kind: jax.ShapeDtypeStruct(shape, kind)

    chain = pl.BlockSpec((4, 1, 64, width), lambda b, at: (0, b // 2, 0, 0))
    return pl.pallas_call(
        feed_kernel,
        grid_spec=pltpu.PrefetchScalarGridSpec(
            num_scalar_prefetch=1,
            grid=(steps,),
            in_specs=[whole(p) for p in mixed]
            + [whole(w) for w in w_out]
            + [rows(width), whole(gain), whole(w_ffn)]
            + [chain, chain],
            out_specs=[rows(width, 64), rows(width), rows(576), rows(1152)]
            + [half, half, rows(width), half, half],
            scratch_shapes=[
                pltpu.VMEM((width, 1024), bf16),
                pltpu.VMEM((256, 1024), bf16),
                pltpu.VMEM((width, 1152), bf16),
            ],
        ),
        out_shape=[
            out((steps * 64, width), f32),
            out((count, width), bf16),
            out((count, 576), bf16),
            out((count, 1152), bf16),
            out((steps // 2, 256, width), bf16),
            out((steps // 2, 256, width), bf16),
            out((count, width), bf16),
            out((steps // 2, 256, width), bf16),
            out((steps // 2, 256, width), bf16),
        ],
        compiler_params=pltpu.CompilerParams(vmem_limit_bytes=VMEM),
        cost_estimate=pl.CostEstimate(flops=9 * 10**9, bytes_accessed=10**7, transcendentals=10**6),
        name="feed",
    )(at, *mixed, *w_out, x, gain, w_ffn, *cotangent)


def weights_kernel(second_ref, up_ref, low_ref, inner_ref, grad_ref):
    grad = product_tn(second_ref[...], low_ref[...])
    grad_ref[:, :512] = grad[:, :512].astype(bf16)
    grad_ref[:, 512:1152] = pltpu.roll(grad[:, 512:], 64, 1).astype(bf16)
    grad_ref[:, 1152:] = product_tn(up_ref[...], inner_ref[...]).astype(bf16)


def weights_back(second, upstream, low, inner):
    count, width = second.shape
    whole = lambda a: pl.BlockSpec(a.shape, lambda b: (0,) * a.ndim)
    columns = pl.BlockSpec((count, 256), lambda b: (0, b))
    return pl.pallas_call(
        weights_kernel,
        grid=(width // 256,),
        in_specs=[columns, columns, whole(low), whole(inner)],
        out_specs=pl.BlockSpec((256, 1728), lambda b: (b, 0)),
        out_shape=jax.ShapeDtypeStruct((width, 1728), bf16),
        compiler_params=pltpu.CompilerParams(vmem_limit_bytes=VMEM),
        cost_estimate=pl.CostEstimate(flops=4 * 10**9, bytes_accessed=10**7, transcendentals=0),
        name="weights_back",
    )(second, upstream, low, inner)


def back_kernel(*refs):
    state_refs = refs[:8]
    normed_ref, w_ref, raw_ref, q_ref, kk_ref, vv_ref, stat_ref, mixed_ref = refs[8:16]
    qk_gain_ref, cos_ref, sin_ref, bias_ref, gain_ref, ffn_ref = refs[16:22]
    own_ref, other_ref, grad_ref = refs[22:25]
    state, low_ref, total, norm_ref, qk_grad_ref = refs[25:]
    step = pl.program_id(0)
    for i, ref in enumerate(state_refs):
        state[i * 64 : i * 64 + 64, :] = ref[0]
    grad_mixed = product(state[...], w_ref[:, 256:]).astype(bf16)
    keys, values = kk_ref[...], vv_ref[...]
    grad_key = jnp.zeros((512, 128), f32)
    grad_value = jnp.zeros((512, 128), f32)
    grad_query = []
    for rows in (slice(0, 256), slice(256, 512)):
        queries, grads = q_ref[rows, :], grad_mixed[rows, :]
        low = halves(queries)
        bias = bias_ref[0, rows, :].astype(f32)
        parts = []
        for head in range(2):
            keep = low == (head == 0)
            one = jnp.where(keep, queries, jnp.zeros_like(queries))
            grad_one = jnp.where(keep, grads, jnp.zeros_like(grads))
            scores = product_nt(one, keys) * 0.125 + bias
            soft = jnp.exp(scores - stat_ref[rows, head * 64 : head * 64 + 1])
            grad_weights = product_nt(grad_one, values)
            center = jnp.sum(soft * grad_weights, axis=-1, keepdims=True)
            grad_scores = (soft * (grad_weights - center)).astype(bf16)
            parts.append(product(grad_scores, keys))
            grad_key = grad_key + product_tn(grad_scores, one)
            grad_value = grad_value + product_tn(soft.astype(bf16), grad_one)
        grad_query.append(jnp.where(halves(parts[0]), parts[0], parts[1]))
    cosine, sine = cos_ref[0], sin_ref[0]

    def prepare_back(grad, raw, gain):
        grad = grad * cosine + turn_back(grad * sine)
        scale = lax.rsqrt(head_mean(raw * raw) + eps)
        unit = raw * scale
        grad_gain = jnp.sum(grad * unit, axis=0, keepdims=True)
        scaled = grad * gain
        return scale * (scaled - unit * head_mean(scaled * unit)), grad_gain

    raw = raw_ref[...]
    grad_q = jnp.concatenate(grad_query, axis=0) * 0.125
    grad_q, gain_q = prepare_back(grad_q, raw[:, :128], qk_gain_ref[0:1, :])
    grad_key = (grad_key + pltpu.roll(grad_key, 64, 1)) * 0.125
    grad_value = grad_value + pltpu.roll(grad_value, 64, 1)
    low = halves(grad_value)
    raw_k = jnp.where(low, raw[:, 128:], 0.0)
    grad_k, gain_k = prepare_back(jnp.where(low, grad_key, 0.0), raw_k, qk_gain_ref[1:2, :])
    low_ref[:, :128] = grad_q.astype(bf16)
    low_ref[:, 128:] = jnp.where(low, grad_k, grad_value).astype(bf16)

    @pl.when(step == 0)
    def _():
        total[...] = jnp.zeros_like(total)
        norm_ref[...] = jnp.zeros_like(norm_ref)
        qk_grad_ref[...] = jnp.zeros_like(qk_grad_ref)

    qk_grad_ref[0:1, :] += gain_q
    qk_grad_ref[1:2, :] += gain_k
    for rows, ref in ((slice(0, 256), own_ref), (slice(256, 512), other_ref)):
        grad = product_nt(low_ref[rows, :], w_ref[:, :256])
        ref[0] = grad.astype(bf16)
        norm_ref[0:1, :] += jnp.sum(grad * normed_ref[rows, :].astype(f32), axis=0, keepdims=True)
    total[:, :256] += product_tn(normed_ref[...], low_ref[...])
    total[:, 256:] += product_tn(state[...], mixed_ref[...])

    @pl.when(step == pl.num_programs(0) - 1)
    def _():
        norm = norm_ref[0:1, :] / gain_ref[0:1, :]
        chunks = [norm[:, i : i + 128] for i in range(0, 1024, 128)]
        chunks += [ffn_ref[0:1, i : i + 128] for i in range(0, 1024, 128)]
        chunks += [qk_grad_ref[0:1, :], qk_grad_ref[1:2, :]]
        lines = [jnp.concatenate(chunks[i : i + 3], axis=1) for i in range(0, 18, 3)]
        lines = jnp.concatenate(lines + [jnp.zeros((10, 384), f32)], axis=0).astype(bf16)
        for i in range(16):
            grad_ref[i, :64, :] = total[i * 64 : i * 64 + 64, :].astype(bf16)
            grad_ref[i, 64:, :] = lines


def back(
    state, normed, w_att, raw, query, keys, values, stat, mixed, qk_gain, cosine, sine, bias, gain, ffn
):
    width = state[0].shape[2]
    micro = state[0].shape[0]
    whole = lambda a: pl.BlockSpec(a.shape, lambda m: (0,) * a.ndim)
    part = lambda a: pl.BlockSpec((1,) + a.shape[1:], lambda m: (m, 0, 0))
    rows = lambda a: pl.BlockSpec((512, a.shape[1]), lambda m: (m, 0))
    half = pl.BlockSpec((1, 256, width), lambda m: (m, 0, 0))
    out = jax.ShapeDtypeStruct
    return pl.pallas_call(
        back_kernel,
        grid=(micro,),
        in_specs=[part(p) for p in state]
        + [rows(normed), whole(w_att), rows(raw), rows(query), rows(keys), rows(values)]
        + [rows(stat), rows(mixed), whole(qk_gain), part(cosine), part(sine), part(bias)]
        + [whole(gain), whole(ffn)],
        out_specs=[half, half, pl.BlockSpec((16, 80, 384), lambda m: (0, 0, 0))],
        scratch_shapes=[
            pltpu.VMEM((512, width), bf16),
            pltpu.VMEM((512, 256), bf16),
            pltpu.VMEM((width, 384), f32),
            pltpu.VMEM((8, width), f32),
            pltpu.VMEM((8, 128), f32),
        ],
        out_shape=[
            out((micro, 256, width), bf16),
            out((micro, 256, width), bf16),
            out((16, 80, 384), bf16),
        ],
        compiler_params=pltpu.CompilerParams(vmem_limit_bytes=VMEM),
        cost_estimate=pl.CostEstimate(flops=4 * 10**9, bytes_accessed=10**7, transcendentals=10**6),
        name="back",
    )(
        *(*state, normed, w_att, raw, query, keys, values, stat, mixed),
        *(qk_gain, cosine, sine, bias, gain, ffn),
    )


def split_kernel(own_ref, got_ref, *refs):
    for k, ref in enumerate(refs):
        rows = slice(k * 64, k * 64 + 64)
        value = own_ref[:, rows].astype(f32) + got_ref[:, rows].astype(f32)
        ref[...] = value.astype(ref.dtype)


def split(own, other, first):
    micro, _, width = own.shape
    out = lambda kind: jax.ShapeDtypeStruct((micro, 64, width), kind)
    return pl.pallas_call(
        split_kernel,
        out_shape=[out(first), out(bf16), out(bf16), out(bf16)],
        compiler_params=pltpu.CompilerParams(vmem_limit_bytes=VMEM),
        name="split",
    )(own, other_core(other))


def local(
    tokens,
    segment_ids,
    cotangent,
    w_query,
    w_key,
    w_value,
    w_out,
    w_gate,
    w_up,
    w_down,
    norm_gain,
    ffn_gain,
    query_gain,
    key_gain,
):
    micro, own, width = tokens.shape
    head_size = query_gain.shape[0]
    nq = w_query.shape[1]
    nk = w_key.shape[1]
    group = segment_ids.shape[1]
    hidden = w_gate.shape[1]
    z = lax.axis_index("z")
    core = lax.axis_index("core")
    at = jnp.stack([lax.axis_index("y"), lax.axis_index("xh") * 2 + lax.axis_index("xl"), z, core])
    at = at.astype(jnp.int32)

    w_ffn = swap(jnp.concatenate([w_gate, w_up, w_down.T], axis=1))
    w_att = jnp.concatenate([w_query, w_key, w_value, w_out.T], axis=1)
    w_att = jnp.concatenate([swap_from_x(w_att, k) for k in range(4)], axis=0)
    x_chain, x_other = gather_chains(from_chain(swap(tokens)))
    segment = swap(segment_ids)
    cotangent_own = swap(cotangent)
    w_att = [w_att] + [from_y(w_att, k) for k in (1, 2, 3)]
    w_ffn, *w_att = tie(w_ffn, *w_att)
    w_ffn = lax.all_gather(w_ffn, plane, axis=0, tiled=True)
    w_out_own = jnp.concatenate([w[:, nq + 2 * nk :] for w in w_att], axis=0)
    x_other, cotangent_own, w_out_own = tie(x_other, cotangent_own, w_out_own)
    cotangent_chain = from_chain(cotangent_own)
    w_out_chain = from_chain(w_out_own)

    index = jnp.arange(group, dtype=jnp.int32)
    change = jnp.concatenate(
        [jnp.ones((micro, 1), dtype=bool), segment[:, 1:] != segment[:, :-1]], axis=1
    )
    start = lax.cummax(jnp.where(change, index, 0), axis=1)
    start = ordered(start, z, core, 1)
    index = ordered(index[None], z, core, 1)
    place = (index - start).astype(f32)
    freq = rope_base ** (-(jnp.arange(head_size // 2, dtype=f32) * 2.0 / head_size))
    angle = place[:, :, None] * jnp.tile(freq, 4)
    cosine, sine = jnp.cos(angle), jnp.sin(angle)
    allowed = (start[:, :, None] == start[:, None, :]) & (index[:, :, None] >= index[:, None, :])
    bias = jnp.where(allowed, 0.0, -1e30).astype(bf16)
    qk_gain = jnp.stack([jnp.tile(query_gain, 2), jnp.tile(key_gain, 2)])
    qk_gain = jnp.concatenate([qk_gain, jnp.zeros((6, 128), f32)])
    gain_rows = lambda gain: jnp.broadcast_to(gain, (8, width))

    mixed, x, normed, w_abs, raw, query, keys, values, stat = attend(
        at, (x_chain, x_other), w_att, gain_rows(norm_gain), qk_gain, cosine, sine, bias
    )
    mixed, *chains = tie(mixed, *cotangent_chain, *w_out_chain)
    mixed_pieces = gather(mixed)
    w_out_all = gather_chains(chains[4:])
    cotangent_all = gather_chains(chains[:4])
    state, second, inner, gu_low, grad_own, grad_other, upstream, down_own, down_other = feed(
        at, mixed_pieces, w_out_all, x, cotangent_all, gain_rows(ffn_gain), w_ffn
    )
    parts = split(grad_own, grad_other, f32)
    got = [from_z(parts[k], -k) for k in (1, 2, 3)]
    grad_ffn = weights_back(second, upstream, gu_low, inner)
    grad_second = parts[0]
    for part in got:
        grad_second = grad_second + part.astype(f32)
    grad_ffn = lax.psum_scatter(grad_ffn, plane, scatter_dimension=0, tiled=True)
    state_own = state.reshape(micro, 2, own, width)[:, 0]
    _, norm_pull = jax.vjp(rms_rows, state_own, ffn_gain)
    grad_state_norm, grad_ffn_gain = norm_pull(grad_second)
    grad_state = (cotangent_own.astype(f32) + grad_state_norm).astype(bf16)
    state_pieces = gather(grad_state)

    down_own, state_pieces[1] = tie(down_own, state_pieces[1])
    down = split(down_own, down_other, f32)
    down = [(down[0] + state_own).astype(bf16)] + list(down[1:])
    state_pieces[-1], down[1] = tie(state_pieces[-1], down[1])
    output = sum(swap_from_z(down[k], -k).astype(f32) for k in range(4)).astype(bf16)

    grad_own, grad_other, grad_att = back(
        *(state_pieces, normed, w_abs, raw, query, keys, values, stat, mixed, qk_gain),
        *(cosine, sine, bias, gain_rows(norm_gain), gain_rows(grad_ffn_gain)),
    )
    parts = split(grad_own, grad_other, bf16)
    got = [swap_from_z(parts[k], -k).astype(f32) for k in range(4)]
    grad_att, got[0] = tie(grad_att, got[0])
    grad_normed = sum(got)
    grad_att = lax.all_to_all(grad_att, plane, 0, 0)
    grad_att = jnp.sum(grad_att.astype(f32), axis=0)
    gains = group_sum(grad_att[64:70].reshape(-1))
    grad_att = swap(grad_att[:64])
    _, first_pull = jax.vjp(rms_rows, tokens.astype(f32), norm_gain)
    grad_resid_norm, _ = first_pull(grad_normed)
    input_grad = (swap(grad_state).astype(f32) + grad_resid_norm).astype(bf16)
    grad_ffn = swap(grad_ffn).astype(f32)
    both = nq + nk
    q_gains = gains[2 * width :]
    return (
        output,
        input_grad,
        grad_att[:, :nq],
        grad_att[:, nq:both],
        grad_att[:, both : both + nk],
        grad_att[:, both + nk :].T,
        grad_ffn[:, :hidden],
        grad_ffn[:, hidden : 2 * hidden],
        grad_ffn[:, 2 * hidden :].T,
        gains[:width],
        gains[width : 2 * width],
        q_gains[:head_size] + q_gains[head_size : 2 * head_size],
        q_gains[2 * head_size : 3 * head_size],
    )


def solution(mesh):
    inner = Mesh(mesh.devices.reshape(4, 2, 2, 4, 2), axes)
    dp, mp = ("y", "xh", "core"), ("z", "xl")
    rows = P(None, dp + mp, None)
    weight_in = [P(dp, mp)] * 3 + [P(mp, dp)] + [P(dp, mp)] * 2 + [P(mp, dp)]
    return jax.shard_map(
        local,
        mesh=inner,
        in_specs=tuple([rows, P(None, dp), rows] + weight_in + [P()] * 4),
        out_specs=tuple([rows, rows] + weight_in + [P()] * 4),
        check_vma=False,
    )
```

```python
import jax
import jax.numpy as jnp
from jax import lax
from jax.experimental import pallas as pl
from jax.experimental.pallas import tpu as pltpu
from jax.sharding import Mesh, PartitionSpec as P

eps = 1e-05
rope_base = 1000000.0
axes = ("y", "xh", "core", "z", "xl")
plane = ("y", "xh", "xl")
CORE = [(0, 1), (1, 0)]
bf16 = jnp.bfloat16
f32 = jnp.float32
VMEM = 60 * 2**20


def product(left, right):
    return jnp.dot(left, right, preferred_element_type=jnp.float32)


def product_nt(left, right):
    return lax.dot_general(
        left, right, (((1,), (1,)), ((), ())), preferred_element_type=jnp.float32
    )


def product_tn(left, right):
    return lax.dot_general(
        left, right, (((0,), (0,)), ((), ())), preferred_element_type=jnp.float32
    )


def rms_scale(value):
    return lax.rsqrt(jnp.mean(value * value, axis=-1, keepdims=True) + eps)


def rms_rows(value, gain):
    return value * rms_scale(value) * gain


def swap(value):
    return lax.ppermute(
        value, ("core", "xl"), [(a * 2 + b, b * 2 + a) for a in range(2) for b in range(2)]
    )


def from_z(value, k):
    return lax.ppermute(value, "z", [(z, (z - k) % 4) for z in range(4)])


def swap_from_x(value, k):
    perm = []
    for xh in range(2):
        for a in range(2):
            for b in range(2):
                x = (xh * 2 + a - k) % 4
                perm.append((xh * 4 + a * 2 + b, (x // 2) * 4 + b * 2 + x % 2))
    return lax.ppermute(value, ("xh", "core", "xl"), perm)


def from_y(value, k):
    return lax.ppermute(value, "y", [(y, (y - k) % 4) for y in range(4)])


def other_core(value):
    return lax.ppermute(value, "core", CORE)


def from_chain(value):
    return [value] + [from_z(value, k) for k in (1, 2, 3)]


def gather_chains(pieces):
    chain = jnp.stack(pieces)
    return chain, other_core(chain)


def gather(value):
    chain = tie(*from_chain(value))
    return chain + [other_core(v) for v in chain]


def ordered(value, z, core, axis):
    shape = value.shape
    block = shape[axis] // 8
    v = value.reshape(shape[:axis] + (4, 2, block) + shape[axis + 1 :])
    v = lax.dynamic_slice_in_dim(jnp.concatenate([v, v], axis), z, 4, axis)
    v = lax.dynamic_slice_in_dim(jnp.concatenate([v, v], axis + 1), core, 2, axis + 1)
    return jnp.swapaxes(v, axis, axis + 1).reshape(shape)


def group_sum(value):
    value = value + other_core(value)
    return value + sum(from_z(value, k) for k in (1, 2, 3))


def tie(*values):
    return list(lax.optimization_barrier(values))


def halves(value):
    lane = lax.broadcasted_iota(jnp.int32, value.shape, value.ndim - 1)
    return lane < 64


def quarter(value):
    lane = lax.broadcasted_iota(jnp.int32, value.shape, value.ndim - 1)
    return (lane & 32) == 0


def turn(value):
    return jnp.where(quarter(value), -pltpu.roll(value, 96, 1), pltpu.roll(value, 32, 1))


def turn_back(value):
    return jnp.where(quarter(value), pltpu.roll(value, 96, 1), -pltpu.roll(value, 32, 1))


def head_mean(value):
    low = halves(value)
    first = jnp.sum(jnp.where(low, value, 0.0), axis=-1, keepdims=True)
    second = jnp.sum(jnp.where(low, 0.0, value), axis=-1, keepdims=True)
    return jnp.where(low, first, second) * (1.0 / 64)


def attend_kernel(at_ref, *refs):
    x_refs, w_refs = refs[:2], refs[2:6]
    gain_ref, qk_gain_ref, cos_ref, sin_ref, bias_ref = refs[6:11]
    mixed_ref, x_ref, normed_ref, w_ref, raw_ref, q_ref, kk_ref, vv_ref, stat_ref = refs[11:]

    @pl.when(pl.program_id(0) == 0)
    def _():
        for ky in range(4):
            for kx in range(4):
                row = lax.rem(at_ref[0] + ky, 4) * 256 + lax.rem(at_ref[1] + kx, 4) * 64
                row = pl.multiple_of(row, 64)
                w_ref[pl.ds(row, 64), :] = w_refs[ky][kx * 64 : kx * 64 + 64, :]

    for i in range(8):
        block = x_refs[i // 4][i % 4, 0]
        x_ref[i * 64 : i * 64 + 64, :] = block
        block = block.astype(f32)
        normed_ref[i * 64 : i * 64 + 64, :] = (
            block * rms_scale(block) * gain_ref[0:1, :]
        ).astype(bf16)
    raw = product(normed_ref[...], w_ref[:, :256])
    raw_ref[...] = raw
    cosine, sine = cos_ref[0], sin_ref[0]
    query, kv = raw[:, :128], raw[:, 128:]
    low = halves(kv)
    query = query * lax.rsqrt(head_mean(query * query) + eps) * qk_gain_ref[0:1, :]
    q_ref[...] = (query * cosine + turn(query) * sine).astype(bf16)
    key = kv * lax.rsqrt(head_mean(kv * kv) + eps) * qk_gain_ref[1:2, :]
    key = key * cosine + turn(key) * sine
    kk_ref[...] = jnp.where(low, key, pltpu.roll(key, 64, 1)).astype(bf16)
    vv_ref[...] = jnp.where(low, pltpu.roll(kv, 64, 1), kv).astype(bf16)
    keys, values = kk_ref[...], vv_ref[...]
    for rows in (slice(0, 256), slice(256, 512)):
        queries = q_ref[rows, :]
        low = halves(queries)
        bias = bias_ref[0, rows, :].astype(f32)
        parts = []
        for head in range(2):
            one = jnp.where(low == (head == 0), queries, jnp.zeros_like(queries))
            scores = product_nt(one, keys) * 0.125 + bias
            top = jnp.max(scores, axis=-1, keepdims=True)
            expo = jnp.exp(scores - top)
            total = jnp.sum(expo, axis=-1, keepdims=True)
            weights = (expo * (1.0 / total)).astype(bf16)
            parts.append((product(weights, values), top + jnp.log(total)))
        first = halves(parts[0][0])
        mixed_ref[rows, :] = jnp.where(first, parts[0][0], parts[1][0]).astype(bf16)
        stat_ref[rows, :] = jnp.where(first, parts[0][1], parts[1][1])


def attend(at, pieces, weights, gain, qk_gain, cosine, sine, bias):
    width = pieces[0].shape[3]
    micro = pieces[0].shape[1]
    group = 512
    chain = pl.BlockSpec((4, 1, 64, width), lambda m, at: (0, m, 0, 0))
    whole = lambda a: pl.BlockSpec(a.shape, lambda m, at: (0,) * a.ndim)
    part = lambda a: pl.BlockSpec((1,) + a.shape[1:], lambda m, at: (m, 0, 0))
    rows = lambda cols: pl.BlockSpec((group, cols), lambda m, at: (m, 0))
    out = lambda cols, kind: jax.ShapeDtypeStruct((micro * group, cols), kind)
    return pl.pallas_call(
        attend_kernel,
        grid_spec=pltpu.PrefetchScalarGridSpec(
            num_scalar_prefetch=1,
            grid=(micro,),
            in_specs=[chain, chain]
            + [whole(w) for w in weights]
            + [whole(gain), whole(qk_gain), part(cosine), part(sine), part(bias)],
            out_specs=[
                rows(128),
                rows(width),
                rows(width),
                pl.BlockSpec((width, 384), lambda m, at: (0, 0)),
                rows(256),
                rows(128),
                rows(128),
                rows(128),
                rows(128),
            ],
        ),
        out_shape=[
            out(128, bf16),
            out(width, bf16),
            out(width, bf16),
            jax.ShapeDtypeStruct((width, 384), bf16),
            out(256, f32),
            out(128, bf16),
            out(128, bf16),
            out(128, bf16),
            out(128, f32),
        ],
        compiler_params=pltpu.CompilerParams(vmem_limit_bytes=VMEM),
        cost_estimate=pl.CostEstimate(flops=12 * 10**9, bytes_accessed=10**7, transcendentals=10**6),
        name="attend",
    )(at, *pieces, *weights, gain, qk_gain, cosine, sine, bias)


def feed_kernel(at_ref, *refs):
    mixed_refs, w_refs = refs[:8], refs[8:10]
    x_ref, gain_ref, wf_ref = refs[10:13]
    up_refs = refs[13:15]
    state_ref, second_ref, inner_ref, low_ref, own_ref, other_ref = refs[15:21]
    up_ref, down_own_ref, down_other_ref = refs[21:24]
    w_out, mixed, w_gu = refs[24:]
    step = pl.program_id(0)
    micro, side = step // 2, lax.rem(step, 2)

    @pl.when(step == 0)
    def _():
        for i in range(8):
            for ky in range(4):
                for kx in range(4):
                    row = lax.rem(at_ref[0] + ky, 4) * 256 + lax.rem(at_ref[1] + kx, 4) * 64
                    row = pl.multiple_of(row, 64)
                    w_out[pl.ds(row, 64), i * 128 : i * 128 + 128] = w_refs[i // 4][
                        i % 4, ky * 256 + kx * 64 : ky * 256 + kx * 64 + 64, :
                    ]
        for rows in (slice(i, i + 128) for i in range(0, w_gu.shape[0], 128)):
            w_gu[rows, :512] = wf_ref[rows, :512]
            rest = wf_ref[rows, 512:1152].astype(f32)
            w_gu[rows, 512:] = pltpu.roll(rest, 576, 1).astype(bf16)

    for i, ref in enumerate(up_refs):

        @pl.when(side == i)
        def _():
            for j in range(4):
                up_ref[j * 64 : j * 64 + 64, :] = ref[j, 0]

    for i, ref in enumerate(mixed_refs):
        flip, k = i // 4, i % 4
        base = micro * 512 + lax.rem(side + flip, 2) * 256
        for j in range(4):
            row = pl.multiple_of(base + (j - k) % 4 * 64, 64)
            mixed[j * 64 : j * 64 + 64, i * 128 : i * 128 + 128] = ref[pl.ds(row, 64), :]
    state = x_ref[...].astype(f32) + product_nt(mixed[...], w_out[...])
    state_ref[...] = state[:64]
    second = (state * rms_scale(state) * gain_ref[0:1, :]).astype(bf16)
    second_ref[...] = second
    both = product(second, w_gu[...])
    grad_inner = product(up_ref[...], wf_ref[:, 1152:1728])

    def glu(gate, up, grad):
        sig = 1.0 / (1.0 + jnp.exp(-gate))
        silu = gate * sig
        inner = (silu * up).astype(bf16)
        grad_gate = (grad * up * sig * (1.0 + gate * (1.0 - sig))).astype(bf16)
        return inner, grad_gate, (grad * silu).astype(bf16)

    inner, grad_gate, grad_up = glu(both[:, :512], both[:, 512:1024], grad_inner[:, :512])
    inner_ref[:, :512] = inner
    low_ref[:, :512] = grad_gate
    low_ref[:, 512:1024] = grad_up
    tail = both[:, 1024:]
    gate_tail = pltpu.roll(tail, 64, 1)
    inner, grad_gate, grad_up = glu(gate_tail[:, :64], tail[:, :64], grad_inner[:, 512:])
    inner_ref[:, 512:] = inner
    low_ref[:, 1024:1088] = grad_up
    low_ref[:, 1088:] = grad_gate
    grad = product_nt(low_ref[...], w_gu[...]).astype(bf16)
    down = product_nt(inner_ref[...], wf_ref[:, 1152:]).astype(bf16)

    @pl.when(side == 0)
    def _():
        own_ref[0] = grad
        down_own_ref[0] = down

    @pl.when(side == 1)
    def _():
        other_ref[0] = grad
        down_other_ref[0] = down


def feed(at, mixed, w_out, x, cotangent, gain, w_ffn):
    count, width = x.shape
    steps = count // 256
    whole = lambda a: pl.BlockSpec(a.shape, lambda b, at: (0,) * a.ndim)
    rows = lambda cols, block=256: pl.BlockSpec((block, cols), lambda b, at: (b, 0))
    half = pl.BlockSpec((1, 256, width), lambda b, at: (b // 2, 0, 0))
    out = lambda shape, kind: jax.ShapeDtypeStruct(shape, kind)

    chain = pl.BlockSpec((4, 1, 64, width), lambda b, at: (0, b // 2, 0, 0))
    return pl.pallas_call(
        feed_kernel,
        grid_spec=pltpu.PrefetchScalarGridSpec(
            num_scalar_prefetch=1,
            grid=(steps,),
            in_specs=[whole(p) for p in mixed]
            + [whole(w) for w in w_out]
            + [rows(width), whole(gain), whole(w_ffn)]
            + [chain, chain],
            out_specs=[rows(width, 64), rows(width), rows(576), rows(1152)]
            + [half, half, rows(width), half, half],
            scratch_shapes=[
                pltpu.VMEM((width, 1024), bf16),
                pltpu.VMEM((256, 1024), bf16),
                pltpu.VMEM((width, 1152), bf16),
            ],
        ),
        out_shape=[
            out((steps * 64, width), f32),
            out((count, width), bf16),
            out((count, 576), bf16),
            out((count, 1152), bf16),
            out((steps // 2, 256, width), bf16),
            out((steps // 2, 256, width), bf16),
            out((count, width), bf16),
            out((steps // 2, 256, width), bf16),
            out((steps // 2, 256, width), bf16),
        ],
        compiler_params=pltpu.CompilerParams(vmem_limit_bytes=VMEM),
        cost_estimate=pl.CostEstimate(flops=9 * 10**9, bytes_accessed=10**7, transcendentals=10**6),
        name="feed",
    )(at, *mixed, *w_out, x, gain, w_ffn, *cotangent)


def weights_kernel(second_ref, up_ref, low_ref, inner_ref, grad_ref):
    grad = product_tn(second_ref[...], low_ref[...])
    grad_ref[:, :512] = grad[:, :512].astype(bf16)
    grad_ref[:, 512:1152] = pltpu.roll(grad[:, 512:], 64, 1).astype(bf16)
    grad_ref[:, 1152:] = product_tn(up_ref[...], inner_ref[...]).astype(bf16)


def weights_back(second, upstream, low, inner):
    count, width = second.shape
    whole = lambda a: pl.BlockSpec(a.shape, lambda b: (0,) * a.ndim)
    columns = pl.BlockSpec((count, 256), lambda b: (0, b))
    return pl.pallas_call(
        weights_kernel,
        grid=(width // 256,),
        in_specs=[columns, columns, whole(low), whole(inner)],
        out_specs=pl.BlockSpec((256, 1728), lambda b: (b, 0)),
        out_shape=jax.ShapeDtypeStruct((width, 1728), bf16),
        compiler_params=pltpu.CompilerParams(vmem_limit_bytes=VMEM),
        cost_estimate=pl.CostEstimate(flops=4 * 10**9, bytes_accessed=10**7, transcendentals=0),
        name="weights_back",
    )(second, upstream, low, inner)


def back_kernel(*refs):
    state_refs = refs[:8]
    normed_ref, w_ref, raw_ref, q_ref, kk_ref, vv_ref, stat_ref, mixed_ref = refs[8:16]
    qk_gain_ref, cos_ref, sin_ref, bias_ref, gain_ref, ffn_ref = refs[16:22]
    own_ref, other_ref, grad_ref = refs[22:25]
    state, low_ref, total, norm_ref, qk_grad_ref = refs[25:]
    step = pl.program_id(0)
    for i, ref in enumerate(state_refs):
        state[i * 64 : i * 64 + 64, :] = ref[0]
    grad_mixed = product(state[...], w_ref[:, 256:]).astype(bf16)
    keys, values = kk_ref[...], vv_ref[...]
    grad_key = jnp.zeros((512, 128), f32)
    grad_value = jnp.zeros((512, 128), f32)
    grad_query = []
    for rows in (slice(0, 256), slice(256, 512)):
        queries, grads = q_ref[rows, :], grad_mixed[rows, :]
        low = halves(queries)
        bias = bias_ref[0, rows, :].astype(f32)
        parts = []
        for head in range(2):
            keep = low == (head == 0)
            one = jnp.where(keep, queries, jnp.zeros_like(queries))
            grad_one = jnp.where(keep, grads, jnp.zeros_like(grads))
            scores = product_nt(one, keys) * 0.125 + bias
            soft = jnp.exp(scores - stat_ref[rows, head * 64 : head * 64 + 1])
            grad_weights = product_nt(grad_one, values)
            center = jnp.sum(soft * grad_weights, axis=-1, keepdims=True)
            grad_scores = (soft * (grad_weights - center)).astype(bf16)
            parts.append(product(grad_scores, keys))
            grad_key = grad_key + product_tn(grad_scores, one)
            grad_value = grad_value + product_tn(soft.astype(bf16), grad_one)
        grad_query.append(jnp.where(halves(parts[0]), parts[0], parts[1]))
    cosine, sine = cos_ref[0], sin_ref[0]

    def prepare_back(grad, raw, gain):
        grad = grad * cosine + turn_back(grad * sine)
        scale = lax.rsqrt(head_mean(raw * raw) + eps)
        unit = raw * scale
        grad_gain = jnp.sum(grad * unit, axis=0, keepdims=True)
        scaled = grad * gain
        return scale * (scaled - unit * head_mean(scaled * unit)), grad_gain

    raw = raw_ref[...]
    grad_q = jnp.concatenate(grad_query, axis=0) * 0.125
    grad_q, gain_q = prepare_back(grad_q, raw[:, :128], qk_gain_ref[0:1, :])
    grad_key = (grad_key + pltpu.roll(grad_key, 64, 1)) * 0.125
    grad_value = grad_value + pltpu.roll(grad_value, 64, 1)
    low = halves(grad_value)
    raw_k = jnp.where(low, raw[:, 128:], 0.0)
    grad_k, gain_k = prepare_back(jnp.where(low, grad_key, 0.0), raw_k, qk_gain_ref[1:2, :])
    low_ref[:, :128] = grad_q.astype(bf16)
    low_ref[:, 128:] = jnp.where(low, grad_k, grad_value).astype(bf16)

    @pl.when(step == 0)
    def _():
        total[...] = jnp.zeros_like(total)
        norm_ref[...] = jnp.zeros_like(norm_ref)
        qk_grad_ref[...] = jnp.zeros_like(qk_grad_ref)

    qk_grad_ref[0:1, :] += gain_q
    qk_grad_ref[1:2, :] += gain_k
    for rows, ref in ((slice(0, 256), own_ref), (slice(256, 512), other_ref)):
        grad = product_nt(low_ref[rows, :], w_ref[:, :256])
        ref[0] = grad.astype(bf16)
        norm_ref[0:1, :] += jnp.sum(grad * normed_ref[rows, :].astype(f32), axis=0, keepdims=True)
    total[:, :256] += product_tn(normed_ref[...], low_ref[...])
    total[:, 256:] += product_tn(state[...], mixed_ref[...])

    @pl.when(step == pl.num_programs(0) - 1)
    def _():
        norm = norm_ref[0:1, :] / gain_ref[0:1, :]
        chunks = [norm[:, i : i + 128] for i in range(0, 1024, 128)]
        chunks += [ffn_ref[0:1, i : i + 128] for i in range(0, 1024, 128)]
        chunks += [qk_grad_ref[0:1, :], qk_grad_ref[1:2, :]]
        lines = [jnp.concatenate(chunks[i : i + 3], axis=1) for i in range(0, 18, 3)]
        lines = jnp.concatenate(lines + [jnp.zeros((10, 384), f32)], axis=0).astype(bf16)
        for i in range(16):
            grad_ref[i, :64, :] = total[i * 64 : i * 64 + 64, :].astype(bf16)
            grad_ref[i, 64:, :] = lines


def back(
    state, normed, w_att, raw, query, keys, values, stat, mixed, qk_gain, cosine, sine, bias, gain, ffn
):
    width = state[0].shape[2]
    micro = state[0].shape[0]
    whole = lambda a: pl.BlockSpec(a.shape, lambda m: (0,) * a.ndim)
    part = lambda a: pl.BlockSpec((1,) + a.shape[1:], lambda m: (m, 0, 0))
    rows = lambda a: pl.BlockSpec((512, a.shape[1]), lambda m: (m, 0))
    half = pl.BlockSpec((1, 256, width), lambda m: (m, 0, 0))
    out = jax.ShapeDtypeStruct
    return pl.pallas_call(
        back_kernel,
        grid=(micro,),
        in_specs=[part(p) for p in state]
        + [rows(normed), whole(w_att), rows(raw), rows(query), rows(keys), rows(values)]
        + [rows(stat), rows(mixed), whole(qk_gain), part(cosine), part(sine), part(bias)]
        + [whole(gain), whole(ffn)],
        out_specs=[half, half, pl.BlockSpec((16, 80, 384), lambda m: (0, 0, 0))],
        scratch_shapes=[
            pltpu.VMEM((512, width), bf16),
            pltpu.VMEM((512, 256), bf16),
            pltpu.VMEM((width, 384), f32),
            pltpu.VMEM((8, width), f32),
            pltpu.VMEM((8, 128), f32),
        ],
        out_shape=[
            out((micro, 256, width), bf16),
            out((micro, 256, width), bf16),
            out((16, 80, 384), bf16),
        ],
        compiler_params=pltpu.CompilerParams(vmem_limit_bytes=VMEM),
        cost_estimate=pl.CostEstimate(flops=15 * 10**9, bytes_accessed=10**7, transcendentals=10**6),
        name="back",
    )(
        *(*state, normed, w_att, raw, query, keys, values, stat, mixed),
        *(qk_gain, cosine, sine, bias, gain, ffn),
    )


def split_kernel(*refs):
    count = len(refs) // 2 - 2
    for i in range(count):
        own_ref, got_ref = refs[2 * i], refs[2 * i + 1]
        micro = own_ref.shape[0]
        for k, ref in enumerate(refs[-4:]):
            rows = slice(k * 64, k * 64 + 64)
            value = own_ref[:, rows].astype(f32) + got_ref[:, rows].astype(f32)
            ref[i * micro : (i + 1) * micro] = value.astype(ref.dtype)


def split(own, other, *more):
    micro, _, width = own.shape
    values = (own, other_core(other)) + more
    out = lambda kind: jax.ShapeDtypeStruct((len(values) // 2 * micro, 64, width), kind)
    return pl.pallas_call(
        split_kernel,
        out_shape=[out(f32), out(bf16), out(bf16), out(bf16)],
        compiler_params=pltpu.CompilerParams(vmem_limit_bytes=VMEM),
        name="split",
    )(*values)


def local(
    tokens,
    segment_ids,
    cotangent,
    w_query,
    w_key,
    w_value,
    w_out,
    w_gate,
    w_up,
    w_down,
    norm_gain,
    ffn_gain,
    query_gain,
    key_gain,
):
    micro, own, width = tokens.shape
    head_size = query_gain.shape[0]
    nq = w_query.shape[1]
    nk = w_key.shape[1]
    group = segment_ids.shape[1]
    hidden = w_gate.shape[1]
    z = lax.axis_index("z")
    core = lax.axis_index("core")
    at = jnp.stack([lax.axis_index("y"), lax.axis_index("xh") * 2 + lax.axis_index("xl"), z, core])
    at = at.astype(jnp.int32)

    segment = swap(segment_ids)
    tokens_own = swap(jnp.concatenate([tokens, cotangent]))
    w_att = jnp.concatenate([w_query, w_key, w_value, w_out.T], axis=1)
    w_att = jnp.concatenate([swap_from_x(w_att, k) for k in range(4)], axis=0)
    w_ffn = jnp.concatenate([w_gate, w_up, w_down.T], axis=1)
    w_att, tokens_own, segment, w_ffn = tie(w_att, tokens_own, segment, w_ffn)
    token_pieces = from_chain(tokens_own)
    w_att = [w_att] + [from_y(w_att, k) for k in (1, 2, 3)]
    w_ffn = swap(w_ffn)

    index = jnp.arange(group, dtype=jnp.int32)
    change = jnp.concatenate(
        [jnp.ones((micro, 1), dtype=bool), segment[:, 1:] != segment[:, :-1]], axis=1
    )
    start = lax.cummax(jnp.where(change, index, 0), axis=1)
    start = ordered(start, z, core, 1)
    index = ordered(index[None], z, core, 1)
    place = (index - start).astype(f32)
    freq = rope_base ** (-(jnp.arange(head_size // 2, dtype=f32) * 2.0 / head_size))
    angle = place[:, :, None] * jnp.tile(freq, 4)
    cosine, sine = jnp.cos(angle), jnp.sin(angle)
    allowed = (start[:, :, None] == start[:, None, :]) & (index[:, :, None] >= index[:, None, :])
    bias = jnp.where(allowed, 0.0, -1e30).astype(bf16)
    qk_gain = jnp.stack([jnp.tile(query_gain, 2), jnp.tile(key_gain, 2)])

    w_ffn, *w_att = tie(w_ffn, *w_att)
    w_ffn = lax.all_gather(w_ffn, plane, axis=0, tiled=True)
    w_out_chain = from_chain(jnp.concatenate([w[:, nq + 2 * nk :] for w in w_att], axis=0))
    token_pieces = tie(*token_pieces)
    x_chain, x_other = gather_chains([piece[:micro] for piece in token_pieces])
    cotangent_all = gather_chains([piece[micro:] for piece in token_pieces])

    mixed, x, normed, w_abs, raw, query, keys, values, stat = attend(
        at, (x_chain, x_other), w_att, norm_gain.reshape(1, width), qk_gain, cosine, sine, bias
    )
    mixed, *w_out_chain = tie(mixed, *w_out_chain)
    w_out_all = gather_chains(w_out_chain)
    mixed_pieces = gather(mixed)
    state, second, inner, gu_low, grad_own, grad_other, upstream, down_own, down_other = feed(
        at, mixed_pieces, w_out_all, x, cotangent_all, ffn_gain.reshape(1, width), w_ffn
    )
    down_got = other_core(down_other)
    parts = split(grad_own, grad_other)
    got = [from_z(parts[k], -k) for k in (1, 2, 3)]
    grad_ffn = weights_back(second, upstream, gu_low, inner)
    got = tie(*got)
    grad_second = parts[0] + sum(piece.astype(f32) for piece in got)
    state_own = state.reshape(micro, 2, own, width)[:, 0]
    _, norm_pull = jax.vjp(rms_rows, state_own, ffn_gain)
    grad_state_norm, grad_ffn_gain = norm_pull(grad_second)
    grad_state = (tokens_own[micro:].astype(f32) + grad_state_norm).astype(bf16)
    grad_ffn, *state_pieces = tie(grad_ffn, *from_chain(grad_state))
    state_pieces += [other_core(piece) for piece in state_pieces]
    grad_ffn = lax.psum_scatter(grad_ffn, plane, scatter_dimension=0, tiled=True)

    grad_own, grad_other, grad_att = back(
        *(state_pieces, normed, w_abs, raw, query, keys, values, stat, mixed, qk_gain),
        *(cosine, sine, bias, norm_gain.reshape(1, width), grad_ffn_gain.reshape(1, width)),
    )
    grad_att = lax.all_to_all(grad_att, plane, 0, 0)
    parts = split(grad_own, grad_other, down_own, down_got)
    grad_att, *got = tie(grad_att, *[from_z(parts[k], -k) for k in (1, 2, 3)])
    total = parts[0] + sum(piece.astype(f32) for piece in got)
    _, first_pull = jax.vjp(rms_rows, tokens_own[:micro].astype(f32), norm_gain)
    grad_resid_norm, _ = first_pull(total[:micro])
    input_grad = grad_state.astype(f32) + grad_resid_norm
    results = swap(jnp.concatenate([state_own + total[micro:], input_grad]).astype(bf16))
    grad_att = jnp.sum(grad_att.astype(f32), axis=0)
    gains = group_sum(grad_att[64:70].reshape(-1))
    grad_att = swap(grad_att[:64])
    grad_ffn = swap(grad_ffn).astype(f32)
    both = nq + nk
    q_gains = gains[2 * width :]
    return (
        results[:micro],
        results[micro:],
        grad_att[:, :nq],
        grad_att[:, nq:both],
        grad_att[:, both : both + nk],
        grad_att[:, both + nk :].T,
        grad_ffn[:, :hidden],
        grad_ffn[:, hidden : 2 * hidden],
        grad_ffn[:, 2 * hidden :].T,
        gains[:width],
        gains[width : 2 * width],
        q_gains[:head_size] + q_gains[head_size : 2 * head_size],
        q_gains[2 * head_size : 3 * head_size],
    )


def solution(mesh):
    inner = Mesh(mesh.devices.reshape(4, 2, 2, 4, 2), axes)
    dp, mp = ("y", "xh", "core"), ("z", "xl")
    rows = P(None, dp + mp, None)
    weight_in = [P(dp, mp)] * 3 + [P(mp, dp)] + [P(dp, mp)] * 2 + [P(mp, dp)]
    return jax.shard_map(
        local,
        mesh=inner,
        in_specs=tuple([rows, P(None, dp), rows] + weight_in + [P()] * 4),
        out_specs=tuple([rows, rows] + weight_in + [P()] * 4),
        check_vma=False,
    )
```

```python
import jax
import jax.numpy as jnp
from jax import lax
from jax.experimental import pallas as pl
from jax.experimental.pallas import tpu as pltpu
from jax.sharding import Mesh, PartitionSpec as P

eps = 1e-05
rope_base = 1000000.0
axes = ("y", "xh", "core", "z", "xl")
plane = ("y", "xh", "xl")
CORE = [(0, 1), (1, 0)]
bf16 = jnp.bfloat16
f32 = jnp.float32
VMEM = 60 * 2**20


def product(left, right):
    return jnp.dot(left, right, preferred_element_type=jnp.float32)


def product_nt(left, right):
    return lax.dot_general(
        left, right, (((1,), (1,)), ((), ())), preferred_element_type=jnp.float32
    )


def product_tn(left, right):
    return lax.dot_general(
        left, right, (((0,), (0,)), ((), ())), preferred_element_type=jnp.float32
    )


def rms_scale(value):
    return lax.rsqrt(jnp.mean(value * value, axis=-1, keepdims=True) + eps)


def rms_rows(value, gain):
    return value * rms_scale(value) * gain


def swap(value):
    return lax.ppermute(
        value, ("core", "xl"), [(a * 2 + b, b * 2 + a) for a in range(2) for b in range(2)]
    )


def from_z(value, k):
    return lax.ppermute(value, "z", [(z, (z - k) % 4) for z in range(4)])


def swap_from_x(value, k):
    perm = []
    for xh in range(2):
        for a in range(2):
            for b in range(2):
                x = (xh * 2 + a - k) % 4
                perm.append((xh * 4 + a * 2 + b, (x // 2) * 4 + b * 2 + x % 2))
    return lax.ppermute(value, ("xh", "core", "xl"), perm)


def to_x(value, k):
    return lax.ppermute(value, ("xh", "xl"), [(x, (x + k) % 4) for x in range(4)])


def from_y(value, k):
    return lax.ppermute(value, "y", [(y, (y - k) % 4) for y in range(4)])


def other_core(value):
    return lax.ppermute(value, "core", CORE)


def from_chain(value):
    return [value] + [from_z(value, k) for k in (1, 2, 3)]


def gather_chains(pieces):
    chain = jnp.stack(pieces)
    return chain, other_core(chain)


def gather(value):
    chain = tie(*from_chain(value))
    return chain + [other_core(v) for v in chain]


def ordered(value, z, core, axis):
    shape = value.shape
    block = shape[axis] // 8
    v = value.reshape(shape[:axis] + (4, 2, block) + shape[axis + 1 :])
    v = lax.dynamic_slice_in_dim(jnp.concatenate([v, v], axis), z, 4, axis)
    v = lax.dynamic_slice_in_dim(jnp.concatenate([v, v], axis + 1), core, 2, axis + 1)
    return jnp.swapaxes(v, axis, axis + 1).reshape(shape)


def group_sum(value):
    value = value + other_core(value)
    return value + sum(from_z(value, k) for k in (1, 2, 3))


def tie(*values):
    return list(lax.optimization_barrier(values))


def halves(value):
    lane = lax.broadcasted_iota(jnp.int32, value.shape, value.ndim - 1)
    return lane < 64


def quarter(value):
    lane = lax.broadcasted_iota(jnp.int32, value.shape, value.ndim - 1)
    return (lane & 32) == 0


def turn(value):
    return jnp.where(quarter(value), -pltpu.roll(value, 96, 1), pltpu.roll(value, 32, 1))


def turn_back(value):
    return jnp.where(quarter(value), pltpu.roll(value, 96, 1), -pltpu.roll(value, 32, 1))


def head_mean(value):
    low = halves(value)
    first = jnp.sum(jnp.where(low, value, 0.0), axis=-1, keepdims=True)
    second = jnp.sum(jnp.where(low, 0.0, value), axis=-1, keepdims=True)
    return jnp.where(low, first, second) * (1.0 / 64)


def attend_kernel(at_ref, *refs):
    x_refs, w_refs = refs[:2], refs[2:6]
    gain_ref, qk_gain_ref, cos_ref, sin_ref, bias_ref = refs[6:11]
    mixed_ref, x_ref, normed_ref, w_ref, raw_ref, q_ref, kk_ref, vv_ref, stat_ref = refs[11:]

    @pl.when(pl.program_id(0) == 0)
    def _():
        for ky in range(4):
            for kx in range(4):
                row = lax.rem(at_ref[0] + ky, 4) * 256 + lax.rem(at_ref[1] + kx, 4) * 64
                row = pl.multiple_of(row, 64)
                w_ref[pl.ds(row, 64), :] = w_refs[ky][kx * 64 : kx * 64 + 64, :]

    for i in range(8):
        block = x_refs[i // 4][i % 4, 0]
        x_ref[i * 64 : i * 64 + 64, :] = block
        block = block.astype(f32)
        normed_ref[i * 64 : i * 64 + 64, :] = (
            block * rms_scale(block) * gain_ref[0:1, :]
        ).astype(bf16)
    raw = product(normed_ref[...], w_ref[:, :256])
    raw_ref[...] = raw
    cosine, sine = cos_ref[0], sin_ref[0]
    query, kv = raw[:, :128], raw[:, 128:]
    low = halves(kv)
    query = query * lax.rsqrt(head_mean(query * query) + eps) * qk_gain_ref[0:1, :]
    q_ref[...] = (query * cosine + turn(query) * sine).astype(bf16)
    key = kv * lax.rsqrt(head_mean(kv * kv) + eps) * qk_gain_ref[1:2, :]
    key = key * cosine + turn(key) * sine
    kk_ref[...] = jnp.where(low, key, pltpu.roll(key, 64, 1)).astype(bf16)
    vv_ref[...] = jnp.where(low, pltpu.roll(kv, 64, 1), kv).astype(bf16)
    keys, values = kk_ref[...], vv_ref[...]
    for rows in (slice(0, 256), slice(256, 512)):
        queries = q_ref[rows, :]
        low = halves(queries)
        bias = bias_ref[0, rows, :].astype(f32)
        parts = []
        for head in range(2):
            one = jnp.where(low == (head == 0), queries, jnp.zeros_like(queries))
            scores = product_nt(one, keys) * 0.125 + bias
            top = jnp.max(scores, axis=-1, keepdims=True)
            expo = jnp.exp(scores - top)
            total = jnp.sum(expo, axis=-1, keepdims=True)
            weights = (expo * (1.0 / total)).astype(bf16)
            parts.append((product(weights, values), top + jnp.log(total)))
        first = halves(parts[0][0])
        mixed_ref[rows, :] = jnp.where(first, parts[0][0], parts[1][0]).astype(bf16)
        stat_ref[rows, :] = jnp.where(first, parts[0][1], parts[1][1])


def attend(at, pieces, weights, gain, qk_gain, cosine, sine, bias):
    width = pieces[0].shape[3]
    micro = pieces[0].shape[1]
    group = 512
    chain = pl.BlockSpec((4, 1, 64, width), lambda m, at: (0, m, 0, 0))
    whole = lambda a: pl.BlockSpec(a.shape, lambda m, at: (0,) * a.ndim)
    part = lambda a: pl.BlockSpec((1,) + a.shape[1:], lambda m, at: (m, 0, 0))
    rows = lambda cols: pl.BlockSpec((group, cols), lambda m, at: (m, 0))
    out = lambda cols, kind: jax.ShapeDtypeStruct((micro * group, cols), kind)
    return pl.pallas_call(
        attend_kernel,
        grid_spec=pltpu.PrefetchScalarGridSpec(
            num_scalar_prefetch=1,
            grid=(micro,),
            in_specs=[chain, chain]
            + [whole(w) for w in weights]
            + [whole(gain), whole(qk_gain), part(cosine), part(sine), part(bias)],
            out_specs=[
                rows(128),
                rows(width),
                rows(width),
                pl.BlockSpec((width, 384), lambda m, at: (0, 0)),
                rows(256),
                rows(128),
                rows(128),
                rows(128),
                rows(128),
            ],
        ),
        out_shape=[
            out(128, bf16),
            out(width, bf16),
            out(width, bf16),
            jax.ShapeDtypeStruct((width, 384), bf16),
            out(256, f32),
            out(128, bf16),
            out(128, bf16),
            out(128, bf16),
            out(128, f32),
        ],
        compiler_params=pltpu.CompilerParams(vmem_limit_bytes=VMEM),
        cost_estimate=pl.CostEstimate(flops=12 * 10**9, bytes_accessed=10**7, transcendentals=10**6),
        name="attend",
    )(at, *pieces, *weights, gain, qk_gain, cosine, sine, bias)


def state_kernel(at_ref, *refs):
    mixed_refs, w_refs = refs[:8], refs[8:10]
    x_ref, gain_ref, state_ref, second_ref, w_out, mixed = refs[10:]
    step = pl.program_id(0)
    micro, side = step // 2, lax.rem(step, 2)

    @pl.when(step == 0)
    def _():
        for i in range(8):
            for ky in range(4):
                for kx in range(4):
                    row = lax.rem(at_ref[0] + ky, 4) * 256 + lax.rem(at_ref[1] + kx, 4) * 64
                    row = pl.multiple_of(row, 64)
                    w_out[pl.ds(row, 64), i * 128 : i * 128 + 128] = w_refs[i // 4][
                        i % 4, ky * 256 + kx * 64 : ky * 256 + kx * 64 + 64, :
                    ]

    for i, ref in enumerate(mixed_refs):
        flip, k = i // 4, i % 4
        base = micro * 512 + lax.rem(side + flip, 2) * 256
        for j in range(4):
            row = pl.multiple_of(base + (j - k) % 4 * 64, 64)
            mixed[j * 64 : j * 64 + 64, i * 128 : i * 128 + 128] = ref[pl.ds(row, 64), :]
    state = x_ref[...].astype(f32) + product_nt(mixed[...], w_out[...])
    state_ref[...] = state[:64]
    second_ref[...] = (state * rms_scale(state) * gain_ref[0:1, :]).astype(bf16)


def second_norm(at, mixed, w_out, x, gain):
    count, width = x.shape
    steps = count // 256
    whole = lambda a: pl.BlockSpec(a.shape, lambda b, at: (0,) * a.ndim)
    rows = lambda block: pl.BlockSpec((block, width), lambda b, at: (b, 0))
    return pl.pallas_call(
        state_kernel,
        grid_spec=pltpu.PrefetchScalarGridSpec(
            num_scalar_prefetch=1,
            grid=(steps,),
            in_specs=[whole(p) for p in mixed]
            + [whole(w) for w in w_out]
            + [rows(256), whole(gain)],
            out_specs=[rows(64), rows(256)],
            scratch_shapes=[pltpu.VMEM((width, 1024), bf16), pltpu.VMEM((256, 1024), bf16)],
        ),
        out_shape=[
            jax.ShapeDtypeStruct((steps * 64, width), f32),
            jax.ShapeDtypeStruct((count, width), bf16),
        ],
        compiler_params=pltpu.CompilerParams(vmem_limit_bytes=VMEM),
        cost_estimate=pl.CostEstimate(flops=3 * 10**9, bytes_accessed=10**7, transcendentals=0),
        name="second_norm",
    )(at, *mixed, *w_out, x, gain)


def feed_kernel(second_ref, wf_ref, *refs):
    up_refs = refs[:2]
    inner_ref, low_ref, own_ref, other_ref = refs[2:6]
    up_ref, down_own_ref, down_other_ref, w_gu = refs[6:]
    step = pl.program_id(0)
    side = lax.rem(step, 2)

    @pl.when(step == 0)
    def _():
        for rows in (slice(i, i + 128) for i in range(0, w_gu.shape[0], 128)):
            w_gu[rows, :512] = wf_ref[rows, :512]
            rest = wf_ref[rows, 512:1152].astype(f32)
            w_gu[rows, 512:] = pltpu.roll(rest, 576, 1).astype(bf16)

    for i, ref in enumerate(up_refs):

        @pl.when(side == i)
        def _():
            for j in range(4):
                up_ref[j * 64 : j * 64 + 64, :] = ref[j, 0]

    both = product(second_ref[...], w_gu[...])
    grad_inner = product(up_ref[...], wf_ref[:, 1152:1728])

    def glu(gate, up, grad):
        sig = 1.0 / (1.0 + jnp.exp(-gate))
        silu = gate * sig
        inner = (silu * up).astype(bf16)
        grad_gate = (grad * up * sig * (1.0 + gate * (1.0 - sig))).astype(bf16)
        return inner, grad_gate, (grad * silu).astype(bf16)

    inner, grad_gate, grad_up = glu(both[:, :512], both[:, 512:1024], grad_inner[:, :512])
    inner_ref[:, :512] = inner
    low_ref[:, :512] = grad_gate
    low_ref[:, 512:1024] = grad_up
    tail = both[:, 1024:]
    gate_tail = pltpu.roll(tail, 64, 1)
    inner, grad_gate, grad_up = glu(gate_tail[:, :64], tail[:, :64], grad_inner[:, 512:])
    inner_ref[:, 512:] = inner
    low_ref[:, 1024:1088] = grad_up
    low_ref[:, 1088:] = grad_gate
    grad = product_nt(low_ref[...], w_gu[...]).astype(bf16)
    down = product_nt(inner_ref[...], wf_ref[:, 1152:]).astype(bf16)

    @pl.when(side == 0)
    def _():
        own_ref[0] = grad
        down_own_ref[0] = down

    @pl.when(side == 1)
    def _():
        other_ref[0] = grad
        down_other_ref[0] = down


def feed(second, w_ffn, cotangent):
    count, width = second.shape
    steps = count // 256
    whole = lambda a: pl.BlockSpec(a.shape, lambda b: (0,) * a.ndim)
    rows = lambda cols: pl.BlockSpec((256, cols), lambda b: (b, 0))
    half = pl.BlockSpec((1, 256, width), lambda b: (b // 2, 0, 0))
    chain = pl.BlockSpec((4, 1, 64, width), lambda b: (0, b // 2, 0, 0))
    out = lambda *shape: jax.ShapeDtypeStruct(shape, bf16)
    halves_out = out(steps // 2, 256, width)
    return pl.pallas_call(
        feed_kernel,
        grid=(steps,),
        in_specs=[rows(width), whole(w_ffn), chain, chain],
        out_specs=[rows(576), rows(1152), half, half, rows(width), half, half],
        scratch_shapes=[pltpu.VMEM((width, 1152), bf16)],
        out_shape=[
            *(out(count, 576), out(count, 1152), halves_out, halves_out),
            *(out(count, width), halves_out, halves_out),
        ],
        compiler_params=pltpu.CompilerParams(vmem_limit_bytes=VMEM),
        cost_estimate=pl.CostEstimate(flops=9 * 10**9, bytes_accessed=10**7, transcendentals=10**6),
        name="feed",
    )(second, w_ffn, *cotangent)


def weights_kernel(at_ref, second_ref, up_ref, low_ref, inner_ref, *refs):
    out_refs, total = refs[:4], refs[4]
    grad = product_tn(second_ref[...], low_ref[...])
    total[:, :512] = grad[:, :512].astype(bf16)
    total[:, 512:1152] = pltpu.roll(grad[:, 512:], 64, 1).astype(bf16)
    total[:, 1152:] = product_tn(up_ref[...], inner_ref[...]).astype(bf16)
    for k, ref in enumerate(out_refs):
        row = pl.multiple_of(lax.rem(at_ref[1] + k, 4) * 64, 64)
        ref[0] = total[pl.ds(row, 64), :]


def weights_back(at, second, upstream, low, inner):
    count, width = second.shape
    whole = lambda a: pl.BlockSpec(a.shape, lambda b, at: (0,) * a.ndim)
    columns = pl.BlockSpec((count, 256), lambda b, at: (0, lax.rem(at[0] + b, 4)))
    return pl.pallas_call(
        weights_kernel,
        grid_spec=pltpu.PrefetchScalarGridSpec(
            num_scalar_prefetch=1,
            grid=(4,),
            in_specs=[columns, columns, whole(low), whole(inner)],
            out_specs=[pl.BlockSpec((1, 64, 1728), lambda b, at: (b, 0, 0))] * 4,
            scratch_shapes=[pltpu.VMEM((256, 1728), bf16)],
        ),
        out_shape=[jax.ShapeDtypeStruct((4, 64, 1728), bf16)] * 4,
        compiler_params=pltpu.CompilerParams(vmem_limit_bytes=VMEM),
        cost_estimate=pl.CostEstimate(flops=4 * 10**9, bytes_accessed=10**7, transcendentals=0),
        name="weights_back",
    )(at, second, upstream, low, inner)


def rows_kernel(*refs):
    for k, out_ref in enumerate(refs[4:]):
        value = sum(ref[k].astype(f32) for ref in refs[:4])
        out_ref[...] = value.astype(out_ref.dtype)


def sum_rows(values):
    shape = values[0].shape[1:]
    return pl.pallas_call(
        rows_kernel,
        out_shape=[jax.ShapeDtypeStruct(shape, f32)] + [jax.ShapeDtypeStruct(shape, bf16)] * 3,
        compiler_params=pltpu.CompilerParams(vmem_limit_bytes=VMEM),
        name="sum_rows",
    )(*values)


def back_kernel(*refs):
    state_refs = refs[:8]
    normed_ref, w_ref, raw_ref, q_ref, kk_ref, vv_ref, stat_ref, mixed_ref = refs[8:16]
    qk_gain_ref, cos_ref, sin_ref, bias_ref, gain_ref, ffn_ref = refs[16:22]
    own_ref, other_ref, grad_ref = refs[22:25]
    state, low_ref, total, norm_ref, qk_grad_ref = refs[25:]
    step = pl.program_id(0)
    for i, ref in enumerate(state_refs):
        state[i * 64 : i * 64 + 64, :] = ref[0]
    grad_mixed = product(state[...], w_ref[:, 256:]).astype(bf16)
    keys, values = kk_ref[...], vv_ref[...]
    grad_key = jnp.zeros((512, 128), f32)
    grad_value = jnp.zeros((512, 128), f32)
    grad_query = []
    for rows in (slice(0, 256), slice(256, 512)):
        queries, grads = q_ref[rows, :], grad_mixed[rows, :]
        low = halves(queries)
        bias = bias_ref[0, rows, :].astype(f32)
        parts = []
        for head in range(2):
            keep = low == (head == 0)
            one = jnp.where(keep, queries, jnp.zeros_like(queries))
            grad_one = jnp.where(keep, grads, jnp.zeros_like(grads))
            scores = product_nt(one, keys) * 0.125 + bias
            soft = jnp.exp(scores - stat_ref[rows, head * 64 : head * 64 + 1])
            grad_weights = product_nt(grad_one, values)
            center = jnp.sum(soft * grad_weights, axis=-1, keepdims=True)
            grad_scores = (soft * (grad_weights - center)).astype(bf16)
            parts.append(product(grad_scores, keys))
            grad_key = grad_key + product_tn(grad_scores, one)
            grad_value = grad_value + product_tn(soft.astype(bf16), grad_one)
        grad_query.append(jnp.where(halves(parts[0]), parts[0], parts[1]))
    cosine, sine = cos_ref[0], sin_ref[0]

    def prepare_back(grad, raw, gain):
        grad = grad * cosine + turn_back(grad * sine)
        scale = lax.rsqrt(head_mean(raw * raw) + eps)
        unit = raw * scale
        grad_gain = jnp.sum(grad * unit, axis=0, keepdims=True)
        scaled = grad * gain
        return scale * (scaled - unit * head_mean(scaled * unit)), grad_gain

    raw = raw_ref[...]
    grad_q = jnp.concatenate(grad_query, axis=0) * 0.125
    grad_q, gain_q = prepare_back(grad_q, raw[:, :128], qk_gain_ref[0:1, :])
    grad_key = (grad_key + pltpu.roll(grad_key, 64, 1)) * 0.125
    grad_value = grad_value + pltpu.roll(grad_value, 64, 1)
    low = halves(grad_value)
    raw_k = jnp.where(low, raw[:, 128:], 0.0)
    grad_k, gain_k = prepare_back(jnp.where(low, grad_key, 0.0), raw_k, qk_gain_ref[1:2, :])
    low_ref[:, :128] = grad_q.astype(bf16)
    low_ref[:, 128:] = jnp.where(low, grad_k, grad_value).astype(bf16)

    @pl.when(step == 0)
    def _():
        total[...] = jnp.zeros_like(total)
        norm_ref[...] = jnp.zeros_like(norm_ref)
        qk_grad_ref[...] = jnp.zeros_like(qk_grad_ref)

    qk_grad_ref[0:1, :] += gain_q
    qk_grad_ref[1:2, :] += gain_k
    for rows, ref in ((slice(0, 256), own_ref), (slice(256, 512), other_ref)):
        grad = product_nt(low_ref[rows, :], w_ref[:, :256])
        ref[0] = grad.astype(bf16)
        norm_ref[0:1, :] += jnp.sum(grad * normed_ref[rows, :].astype(f32), axis=0, keepdims=True)
    total[:, :256] += product_tn(normed_ref[...], low_ref[...])
    total[:, 256:] += product_tn(state[...], mixed_ref[...])

    @pl.when(step == pl.num_programs(0) - 1)
    def _():
        norm = norm_ref[0:1, :] / gain_ref[0:1, :]
        chunks = [norm[:, i : i + 128] for i in range(0, 1024, 128)]
        chunks += [ffn_ref[0:1, i : i + 128] for i in range(0, 1024, 128)]
        chunks += [qk_grad_ref[0:1, :], qk_grad_ref[1:2, :]]
        lines = [jnp.concatenate(chunks[i : i + 3], axis=1) for i in range(0, 18, 3)]
        lines = jnp.concatenate(lines + [jnp.zeros((10, 384), f32)], axis=0).astype(bf16)
        for i in range(16):
            grad_ref[i, :64, :] = total[i * 64 : i * 64 + 64, :].astype(bf16)
            grad_ref[i, 64:, :] = lines


def back(
    state, normed, w_att, raw, query, keys, values, stat, mixed, qk_gain, cosine, sine, bias, gain, ffn
):
    width = state[0].shape[2]
    micro = state[0].shape[0]
    whole = lambda a: pl.BlockSpec(a.shape, lambda m: (0,) * a.ndim)
    part = lambda a: pl.BlockSpec((1,) + a.shape[1:], lambda m: (m, 0, 0))
    rows = lambda a: pl.BlockSpec((512, a.shape[1]), lambda m: (m, 0))
    half = pl.BlockSpec((1, 256, width), lambda m: (m, 0, 0))
    out = jax.ShapeDtypeStruct
    return pl.pallas_call(
        back_kernel,
        grid=(micro,),
        in_specs=[part(p) for p in state]
        + [rows(normed), whole(w_att), rows(raw), rows(query), rows(keys), rows(values)]
        + [rows(stat), rows(mixed), whole(qk_gain), part(cosine), part(sine), part(bias)]
        + [whole(gain), whole(ffn)],
        out_specs=[half, half, pl.BlockSpec((16, 80, 384), lambda m: (0, 0, 0))],
        scratch_shapes=[
            pltpu.VMEM((512, width), bf16),
            pltpu.VMEM((512, 256), bf16),
            pltpu.VMEM((width, 384), f32),
            pltpu.VMEM((8, width), f32),
            pltpu.VMEM((8, 128), f32),
        ],
        out_shape=[
            out((micro, 256, width), bf16),
            out((micro, 256, width), bf16),
            out((16, 80, 384), bf16),
        ],
        compiler_params=pltpu.CompilerParams(vmem_limit_bytes=VMEM),
        cost_estimate=pl.CostEstimate(flops=15 * 10**9, bytes_accessed=10**7, transcendentals=10**6),
        name="back",
    )(
        *(*state, normed, w_att, raw, query, keys, values, stat, mixed),
        *(qk_gain, cosine, sine, bias, gain, ffn),
    )


def split_kernel(own_ref, got_ref, *refs):
    for k, ref in enumerate(refs):
        rows = slice(k * 64, k * 64 + 64)
        value = own_ref[:, rows].astype(f32) + got_ref[:, rows].astype(f32)
        ref[...] = value.astype(ref.dtype)


def split(own, got):
    micro, _, width = own.shape
    out = lambda kind: jax.ShapeDtypeStruct((micro, 64, width), kind)
    return pl.pallas_call(
        split_kernel,
        out_shape=[out(f32), out(bf16), out(bf16), out(bf16)],
        compiler_params=pltpu.CompilerParams(vmem_limit_bytes=VMEM),
        name="split",
    )(own, got)


def local(
    tokens,
    segment_ids,
    cotangent,
    w_query,
    w_key,
    w_value,
    w_out,
    w_gate,
    w_up,
    w_down,
    norm_gain,
    ffn_gain,
    query_gain,
    key_gain,
):
    micro, own, width = tokens.shape
    head_size = query_gain.shape[0]
    nq = w_query.shape[1]
    nk = w_key.shape[1]
    group = segment_ids.shape[1]
    hidden = w_gate.shape[1]
    z = lax.axis_index("z")
    core = lax.axis_index("core")
    at = jnp.stack([lax.axis_index("y"), lax.axis_index("xh") * 2 + lax.axis_index("xl"), z, core])
    at = at.astype(jnp.int32)

    segment = swap(segment_ids)
    x_own = swap(tokens)
    w_att = jnp.concatenate([w_query, w_key, w_value, w_out.T], axis=1)
    w_att = jnp.concatenate([swap_from_x(w_att, k) for k in range(4)], axis=0)
    w_att, x_own, segment = tie(w_att, x_own, segment)
    x_pieces = from_chain(x_own)
    w_att = [w_att] + [from_y(w_att, k) for k in (1, 2, 3)]
    w_ffn = swap(jnp.concatenate([w_gate, w_up, w_down.T], axis=1))
    cotangent_own = swap(cotangent)

    index = jnp.arange(group, dtype=jnp.int32)
    change = jnp.concatenate(
        [jnp.ones((micro, 1), dtype=bool), segment[:, 1:] != segment[:, :-1]], axis=1
    )
    start = lax.cummax(jnp.where(change, index, 0), axis=1)
    start = ordered(start, z, core, 1)
    index = ordered(index[None], z, core, 1)
    place = (index - start).astype(f32)
    freq = rope_base ** (-(jnp.arange(head_size // 2, dtype=f32) * 2.0 / head_size))
    angle = place[:, :, None] * jnp.tile(freq, 4)
    cosine, sine = jnp.cos(angle), jnp.sin(angle)
    allowed = (start[:, :, None] == start[:, None, :]) & (index[:, :, None] >= index[:, None, :])
    bias = jnp.where(allowed, 0.0, -1e30).astype(bf16)
    qk_gain = jnp.stack([jnp.tile(query_gain, 2), jnp.tile(key_gain, 2)])

    w_ffn, *pieces = tie(w_ffn, *w_att, *x_pieces)
    w_att, x_pieces = pieces[:4], pieces[4:]
    w_ffn = lax.all_gather(w_ffn, plane, axis=0, tiled=True)
    w_out_chain = from_chain(jnp.concatenate([w[:, nq + 2 * nk :] for w in w_att], axis=0))
    x_chain, x_other = gather_chains(x_pieces)

    mixed, x, normed, w_abs, raw, query, keys, values, stat = attend(
        at, (x_chain, x_other), w_att, norm_gain.reshape(1, width), qk_gain, cosine, sine, bias
    )
    mixed, *chains = tie(mixed, *w_out_chain, *from_chain(cotangent_own))
    w_out_all = gather_chains(chains[:4])
    cotangent_all = gather_chains(chains[4:])
    state, second = second_norm(at, gather(mixed), w_out_all, x, ffn_gain.reshape(1, width))
    inner, gu_low, grad_own, grad_other, upstream, down_own, down_other = feed(
        second, w_ffn, cotangent_all
    )
    parts = split(grad_own, other_core(grad_other))
    got = [from_z(parts[k], -k) for k in (1, 2, 3)]
    grad_ffn = weights_back(at, second, upstream, gu_low, inner)
    *grad_ffn, got_1, got_2, got_3 = tie(*grad_ffn, *got)
    got = [got_1, got_2, got_3]
    grad_ffn_got = [to_x(grad_ffn[k], k) for k in (1, 2, 3)]
    grad_second = parts[0] + sum(piece.astype(f32) for piece in got)
    state_own = state.reshape(micro, 2, own, width)[:, 0]
    _, norm_pull = jax.vjp(rms_rows, state_own, ffn_gain)
    grad_state_norm, grad_ffn_gain = norm_pull(grad_second)
    grad_state = (cotangent_own.astype(f32) + grad_state_norm).astype(bf16)
    down = split(down_own, other_core(down_other))
    state_pieces = from_chain(grad_state)
    *state_pieces, down_first, down_low = tie(*state_pieces, *down[:2])
    down = [down_first, down_low] + list(down[2:])
    down_got = [from_z(down[k], -k) for k in (1, 2, 3)]
    state_pieces += [other_core(piece) for piece in state_pieces]

    grad_own, grad_other, grad_att = back(
        *(state_pieces, normed, w_abs, raw, query, keys, values, stat, mixed, qk_gain),
        *(cosine, sine, bias, norm_gain.reshape(1, width), grad_ffn_gain.reshape(1, width)),
    )
    grad_att = lax.all_to_all(grad_att, plane, 0, 0)
    grad_got, *down_got = tie(other_core(grad_other), *down_got)
    output = state_own + down[0] + sum(piece.astype(f32) for piece in down_got)
    output = swap(output.astype(bf16))
    parts = split(grad_own, grad_got)
    got = [from_z(parts[k], -k) for k in (1, 2, 3)]
    grad_att, got[0], got[1], got[2], *grad_ffn_got = tie(grad_att, *got, *grad_ffn_got)
    grad_ffn = sum_rows([grad_ffn[0]] + grad_ffn_got)
    grad_ffn_got = [from_y(grad_ffn[k], -k) for k in (1, 2, 3)]
    grad_ffn = grad_ffn[0] + sum(piece.astype(f32) for piece in grad_ffn_got)
    grad_normed = parts[0] + sum(piece.astype(f32) for piece in got)
    _, first_pull = jax.vjp(rms_rows, x_own.astype(f32), norm_gain)
    grad_resid_norm, _ = first_pull(grad_normed)
    input_grad = swap((grad_state.astype(f32) + grad_resid_norm).astype(bf16))
    grad_att = jnp.sum(grad_att.astype(f32), axis=0)
    gains = group_sum(grad_att[64:70].reshape(-1))
    grad_att = swap(grad_att[:64])
    grad_ffn = swap(grad_ffn.astype(bf16)).astype(f32)
    both = nq + nk
    q_gains = gains[2 * width :]
    return (
        output,
        input_grad,
        grad_att[:, :nq],
        grad_att[:, nq:both],
        grad_att[:, both : both + nk],
        grad_att[:, both + nk :].T,
        grad_ffn[:, :hidden],
        grad_ffn[:, hidden : 2 * hidden],
        grad_ffn[:, 2 * hidden :].T,
        gains[:width],
        gains[width : 2 * width],
        q_gains[:head_size] + q_gains[head_size : 2 * head_size],
        q_gains[2 * head_size : 3 * head_size],
    )


def solution(mesh):
    inner = Mesh(mesh.devices.reshape(4, 2, 2, 4, 2), axes)
    dp, mp = ("y", "xh", "core"), ("z", "xl")
    rows = P(None, dp + mp, None)
    weight_in = [P(dp, mp)] * 3 + [P(mp, dp)] + [P(dp, mp)] * 2 + [P(mp, dp)]
    return jax.shard_map(
        local,
        mesh=inner,
        in_specs=tuple([rows, P(None, dp), rows] + weight_in + [P()] * 4),
        out_specs=tuple([rows, rows] + weight_in + [P()] * 4),
        check_vma=False,
    )
```

```python
import jax
import jax.numpy as jnp
from jax import lax
from jax.experimental import pallas as pl
from jax.experimental.pallas import tpu as pltpu
from jax.sharding import Mesh, PartitionSpec as P

eps = 1e-05
rope_base = 1000000.0
axes = ("y", "xh", "core", "z", "xl")
plane = ("y", "xh", "xl")
CORE = [(0, 1), (1, 0)]
bf16 = jnp.bfloat16
f32 = jnp.float32
VMEM = 60 * 2**20


def product(left, right):
    return jnp.dot(left, right, preferred_element_type=jnp.float32)


def product_nt(left, right):
    return lax.dot_general(
        left, right, (((1,), (1,)), ((), ())), preferred_element_type=jnp.float32
    )


def product_tn(left, right):
    return lax.dot_general(
        left, right, (((0,), (0,)), ((), ())), preferred_element_type=jnp.float32
    )


def rms_scale(value):
    return lax.rsqrt(jnp.mean(value * value, axis=-1, keepdims=True) + eps)


def rms_rows(value, gain):
    return value * rms_scale(value) * gain


def swap(value):
    return lax.ppermute(
        value, ("core", "xl"), [(a * 2 + b, b * 2 + a) for a in range(2) for b in range(2)]
    )


def from_z(value, k):
    return lax.ppermute(value, "z", [(z, (z - k) % 4) for z in range(4)])


def swap_from_x(value, k):
    perm = []
    for xh in range(2):
        for a in range(2):
            for b in range(2):
                x = (xh * 2 + a - k) % 4
                perm.append((xh * 4 + a * 2 + b, (x // 2) * 4 + b * 2 + x % 2))
    return lax.ppermute(value, ("xh", "core", "xl"), perm)


def from_y(value, k):
    return lax.ppermute(value, "y", [(y, (y - k) % 4) for y in range(4)])


def other_core(value):
    return lax.ppermute(value, "core", CORE)


def from_chain(value):
    return [value] + [from_z(value, k) for k in (1, 2, 3)]


def gather_chains(pieces):
    chain = jnp.stack(pieces)
    return chain, other_core(chain)


def gather(value):
    chain = tie(*from_chain(value))
    return chain + [other_core(v) for v in chain]


def ordered(value, z, core, axis):
    shape = value.shape
    block = shape[axis] // 8
    v = value.reshape(shape[:axis] + (4, 2, block) + shape[axis + 1 :])
    v = lax.dynamic_slice_in_dim(jnp.concatenate([v, v], axis), z, 4, axis)
    v = lax.dynamic_slice_in_dim(jnp.concatenate([v, v], axis + 1), core, 2, axis + 1)
    return jnp.swapaxes(v, axis, axis + 1).reshape(shape)


def group_sum(value):
    value = value + other_core(value)
    return value + sum(from_z(value, k) for k in (1, 2, 3))


def tie(*values):
    return list(lax.optimization_barrier(values))


def halves(value):
    lane = lax.broadcasted_iota(jnp.int32, value.shape, value.ndim - 1)
    return lane < 64


def quarter(value):
    lane = lax.broadcasted_iota(jnp.int32, value.shape, value.ndim - 1)
    return (lane & 32) == 0


def turn(value):
    return jnp.where(quarter(value), -pltpu.roll(value, 96, 1), pltpu.roll(value, 32, 1))


def turn_back(value):
    return jnp.where(quarter(value), pltpu.roll(value, 96, 1), -pltpu.roll(value, 32, 1))


def head_mean(value):
    low = halves(value)
    first = jnp.sum(jnp.where(low, value, 0.0), axis=-1, keepdims=True)
    second = jnp.sum(jnp.where(low, 0.0, value), axis=-1, keepdims=True)
    return jnp.where(low, first, second) * (1.0 / 64)


def attend_kernel(at_ref, *refs):
    x_refs, w_refs = refs[:2], refs[2:6]
    gain_ref, qk_gain_ref, cos_ref, sin_ref, bias_ref = refs[6:11]
    mixed_ref, x_ref, normed_ref, w_ref, raw_ref, q_ref, kk_ref, vv_ref, stat_ref = refs[11:]

    @pl.when(pl.program_id(0) == 0)
    def _():
        for ky in range(4):
            for kx in range(4):
                row = lax.rem(at_ref[0] + ky, 4) * 256 + lax.rem(at_ref[1] + kx, 4) * 64
                row = pl.multiple_of(row, 64)
                w_ref[pl.ds(row, 64), :] = w_refs[ky][kx * 64 : kx * 64 + 64, :]

    for i in range(8):
        block = x_refs[i // 4][i % 4, 0]
        x_ref[i * 64 : i * 64 + 64, :] = block
        block = block.astype(f32)
        normed_ref[i * 64 : i * 64 + 64, :] = (
            block * rms_scale(block) * gain_ref[0:1, :]
        ).astype(bf16)
    raw = product(normed_ref[...], w_ref[:, :256])
    raw_ref[...] = raw
    cosine, sine = cos_ref[0], sin_ref[0]
    query, kv = raw[:, :128], raw[:, 128:]
    low = halves(kv)
    query = query * lax.rsqrt(head_mean(query * query) + eps) * qk_gain_ref[0:1, :]
    q_ref[...] = (query * cosine + turn(query) * sine).astype(bf16)
    key = kv * lax.rsqrt(head_mean(kv * kv) + eps) * qk_gain_ref[1:2, :]
    key = key * cosine + turn(key) * sine
    kk_ref[...] = jnp.where(low, key, pltpu.roll(key, 64, 1)).astype(bf16)
    vv_ref[...] = jnp.where(low, pltpu.roll(kv, 64, 1), kv).astype(bf16)
    keys, values = kk_ref[...], vv_ref[...]
    for rows in (slice(0, 256), slice(256, 512)):
        queries = q_ref[rows, :]
        low = halves(queries)
        bias = bias_ref[0, rows, :].astype(f32)
        parts = []
        for head in range(2):
            one = jnp.where(low == (head == 0), queries, jnp.zeros_like(queries))
            scores = product_nt(one, keys) * 0.125 + bias
            top = jnp.max(scores, axis=-1, keepdims=True)
            expo = jnp.exp(scores - top)
            total = jnp.sum(expo, axis=-1, keepdims=True)
            weights = (expo * (1.0 / total)).astype(bf16)
            parts.append((product(weights, values), top + jnp.log(total)))
        first = halves(parts[0][0])
        mixed_ref[rows, :] = jnp.where(first, parts[0][0], parts[1][0]).astype(bf16)
        stat_ref[rows, :] = jnp.where(first, parts[0][1], parts[1][1])


def attend(at, pieces, weights, gain, qk_gain, cosine, sine, bias):
    width = pieces[0].shape[3]
    micro = pieces[0].shape[1]
    group = 512
    chain = pl.BlockSpec((4, 1, 64, width), lambda m, at: (0, m, 0, 0))
    whole = lambda a: pl.BlockSpec(a.shape, lambda m, at: (0,) * a.ndim)
    part = lambda a: pl.BlockSpec((1,) + a.shape[1:], lambda m, at: (m, 0, 0))
    rows = lambda cols: pl.BlockSpec((group, cols), lambda m, at: (m, 0))
    out = lambda cols, kind: jax.ShapeDtypeStruct((micro * group, cols), kind)
    return pl.pallas_call(
        attend_kernel,
        grid_spec=pltpu.PrefetchScalarGridSpec(
            num_scalar_prefetch=1,
            grid=(micro,),
            in_specs=[chain, chain]
            + [whole(w) for w in weights]
            + [whole(gain), whole(qk_gain), part(cosine), part(sine), part(bias)],
            out_specs=[
                rows(128),
                rows(width),
                rows(width),
                pl.BlockSpec((width, 384), lambda m, at: (0, 0)),
                rows(256),
                rows(128),
                rows(128),
                rows(128),
                rows(128),
            ],
        ),
        out_shape=[
            out(128, bf16),
            out(width, bf16),
            out(width, bf16),
            jax.ShapeDtypeStruct((width, 384), bf16),
            out(256, f32),
            out(128, bf16),
            out(128, bf16),
            out(128, bf16),
            out(128, f32),
        ],
        compiler_params=pltpu.CompilerParams(vmem_limit_bytes=VMEM),
        cost_estimate=pl.CostEstimate(flops=12 * 10**9, bytes_accessed=10**7, transcendentals=10**6),
        name="attend",
    )(at, *pieces, *weights, gain, qk_gain, cosine, sine, bias)


def state_kernel(at_ref, *refs):
    mixed_refs, w_refs = refs[:8], refs[8:10]
    x_ref, gain_ref, state_ref, second_ref, w_out, mixed = refs[10:]
    step = pl.program_id(0)
    micro, side = step // 2, lax.rem(step, 2)

    @pl.when(step == 0)
    def _():
        for i in range(8):
            for ky in range(4):
                for kx in range(4):
                    row = lax.rem(at_ref[0] + ky, 4) * 256 + lax.rem(at_ref[1] + kx, 4) * 64
                    row = pl.multiple_of(row, 64)
                    w_out[pl.ds(row, 64), i * 128 : i * 128 + 128] = w_refs[i // 4][
                        i % 4, ky * 256 + kx * 64 : ky * 256 + kx * 64 + 64, :
                    ]

    for i, ref in enumerate(mixed_refs):
        flip, k = i // 4, i % 4
        base = micro * 512 + lax.rem(side + flip, 2) * 256
        for j in range(4):
            row = pl.multiple_of(base + (j - k) % 4 * 64, 64)
            mixed[j * 64 : j * 64 + 64, i * 128 : i * 128 + 128] = ref[pl.ds(row, 64), :]
    state = x_ref[...].astype(f32) + product_nt(mixed[...], w_out[...])
    state_ref[...] = state[:64]
    second_ref[...] = (state * rms_scale(state) * gain_ref[0:1, :]).astype(bf16)


def second_norm(at, mixed, w_out, x, gain):
    count, width = x.shape
    steps = count // 256
    whole = lambda a: pl.BlockSpec(a.shape, lambda b, at: (0,) * a.ndim)
    rows = lambda block: pl.BlockSpec((block, width), lambda b, at: (b, 0))
    return pl.pallas_call(
        state_kernel,
        grid_spec=pltpu.PrefetchScalarGridSpec(
            num_scalar_prefetch=1,
            grid=(steps,),
            in_specs=[whole(p) for p in mixed]
            + [whole(w) for w in w_out]
            + [rows(256), whole(gain)],
            out_specs=[rows(64), rows(256)],
            scratch_shapes=[pltpu.VMEM((width, 1024), bf16), pltpu.VMEM((256, 1024), bf16)],
        ),
        out_shape=[
            jax.ShapeDtypeStruct((steps * 64, width), f32),
            jax.ShapeDtypeStruct((count, width), bf16),
        ],
        compiler_params=pltpu.CompilerParams(vmem_limit_bytes=VMEM),
        cost_estimate=pl.CostEstimate(flops=3 * 10**9, bytes_accessed=10**7, transcendentals=0),
        name="second_norm",
    )(at, *mixed, *w_out, x, gain)


def feed_kernel(second_ref, wf_ref, *refs):
    up_refs = refs[:2]
    inner_ref, low_ref, own_ref, other_ref = refs[2:6]
    up_ref, down_own_ref, down_other_ref, w_gu = refs[6:]
    step = pl.program_id(0)
    side = lax.rem(step, 2)

    @pl.when(step == 0)
    def _():
        for rows in (slice(i, i + 128) for i in range(0, w_gu.shape[0], 128)):
            w_gu[rows, :512] = wf_ref[rows, :512]
            rest = wf_ref[rows, 512:1152].astype(f32)
            w_gu[rows, 512:] = pltpu.roll(rest, 576, 1).astype(bf16)

    for i, ref in enumerate(up_refs):

        @pl.when(side == i)
        def _():
            for j in range(4):
                up_ref[j * 64 : j * 64 + 64, :] = ref[j, 0]

    both = product(second_ref[...], w_gu[...])
    grad_inner = product(up_ref[...], wf_ref[:, 1152:1728])

    def glu(gate, up, grad):
        sig = 1.0 / (1.0 + jnp.exp(-gate))
        silu = gate * sig
        inner = (silu * up).astype(bf16)
        grad_gate = (grad * up * sig * (1.0 + gate * (1.0 - sig))).astype(bf16)
        return inner, grad_gate, (grad * silu).astype(bf16)

    inner, grad_gate, grad_up = glu(both[:, :512], both[:, 512:1024], grad_inner[:, :512])
    inner_ref[:, :512] = inner
    low_ref[:, :512] = grad_gate
    low_ref[:, 512:1024] = grad_up
    tail = both[:, 1024:]
    gate_tail = pltpu.roll(tail, 64, 1)
    inner, grad_gate, grad_up = glu(gate_tail[:, :64], tail[:, :64], grad_inner[:, 512:])
    inner_ref[:, 512:] = inner
    low_ref[:, 1024:1088] = grad_up
    low_ref[:, 1088:] = grad_gate
    grad = product_nt(low_ref[...], w_gu[...]).astype(bf16)
    down = product_nt(inner_ref[...], wf_ref[:, 1152:]).astype(bf16)

    @pl.when(side == 0)
    def _():
        own_ref[0] = grad
        down_own_ref[0] = down

    @pl.when(side == 1)
    def _():
        other_ref[0] = grad
        down_other_ref[0] = down


def feed(second, w_ffn, cotangent):
    count, width = second.shape
    steps = count // 256
    whole = lambda a: pl.BlockSpec(a.shape, lambda b: (0,) * a.ndim)
    rows = lambda cols: pl.BlockSpec((256, cols), lambda b: (b, 0))
    half = pl.BlockSpec((1, 256, width), lambda b: (b // 2, 0, 0))
    chain = pl.BlockSpec((4, 1, 64, width), lambda b: (0, b // 2, 0, 0))
    out = lambda *shape: jax.ShapeDtypeStruct(shape, bf16)
    halves_out = out(steps // 2, 256, width)
    return pl.pallas_call(
        feed_kernel,
        grid=(steps,),
        in_specs=[rows(width), whole(w_ffn), chain, chain],
        out_specs=[rows(576), rows(1152), half, half, rows(width), half, half],
        scratch_shapes=[pltpu.VMEM((width, 1152), bf16)],
        out_shape=[
            *(out(count, 576), out(count, 1152), halves_out, halves_out),
            *(out(count, width), halves_out, halves_out),
        ],
        compiler_params=pltpu.CompilerParams(vmem_limit_bytes=VMEM),
        cost_estimate=pl.CostEstimate(flops=9 * 10**9, bytes_accessed=10**7, transcendentals=10**6),
        name="feed",
    )(second, w_ffn, *cotangent)


def weights_kernel(second_ref, up_ref, low_ref, inner_ref, grad_ref):
    grad = product_tn(second_ref[...], low_ref[...])
    grad_ref[:, :512] = grad[:, :512].astype(bf16)
    grad_ref[:, 512:1152] = pltpu.roll(grad[:, 512:], 64, 1).astype(bf16)
    grad_ref[:, 1152:] = product_tn(up_ref[...], inner_ref[...]).astype(bf16)


def weights_back(second, upstream, low, inner):
    count, width = second.shape
    whole = lambda a: pl.BlockSpec(a.shape, lambda b: (0,) * a.ndim)
    columns = pl.BlockSpec((count, 256), lambda b: (0, b))
    return pl.pallas_call(
        weights_kernel,
        grid=(width // 256,),
        in_specs=[columns, columns, whole(low), whole(inner)],
        out_specs=pl.BlockSpec((256, 1728), lambda b: (b, 0)),
        out_shape=jax.ShapeDtypeStruct((width, 1728), bf16),
        compiler_params=pltpu.CompilerParams(vmem_limit_bytes=VMEM),
        cost_estimate=pl.CostEstimate(flops=4 * 10**9, bytes_accessed=10**7, transcendentals=0),
        name="weights_back",
    )(second, upstream, low, inner)


def back_kernel(*refs):
    state_refs = refs[:8]
    normed_ref, w_ref, raw_ref, q_ref, kk_ref, vv_ref, stat_ref, mixed_ref = refs[8:16]
    qk_gain_ref, cos_ref, sin_ref, bias_ref, gain_ref, ffn_ref = refs[16:22]
    own_ref, other_ref, grad_ref = refs[22:25]
    state, low_ref, total, norm_ref, qk_grad_ref = refs[25:]
    step = pl.program_id(0)
    for i, ref in enumerate(state_refs):
        state[i * 64 : i * 64 + 64, :] = ref[0]
    grad_mixed = product(state[...], w_ref[:, 256:]).astype(bf16)
    keys, values = kk_ref[...], vv_ref[...]
    grad_key = jnp.zeros((512, 128), f32)
    grad_value = jnp.zeros((512, 128), f32)
    grad_query = []
    for rows in (slice(0, 256), slice(256, 512)):
        queries, grads = q_ref[rows, :], grad_mixed[rows, :]
        low = halves(queries)
        bias = bias_ref[0, rows, :].astype(f32)
        parts = []
        for head in range(2):
            keep = low == (head == 0)
            one = jnp.where(keep, queries, jnp.zeros_like(queries))
            grad_one = jnp.where(keep, grads, jnp.zeros_like(grads))
            scores = product_nt(one, keys) * 0.125 + bias
            soft = jnp.exp(scores - stat_ref[rows, head * 64 : head * 64 + 1])
            grad_weights = product_nt(grad_one, values)
            center = jnp.sum(soft * grad_weights, axis=-1, keepdims=True)
            grad_scores = (soft * (grad_weights - center)).astype(bf16)
            parts.append(product(grad_scores, keys))
            grad_key = grad_key + product_tn(grad_scores, one)
            grad_value = grad_value + product_tn(soft.astype(bf16), grad_one)
        grad_query.append(jnp.where(halves(parts[0]), parts[0], parts[1]))
    cosine, sine = cos_ref[0], sin_ref[0]

    def prepare_back(grad, raw, gain):
        grad = grad * cosine + turn_back(grad * sine)
        scale = lax.rsqrt(head_mean(raw * raw) + eps)
        unit = raw * scale
        grad_gain = jnp.sum(grad * unit, axis=0, keepdims=True)
        scaled = grad * gain
        return scale * (scaled - unit * head_mean(scaled * unit)), grad_gain

    raw = raw_ref[...]
    grad_q = jnp.concatenate(grad_query, axis=0) * 0.125
    grad_q, gain_q = prepare_back(grad_q, raw[:, :128], qk_gain_ref[0:1, :])
    grad_key = (grad_key + pltpu.roll(grad_key, 64, 1)) * 0.125
    grad_value = grad_value + pltpu.roll(grad_value, 64, 1)
    low = halves(grad_value)
    raw_k = jnp.where(low, raw[:, 128:], 0.0)
    grad_k, gain_k = prepare_back(jnp.where(low, grad_key, 0.0), raw_k, qk_gain_ref[1:2, :])
    low_ref[:, :128] = grad_q.astype(bf16)
    low_ref[:, 128:] = jnp.where(low, grad_k, grad_value).astype(bf16)

    @pl.when(step == 0)
    def _():
        total[...] = jnp.zeros_like(total)
        norm_ref[...] = jnp.zeros_like(norm_ref)
        qk_grad_ref[...] = jnp.zeros_like(qk_grad_ref)

    qk_grad_ref[0:1, :] += gain_q
    qk_grad_ref[1:2, :] += gain_k
    for rows, ref in ((slice(0, 256), own_ref), (slice(256, 512), other_ref)):
        grad = product_nt(low_ref[rows, :], w_ref[:, :256])
        ref[0] = grad.astype(bf16)
        norm_ref[0:1, :] += jnp.sum(grad * normed_ref[rows, :].astype(f32), axis=0, keepdims=True)
    total[:, :256] += product_tn(normed_ref[...], low_ref[...])
    total[:, 256:] += product_tn(state[...], mixed_ref[...])

    @pl.when(step == pl.num_programs(0) - 1)
    def _():
        norm = norm_ref[0:1, :] / gain_ref[0:1, :]
        chunks = [norm[:, i : i + 128] for i in range(0, 1024, 128)]
        chunks += [ffn_ref[0:1, i : i + 128] for i in range(0, 1024, 128)]
        chunks += [qk_grad_ref[0:1, :], qk_grad_ref[1:2, :]]
        lines = [jnp.concatenate(chunks[i : i + 3], axis=1) for i in range(0, 18, 3)]
        lines = jnp.concatenate(lines + [jnp.zeros((10, 384), f32)], axis=0).astype(bf16)
        for i in range(16):
            grad_ref[i, :64, :] = total[i * 64 : i * 64 + 64, :].astype(bf16)
            grad_ref[i, 64:, :] = lines


def back(
    state, normed, w_att, raw, query, keys, values, stat, mixed, qk_gain, cosine, sine, bias, gain, ffn
):
    width = state[0].shape[2]
    micro = state[0].shape[0]
    whole = lambda a: pl.BlockSpec(a.shape, lambda m: (0,) * a.ndim)
    part = lambda a: pl.BlockSpec((1,) + a.shape[1:], lambda m: (m, 0, 0))
    rows = lambda a: pl.BlockSpec((512, a.shape[1]), lambda m: (m, 0))
    half = pl.BlockSpec((1, 256, width), lambda m: (m, 0, 0))
    out = jax.ShapeDtypeStruct
    return pl.pallas_call(
        back_kernel,
        grid=(micro,),
        in_specs=[part(p) for p in state]
        + [rows(normed), whole(w_att), rows(raw), rows(query), rows(keys), rows(values)]
        + [rows(stat), rows(mixed), whole(qk_gain), part(cosine), part(sine), part(bias)]
        + [whole(gain), whole(ffn)],
        out_specs=[half, half, pl.BlockSpec((16, 80, 384), lambda m: (0, 0, 0))],
        scratch_shapes=[
            pltpu.VMEM((512, width), bf16),
            pltpu.VMEM((512, 256), bf16),
            pltpu.VMEM((width, 384), f32),
            pltpu.VMEM((8, width), f32),
            pltpu.VMEM((8, 128), f32),
        ],
        out_shape=[
            out((micro, 256, width), bf16),
            out((micro, 256, width), bf16),
            out((16, 80, 384), bf16),
        ],
        compiler_params=pltpu.CompilerParams(vmem_limit_bytes=VMEM),
        cost_estimate=pl.CostEstimate(flops=15 * 10**9, bytes_accessed=10**7, transcendentals=10**6),
        name="back",
    )(
        *(*state, normed, w_att, raw, query, keys, values, stat, mixed),
        *(qk_gain, cosine, sine, bias, gain, ffn),
    )


def split_kernel(*refs):
    count = len(refs) // 2 - 2
    for i in range(count):
        own_ref, got_ref = refs[2 * i], refs[2 * i + 1]
        micro = own_ref.shape[0]
        for k, ref in enumerate(refs[-4:]):
            rows = slice(k * 64, k * 64 + 64)
            value = own_ref[:, rows].astype(f32) + got_ref[:, rows].astype(f32)
            ref[i * micro : (i + 1) * micro] = value.astype(ref.dtype)


def split(own, other, *more):
    micro, _, width = own.shape
    values = (own, other_core(other)) + more
    out = lambda kind: jax.ShapeDtypeStruct((len(values) // 2 * micro, 64, width), kind)
    return pl.pallas_call(
        split_kernel,
        out_shape=[out(f32), out(bf16), out(bf16), out(bf16)],
        compiler_params=pltpu.CompilerParams(vmem_limit_bytes=VMEM),
        name="split",
    )(*values)


def local(
    tokens,
    segment_ids,
    cotangent,
    w_query,
    w_key,
    w_value,
    w_out,
    w_gate,
    w_up,
    w_down,
    norm_gain,
    ffn_gain,
    query_gain,
    key_gain,
):
    micro, own, width = tokens.shape
    head_size = query_gain.shape[0]
    nq = w_query.shape[1]
    nk = w_key.shape[1]
    group = segment_ids.shape[1]
    hidden = w_gate.shape[1]
    z = lax.axis_index("z")
    core = lax.axis_index("core")
    at = jnp.stack([lax.axis_index("y"), lax.axis_index("xh") * 2 + lax.axis_index("xl"), z, core])
    at = at.astype(jnp.int32)

    segment = swap(segment_ids)
    x_own = swap(tokens)
    w_att = jnp.concatenate([w_query, w_key, w_value, w_out.T], axis=1)
    w_att = jnp.concatenate([swap_from_x(w_att, k) for k in range(4)], axis=0)
    w_att, x_own, segment = tie(w_att, x_own, segment)
    x_pieces = from_chain(x_own)
    w_att = [w_att] + [from_y(w_att, k) for k in (1, 2, 3)]
    w_ffn = swap(jnp.concatenate([w_gate, w_up, w_down.T], axis=1))
    cotangent_own = swap(cotangent)

    index = jnp.arange(group, dtype=jnp.int32)
    change = jnp.concatenate(
        [jnp.ones((micro, 1), dtype=bool), segment[:, 1:] != segment[:, :-1]], axis=1
    )
    start = lax.cummax(jnp.where(change, index, 0), axis=1)
    start = ordered(start, z, core, 1)
    index = ordered(index[None], z, core, 1)
    place = (index - start).astype(f32)
    freq = rope_base ** (-(jnp.arange(head_size // 2, dtype=f32) * 2.0 / head_size))
    angle = place[:, :, None] * jnp.tile(freq, 4)
    cosine, sine = jnp.cos(angle), jnp.sin(angle)
    allowed = (start[:, :, None] == start[:, None, :]) & (index[:, :, None] >= index[:, None, :])
    bias = jnp.where(allowed, 0.0, -1e30).astype(bf16)
    qk_gain = jnp.stack([jnp.tile(query_gain, 2), jnp.tile(key_gain, 2)])

    w_ffn, *pieces = tie(w_ffn, *w_att, *x_pieces, cosine, sine, bias, qk_gain, at)
    w_att, x_pieces = pieces[:4], pieces[4:8]
    cosine, sine, bias, qk_gain, at = pieces[8:]
    w_ffn = lax.all_gather(w_ffn, plane, axis=0, tiled=True)
    w_out_chain = from_chain(jnp.concatenate([w[:, nq + 2 * nk :] for w in w_att], axis=0))
    x_chain, x_other = gather_chains(x_pieces)

    mixed, x, normed, w_abs, raw, query, keys, values, stat = attend(
        at, (x_chain, x_other), w_att, norm_gain.reshape(1, width), qk_gain, cosine, sine, bias
    )
    mixed, *chains = tie(mixed, *w_out_chain, *from_chain(cotangent_own))
    w_out_all = gather_chains(chains[:4])
    cotangent_all = gather_chains(chains[4:])
    state, second = second_norm(at, gather(mixed), w_out_all, x, ffn_gain.reshape(1, width))
    inner, gu_low, grad_own, grad_other, upstream, down_own, down_other = feed(
        second, w_ffn, cotangent_all
    )
    down_got = other_core(down_other)
    parts = split(grad_own, grad_other)
    got = [from_z(parts[k], -k) for k in (1, 2, 3)]
    grad_ffn = weights_back(second, upstream, gu_low, inner)
    grad_ffn, *got = tie(grad_ffn, *got)
    grad_ffn = lax.all_to_all(grad_ffn.reshape(16, width // 16, -1), plane, 0, 0)
    grad_second = parts[0] + sum(piece.astype(f32) for piece in got)
    state_own = state.reshape(micro, 2, own, width)[:, 0]
    _, norm_pull = jax.vjp(rms_rows, state_own, ffn_gain)
    grad_state_norm, grad_ffn_gain = norm_pull(grad_second)
    grad_state = (cotangent_own.astype(f32) + grad_state_norm).astype(bf16)
    state_pieces = gather(grad_state)

    grad_own, grad_other, grad_att = back(
        *(state_pieces, normed, w_abs, raw, query, keys, values, stat, mixed, qk_gain),
        *(cosine, sine, bias, norm_gain.reshape(1, width), grad_ffn_gain.reshape(1, width)),
    )
    grad_att = lax.all_to_all(grad_att, plane, 0, 0)
    parts = split(grad_own, grad_other, down_own, down_got)
    got = [from_z(parts[k], -k) for k in (1, 2, 3)]
    grad_att, grad_ffn, *got = tie(grad_att, grad_ffn, *got)
    total = parts[0] + sum(piece.astype(f32) for piece in got)
    _, first_pull = jax.vjp(rms_rows, x_own.astype(f32), norm_gain)
    grad_resid_norm, _ = first_pull(total[:micro])
    input_grad = grad_state.astype(f32) + grad_resid_norm
    results = swap(jnp.concatenate([state_own + total[micro:], input_grad]).astype(bf16))
    grad_ffn = jnp.sum(grad_ffn.astype(f32), axis=0)
    grad_att = jnp.sum(grad_att.astype(f32), axis=0)
    gains = group_sum(grad_att[64:70].reshape(-1))
    grad_att = swap(grad_att[:64])
    grad_ffn = swap(grad_ffn.astype(bf16)).astype(f32)
    both = nq + nk
    q_gains = gains[2 * width :]
    return (
        results[:micro],
        results[micro:],
        grad_att[:, :nq],
        grad_att[:, nq:both],
        grad_att[:, both : both + nk],
        grad_att[:, both + nk :].T,
        grad_ffn[:, :hidden],
        grad_ffn[:, hidden : 2 * hidden],
        grad_ffn[:, 2 * hidden :].T,
        gains[:width],
        gains[width : 2 * width],
        q_gains[:head_size] + q_gains[head_size : 2 * head_size],
        q_gains[2 * head_size : 3 * head_size],
    )


def solution(mesh):
    inner = Mesh(mesh.devices.reshape(4, 2, 2, 4, 2), axes)
    dp, mp = ("y", "xh", "core"), ("z", "xl")
    rows = P(None, dp + mp, None)
    weight_in = [P(dp, mp)] * 3 + [P(mp, dp)] + [P(dp, mp)] * 2 + [P(mp, dp)]
    return jax.shard_map(
        local,
        mesh=inner,
        in_specs=tuple([rows, P(None, dp), rows] + weight_in + [P()] * 4),
        out_specs=tuple([rows, rows] + weight_in + [P()] * 4),
        check_vma=False,
    )
```

```python
import jax
import jax.numpy as jnp
from jax import lax
from jax.experimental import pallas as pl
from jax.experimental.pallas import tpu as pltpu
from jax.sharding import Mesh, PartitionSpec as P

eps = 1e-05
rope_base = 1000000.0
axes = ("y", "xh", "core", "z", "xl")
plane = ("y", "xh", "xl")
CORE = [(0, 1), (1, 0)]
bf16 = jnp.bfloat16
f32 = jnp.float32
VMEM = 60 * 2**20


def product(left, right):
    return jnp.dot(left, right, preferred_element_type=jnp.float32)


def product_nt(left, right):
    return lax.dot_general(
        left, right, (((1,), (1,)), ((), ())), preferred_element_type=jnp.float32
    )


def product_tn(left, right):
    return lax.dot_general(
        left, right, (((0,), (0,)), ((), ())), preferred_element_type=jnp.float32
    )


def rms_scale(value):
    return lax.rsqrt(jnp.mean(value * value, axis=-1, keepdims=True) + eps)


def rms_rows(value, gain):
    return value * rms_scale(value) * gain


def swap(value):
    return lax.ppermute(
        value, ("core", "xl"), [(a * 2 + b, b * 2 + a) for a in range(2) for b in range(2)]
    )


def from_z(value, k):
    return lax.ppermute(value, "z", [(z, (z - k) % 4) for z in range(4)])


def swap_from_x(value, k):
    perm = []
    for xh in range(2):
        for a in range(2):
            for b in range(2):
                x = (xh * 2 + a - k) % 4
                perm.append((xh * 4 + a * 2 + b, (x // 2) * 4 + b * 2 + x % 2))
    return lax.ppermute(value, ("xh", "core", "xl"), perm)


def from_y(value, k):
    return lax.ppermute(value, "y", [(y, (y - k) % 4) for y in range(4)])


def other_core(value):
    return lax.ppermute(value, "core", CORE)


def from_chain(value):
    return [value] + [from_z(value, k) for k in (1, 2, 3)]


def gather_chains(pieces):
    chain = jnp.stack(pieces)
    return chain, other_core(chain)


def gather(value):
    chain = tie(*from_chain(value))
    return chain + [other_core(v) for v in chain]


def ordered(value, z, core, axis):
    shape = value.shape
    block = shape[axis] // 8
    v = value.reshape(shape[:axis] + (4, 2, block) + shape[axis + 1 :])
    v = lax.dynamic_slice_in_dim(jnp.concatenate([v, v], axis), z, 4, axis)
    v = lax.dynamic_slice_in_dim(jnp.concatenate([v, v], axis + 1), core, 2, axis + 1)
    return jnp.swapaxes(v, axis, axis + 1).reshape(shape)


def group_sum(value):
    value = value + other_core(value)
    return value + sum(from_z(value, k) for k in (1, 2, 3))


def tie(*values):
    return list(lax.optimization_barrier(values))


def halves(value):
    lane = lax.broadcasted_iota(jnp.int32, value.shape, value.ndim - 1)
    return lane < 64


def quarter(value):
    lane = lax.broadcasted_iota(jnp.int32, value.shape, value.ndim - 1)
    return (lane & 32) == 0


def turn(value):
    return jnp.where(quarter(value), -pltpu.roll(value, 96, 1), pltpu.roll(value, 32, 1))


def turn_back(value):
    return jnp.where(quarter(value), pltpu.roll(value, 96, 1), -pltpu.roll(value, 32, 1))


def head_mean(value):
    low = halves(value)
    first = jnp.sum(jnp.where(low, value, 0.0), axis=-1, keepdims=True)
    second = jnp.sum(jnp.where(low, 0.0, value), axis=-1, keepdims=True)
    return jnp.where(low, first, second) * (1.0 / 64)


def attend_kernel(at_ref, *refs):
    x_refs, w_refs = refs[:2], refs[2:6]
    gain_ref, qk_gain_ref, cos_ref, sin_ref, bias_ref = refs[6:11]
    mixed_ref, x_ref, normed_ref, w_ref, raw_ref, q_ref, kk_ref, vv_ref, stat_ref = refs[11:]

    @pl.when(pl.program_id(0) == 0)
    def _():
        for ky in range(4):
            for kx in range(4):
                row = lax.rem(at_ref[0] + ky, 4) * 256 + lax.rem(at_ref[1] + kx, 4) * 64
                row = pl.multiple_of(row, 64)
                w_ref[pl.ds(row, 64), :] = w_refs[ky][kx * 64 : kx * 64 + 64, :]

    for i in range(8):
        block = x_refs[i // 4][i % 4, 0]
        x_ref[i * 64 : i * 64 + 64, :] = block
        block = block.astype(f32)
        normed_ref[i * 64 : i * 64 + 64, :] = (
            block * rms_scale(block) * gain_ref[0:1, :]
        ).astype(bf16)
    raw = product(normed_ref[...], w_ref[:, :256])
    raw_ref[...] = raw
    cosine, sine = cos_ref[0], sin_ref[0]
    query, kv = raw[:, :128], raw[:, 128:]
    low = halves(kv)
    query = query * lax.rsqrt(head_mean(query * query) + eps) * qk_gain_ref[0:1, :]
    q_ref[...] = (query * cosine + turn(query) * sine).astype(bf16)
    key = kv * lax.rsqrt(head_mean(kv * kv) + eps) * qk_gain_ref[1:2, :]
    key = key * cosine + turn(key) * sine
    kk_ref[...] = jnp.where(low, key, pltpu.roll(key, 64, 1)).astype(bf16)
    vv_ref[...] = jnp.where(low, pltpu.roll(kv, 64, 1), kv).astype(bf16)
    keys, values = kk_ref[...], vv_ref[...]
    for rows in (slice(0, 256), slice(256, 512)):
        queries = q_ref[rows, :]
        low = halves(queries)
        bias = bias_ref[0, rows, :].astype(f32)
        parts = []
        for head in range(2):
            one = jnp.where(low == (head == 0), queries, jnp.zeros_like(queries))
            scores = product_nt(one, keys) * 0.125 + bias
            top = jnp.max(scores, axis=-1, keepdims=True)
            expo = jnp.exp(scores - top)
            total = jnp.sum(expo, axis=-1, keepdims=True)
            weights = (expo * (1.0 / total)).astype(bf16)
            parts.append((product(weights, values), top + jnp.log(total)))
        first = halves(parts[0][0])
        mixed_ref[rows, :] = jnp.where(first, parts[0][0], parts[1][0]).astype(bf16)
        stat_ref[rows, :] = jnp.where(first, parts[0][1], parts[1][1])


def attend(at, pieces, weights, gain, qk_gain, cosine, sine, bias):
    width = pieces[0].shape[3]
    micro = pieces[0].shape[1]
    group = 512
    chain = pl.BlockSpec((4, 1, 64, width), lambda m, at: (0, m, 0, 0))
    whole = lambda a: pl.BlockSpec(a.shape, lambda m, at: (0,) * a.ndim)
    part = lambda a: pl.BlockSpec((1,) + a.shape[1:], lambda m, at: (m, 0, 0))
    rows = lambda cols: pl.BlockSpec((group, cols), lambda m, at: (m, 0))
    out = lambda cols, kind: jax.ShapeDtypeStruct((micro * group, cols), kind)
    return pl.pallas_call(
        attend_kernel,
        grid_spec=pltpu.PrefetchScalarGridSpec(
            num_scalar_prefetch=1,
            grid=(micro,),
            in_specs=[chain, chain]
            + [whole(w) for w in weights]
            + [whole(gain), whole(qk_gain), part(cosine), part(sine), part(bias)],
            out_specs=[
                rows(128),
                rows(width),
                rows(width),
                pl.BlockSpec((width, 384), lambda m, at: (0, 0)),
                rows(256),
                rows(128),
                rows(128),
                rows(128),
                rows(128),
            ],
        ),
        out_shape=[
            out(128, bf16),
            out(width, bf16),
            out(width, bf16),
            jax.ShapeDtypeStruct((width, 384), bf16),
            out(256, f32),
            out(128, bf16),
            out(128, bf16),
            out(128, bf16),
            out(128, f32),
        ],
        compiler_params=pltpu.CompilerParams(vmem_limit_bytes=VMEM),
        cost_estimate=pl.CostEstimate(flops=12 * 10**9, bytes_accessed=10**7, transcendentals=10**6),
        name="attend",
    )(at, *pieces, *weights, gain, qk_gain, cosine, sine, bias)


def state_kernel(at_ref, *refs):
    mixed_refs, w_refs = refs[:8], refs[8:10]
    x_ref, gain_ref, state_ref, second_ref, w_out, mixed = refs[10:]
    step = pl.program_id(0)
    micro, side = step // 2, lax.rem(step, 2)

    @pl.when(step == 0)
    def _():
        for i in range(8):
            for ky in range(4):
                for kx in range(4):
                    row = lax.rem(at_ref[0] + ky, 4) * 256 + lax.rem(at_ref[1] + kx, 4) * 64
                    row = pl.multiple_of(row, 64)
                    w_out[pl.ds(row, 64), i * 128 : i * 128 + 128] = w_refs[i // 4][
                        i % 4, ky * 256 + kx * 64 : ky * 256 + kx * 64 + 64, :
                    ]

    for i, ref in enumerate(mixed_refs):
        flip, k = i // 4, i % 4
        base = micro * 512 + lax.rem(side + flip, 2) * 256
        for j in range(4):
            row = pl.multiple_of(base + (j - k) % 4 * 64, 64)
            mixed[j * 64 : j * 64 + 64, i * 128 : i * 128 + 128] = ref[pl.ds(row, 64), :]
    state = x_ref[...].astype(f32) + product_nt(mixed[...], w_out[...])
    state_ref[...] = state[:64]
    second_ref[...] = (state * rms_scale(state) * gain_ref[0:1, :]).astype(bf16)


def second_norm(at, mixed, w_out, x, gain):
    count, width = x.shape
    steps = count // 256
    whole = lambda a: pl.BlockSpec(a.shape, lambda b, at: (0,) * a.ndim)
    rows = lambda block: pl.BlockSpec((block, width), lambda b, at: (b, 0))
    return pl.pallas_call(
        state_kernel,
        grid_spec=pltpu.PrefetchScalarGridSpec(
            num_scalar_prefetch=1,
            grid=(steps,),
            in_specs=[whole(p) for p in mixed]
            + [whole(w) for w in w_out]
            + [rows(256), whole(gain)],
            out_specs=[rows(64), rows(256)],
            scratch_shapes=[pltpu.VMEM((width, 1024), bf16), pltpu.VMEM((256, 1024), bf16)],
        ),
        out_shape=[
            jax.ShapeDtypeStruct((steps * 64, width), f32),
            jax.ShapeDtypeStruct((count, width), bf16),
        ],
        compiler_params=pltpu.CompilerParams(vmem_limit_bytes=VMEM),
        cost_estimate=pl.CostEstimate(flops=3 * 10**9, bytes_accessed=10**7, transcendentals=0),
        name="second_norm",
    )(at, *mixed, *w_out, x, gain)


def feed_kernel(second_ref, wf_ref, *refs):
    up_refs = refs[:2]
    inner_ref, low_ref, own_ref, other_ref = refs[2:6]
    up_ref, down_own_ref, down_other_ref, w_gu = refs[6:]
    step = pl.program_id(0)
    side = lax.rem(step, 2)

    @pl.when(step == 0)
    def _():
        for rows in (slice(i, i + 128) for i in range(0, w_gu.shape[0], 128)):
            w_gu[rows, :512] = wf_ref[rows, :512]
            rest = wf_ref[rows, 512:1152].astype(f32)
            w_gu[rows, 512:] = pltpu.roll(rest, 576, 1).astype(bf16)

    for i, ref in enumerate(up_refs):

        @pl.when(side == i)
        def _():
            for j in range(4):
                up_ref[j * 64 : j * 64 + 64, :] = ref[j, 0]

    both = product(second_ref[...], w_gu[...])
    grad_inner = product(up_ref[...], wf_ref[:, 1152:1728])

    def glu(gate, up, grad):
        sig = 1.0 / (1.0 + jnp.exp(-gate))
        silu = gate * sig
        inner = (silu * up).astype(bf16)
        grad_gate = (grad * up * sig * (1.0 + gate * (1.0 - sig))).astype(bf16)
        return inner, grad_gate, (grad * silu).astype(bf16)

    inner, grad_gate, grad_up = glu(both[:, :512], both[:, 512:1024], grad_inner[:, :512])
    inner_ref[:, :512] = inner
    low_ref[:, :512] = grad_gate
    low_ref[:, 512:1024] = grad_up
    tail = both[:, 1024:]
    gate_tail = pltpu.roll(tail, 64, 1)
    inner, grad_gate, grad_up = glu(gate_tail[:, :64], tail[:, :64], grad_inner[:, 512:])
    inner_ref[:, 512:] = inner
    low_ref[:, 1024:1088] = grad_up
    low_ref[:, 1088:] = grad_gate
    grad = product_nt(low_ref[...], w_gu[...]).astype(bf16)
    down = product_nt(inner_ref[...], wf_ref[:, 1152:]).astype(bf16)

    @pl.when(side == 0)
    def _():
        own_ref[0] = grad
        down_own_ref[0] = down

    @pl.when(side == 1)
    def _():
        other_ref[0] = grad
        down_other_ref[0] = down


def feed(second, w_ffn, cotangent):
    count, width = second.shape
    steps = count // 256
    whole = lambda a: pl.BlockSpec(a.shape, lambda b: (0,) * a.ndim)
    rows = lambda cols: pl.BlockSpec((256, cols), lambda b: (b, 0))
    half = pl.BlockSpec((1, 256, width), lambda b: (b // 2, 0, 0))
    chain = pl.BlockSpec((4, 1, 64, width), lambda b: (0, b // 2, 0, 0))
    out = lambda *shape: jax.ShapeDtypeStruct(shape, bf16)
    halves_out = out(steps // 2, 256, width)
    return pl.pallas_call(
        feed_kernel,
        grid=(steps,),
        in_specs=[rows(width), whole(w_ffn), chain, chain],
        out_specs=[rows(576), rows(1152), half, half, rows(width), half, half],
        scratch_shapes=[pltpu.VMEM((width, 1152), bf16)],
        out_shape=[
            *(out(count, 576), out(count, 1152), halves_out, halves_out),
            *(out(count, width), halves_out, halves_out),
        ],
        compiler_params=pltpu.CompilerParams(vmem_limit_bytes=VMEM),
        cost_estimate=pl.CostEstimate(flops=9 * 10**9, bytes_accessed=10**7, transcendentals=10**6),
        name="feed",
    )(second, w_ffn, *cotangent)


def weights_kernel(second_ref, up_ref, low_ref, inner_ref, grad_ref):
    grad = product_tn(second_ref[...], low_ref[...])
    grad_ref[:, :512] = grad[:, :512].astype(bf16)
    grad_ref[:, 512:1152] = pltpu.roll(grad[:, 512:], 64, 1).astype(bf16)
    grad_ref[:, 1152:] = product_tn(up_ref[...], inner_ref[...]).astype(bf16)


def weights_back(second, upstream, low, inner):
    count, width = second.shape
    whole = lambda a: pl.BlockSpec(a.shape, lambda b: (0,) * a.ndim)
    columns = pl.BlockSpec((count, 256), lambda b: (0, b))
    return pl.pallas_call(
        weights_kernel,
        grid=(width // 256,),
        in_specs=[columns, columns, whole(low), whole(inner)],
        out_specs=pl.BlockSpec((256, 1728), lambda b: (b, 0)),
        out_shape=jax.ShapeDtypeStruct((width, 1728), bf16),
        compiler_params=pltpu.CompilerParams(vmem_limit_bytes=VMEM),
        cost_estimate=pl.CostEstimate(flops=4 * 10**9, bytes_accessed=10**7, transcendentals=0),
        name="weights_back",
    )(second, upstream, low, inner)


def back_kernel(*refs):
    state_refs = refs[:8]
    normed_ref, w_ref, raw_ref, q_ref, kk_ref, vv_ref, stat_ref, mixed_ref = refs[8:16]
    qk_gain_ref, cos_ref, sin_ref, bias_ref, gain_ref, ffn_ref = refs[16:22]
    own_ref, other_ref, grad_ref = refs[22:25]
    state, low_ref, total, norm_ref, qk_grad_ref = refs[25:]
    step = pl.program_id(0)
    for i, ref in enumerate(state_refs):
        state[i * 64 : i * 64 + 64, :] = ref[0]
    grad_mixed = product(state[...], w_ref[:, 256:]).astype(bf16)
    keys, values = kk_ref[...], vv_ref[...]
    grad_key = jnp.zeros((512, 128), f32)
    grad_value = jnp.zeros((512, 128), f32)
    grad_query = []
    for rows in (slice(0, 256), slice(256, 512)):
        queries, grads = q_ref[rows, :], grad_mixed[rows, :]
        low = halves(queries)
        bias = bias_ref[0, rows, :].astype(f32)
        parts = []
        for head in range(2):
            keep = low == (head == 0)
            one = jnp.where(keep, queries, jnp.zeros_like(queries))
            grad_one = jnp.where(keep, grads, jnp.zeros_like(grads))
            scores = product_nt(one, keys) * 0.125 + bias
            soft = jnp.exp(scores - stat_ref[rows, head * 64 : head * 64 + 1])
            grad_weights = product_nt(grad_one, values)
            center = jnp.sum(soft * grad_weights, axis=-1, keepdims=True)
            grad_scores = (soft * (grad_weights - center)).astype(bf16)
            parts.append(product(grad_scores, keys))
            grad_key = grad_key + product_tn(grad_scores, one)
            grad_value = grad_value + product_tn(soft.astype(bf16), grad_one)
        grad_query.append(jnp.where(halves(parts[0]), parts[0], parts[1]))
    cosine, sine = cos_ref[0], sin_ref[0]

    def prepare_back(grad, raw, gain):
        grad = grad * cosine + turn_back(grad * sine)
        scale = lax.rsqrt(head_mean(raw * raw) + eps)
        unit = raw * scale
        grad_gain = jnp.sum(grad * unit, axis=0, keepdims=True)
        scaled = grad * gain
        return scale * (scaled - unit * head_mean(scaled * unit)), grad_gain

    raw = raw_ref[...]
    grad_q = jnp.concatenate(grad_query, axis=0) * 0.125
    grad_q, gain_q = prepare_back(grad_q, raw[:, :128], qk_gain_ref[0:1, :])
    grad_key = (grad_key + pltpu.roll(grad_key, 64, 1)) * 0.125
    grad_value = grad_value + pltpu.roll(grad_value, 64, 1)
    low = halves(grad_value)
    raw_k = jnp.where(low, raw[:, 128:], 0.0)
    grad_k, gain_k = prepare_back(jnp.where(low, grad_key, 0.0), raw_k, qk_gain_ref[1:2, :])
    low_ref[:, :128] = grad_q.astype(bf16)
    low_ref[:, 128:] = jnp.where(low, grad_k, grad_value).astype(bf16)

    @pl.when(step == 0)
    def _():
        total[...] = jnp.zeros_like(total)
        norm_ref[...] = jnp.zeros_like(norm_ref)
        qk_grad_ref[...] = jnp.zeros_like(qk_grad_ref)

    qk_grad_ref[0:1, :] += gain_q
    qk_grad_ref[1:2, :] += gain_k
    for rows, ref in ((slice(0, 256), own_ref), (slice(256, 512), other_ref)):
        grad = product_nt(low_ref[rows, :], w_ref[:, :256])
        ref[0] = grad.astype(bf16)
        norm_ref[0:1, :] += jnp.sum(grad * normed_ref[rows, :].astype(f32), axis=0, keepdims=True)
    total[:, :256] += product_tn(normed_ref[...], low_ref[...])
    total[:, 256:] += product_tn(state[...], mixed_ref[...])

    @pl.when(step == pl.num_programs(0) - 1)
    def _():
        norm = norm_ref[0:1, :] / gain_ref[0:1, :]
        chunks = [norm[:, i : i + 128] for i in range(0, 1024, 128)]
        chunks += [ffn_ref[0:1, i : i + 128] for i in range(0, 1024, 128)]
        chunks += [qk_grad_ref[0:1, :], qk_grad_ref[1:2, :]]
        lines = [jnp.concatenate(chunks[i : i + 3], axis=1) for i in range(0, 18, 3)]
        lines = jnp.concatenate(lines + [jnp.zeros((10, 384), f32)], axis=0).astype(bf16)
        for i in range(16):
            grad_ref[i, :64, :] = total[i * 64 : i * 64 + 64, :].astype(bf16)
            grad_ref[i, 64:, :] = lines


def back(
    state, normed, w_att, raw, query, keys, values, stat, mixed, qk_gain, cosine, sine, bias, gain, ffn
):
    width = state[0].shape[2]
    micro = state[0].shape[0]
    whole = lambda a: pl.BlockSpec(a.shape, lambda m: (0,) * a.ndim)
    part = lambda a: pl.BlockSpec((1,) + a.shape[1:], lambda m: (m, 0, 0))
    rows = lambda a: pl.BlockSpec((512, a.shape[1]), lambda m: (m, 0))
    half = pl.BlockSpec((1, 256, width), lambda m: (m, 0, 0))
    out = jax.ShapeDtypeStruct
    return pl.pallas_call(
        back_kernel,
        grid=(micro,),
        in_specs=[part(p) for p in state]
        + [rows(normed), whole(w_att), rows(raw), rows(query), rows(keys), rows(values)]
        + [rows(stat), rows(mixed), whole(qk_gain), part(cosine), part(sine), part(bias)]
        + [whole(gain), whole(ffn)],
        out_specs=[half, half, pl.BlockSpec((16, 80, 384), lambda m: (0, 0, 0))],
        scratch_shapes=[
            pltpu.VMEM((512, width), bf16),
            pltpu.VMEM((512, 256), bf16),
            pltpu.VMEM((width, 384), f32),
            pltpu.VMEM((8, width), f32),
            pltpu.VMEM((8, 128), f32),
        ],
        out_shape=[
            out((micro, 256, width), bf16),
            out((micro, 256, width), bf16),
            out((16, 80, 384), bf16),
        ],
        compiler_params=pltpu.CompilerParams(vmem_limit_bytes=VMEM),
        cost_estimate=pl.CostEstimate(flops=10**6, bytes_accessed=10**4, transcendentals=0),
        name="back",
    )(
        *(*state, normed, w_att, raw, query, keys, values, stat, mixed),
        *(qk_gain, cosine, sine, bias, gain, ffn),
    )


def split_kernel(*refs):
    count = len(refs) // 2 - 2
    for i in range(count):
        own_ref, got_ref = refs[2 * i], refs[2 * i + 1]
        micro = own_ref.shape[0]
        for k, ref in enumerate(refs[-4:]):
            rows = slice(k * 64, k * 64 + 64)
            value = own_ref[:, rows].astype(f32) + got_ref[:, rows].astype(f32)
            ref[i * micro : (i + 1) * micro] = value.astype(ref.dtype)


def split(own, other, *more):
    micro, _, width = own.shape
    values = (own, other_core(other)) + more
    out = lambda kind: jax.ShapeDtypeStruct((len(values) // 2 * micro, 64, width), kind)
    return pl.pallas_call(
        split_kernel,
        out_shape=[out(f32), out(bf16), out(bf16), out(bf16)],
        compiler_params=pltpu.CompilerParams(vmem_limit_bytes=VMEM),
        name="split",
    )(*values)


def local(
    tokens,
    segment_ids,
    cotangent,
    w_query,
    w_key,
    w_value,
    w_out,
    w_gate,
    w_up,
    w_down,
    norm_gain,
    ffn_gain,
    query_gain,
    key_gain,
):
    micro, own, width = tokens.shape
    head_size = query_gain.shape[0]
    nq = w_query.shape[1]
    nk = w_key.shape[1]
    group = segment_ids.shape[1]
    hidden = w_gate.shape[1]
    z = lax.axis_index("z")
    core = lax.axis_index("core")
    at = jnp.stack([lax.axis_index("y"), lax.axis_index("xh") * 2 + lax.axis_index("xl"), z, core])
    at = at.astype(jnp.int32)

    segment = swap(segment_ids)
    x_own = swap(tokens)
    w_att = jnp.concatenate([w_query, w_key, w_value, w_out.T], axis=1)
    w_att = jnp.concatenate([swap_from_x(w_att, k) for k in range(4)], axis=0)
    w_att, x_own, segment = tie(w_att, x_own, segment)
    x_pieces = from_chain(x_own)
    w_att = [w_att] + [from_y(w_att, k) for k in (1, 2, 3)]
    w_ffn = swap(jnp.concatenate([w_gate, w_up, w_down.T], axis=1))
    cotangent_own = swap(cotangent)

    index = jnp.arange(group, dtype=jnp.int32)
    change = jnp.concatenate(
        [jnp.ones((micro, 1), dtype=bool), segment[:, 1:] != segment[:, :-1]], axis=1
    )
    start = lax.cummax(jnp.where(change, index, 0), axis=1)
    start = ordered(start, z, core, 1)
    index = ordered(index[None], z, core, 1)
    place = (index - start).astype(f32)
    freq = rope_base ** (-(jnp.arange(head_size // 2, dtype=f32) * 2.0 / head_size))
    angle = place[:, :, None] * jnp.tile(freq, 4)
    cosine, sine = jnp.cos(angle), jnp.sin(angle)
    allowed = (start[:, :, None] == start[:, None, :]) & (index[:, :, None] >= index[:, None, :])
    bias = jnp.where(allowed, 0.0, -1e30).astype(bf16)
    qk_gain = jnp.stack([jnp.tile(query_gain, 2), jnp.tile(key_gain, 2)])

    w_ffn, *pieces = tie(w_ffn, *w_att, *x_pieces, cosine, sine, bias, qk_gain, at)
    w_att, x_pieces = pieces[:4], pieces[4:8]
    cosine, sine, bias, qk_gain, at = pieces[8:]
    w_ffn = lax.all_gather(w_ffn, plane, axis=0, tiled=True)
    w_out_chain = from_chain(jnp.concatenate([w[:, nq + 2 * nk :] for w in w_att], axis=0))
    x_chain, x_other = gather_chains(x_pieces)

    mixed, x, normed, w_abs, raw, query, keys, values, stat = attend(
        at, (x_chain, x_other), w_att, norm_gain.reshape(1, width), qk_gain, cosine, sine, bias
    )
    mixed, *chains = tie(mixed, *w_out_chain, *from_chain(cotangent_own))
    w_out_all = gather_chains(chains[:4])
    cotangent_all = gather_chains(chains[4:])
    state, second = second_norm(at, gather(mixed), w_out_all, x, ffn_gain.reshape(1, width))
    inner, gu_low, grad_own, grad_other, upstream, down_own, down_other = feed(
        second, w_ffn, cotangent_all
    )
    down_got = other_core(down_other)
    parts = split(grad_own, grad_other)
    got = [from_z(parts[k], -k) for k in (1, 2, 3)]
    grad_ffn = weights_back(second, upstream, gu_low, inner)
    grad_ffn, *got = tie(grad_ffn, *got)
    grad_ffn = lax.psum_scatter(grad_ffn, plane, scatter_dimension=0, tiled=True)
    grad_second = parts[0] + sum(piece.astype(f32) for piece in got)
    state_own = state.reshape(micro, 2, own, width)[:, 0]
    _, norm_pull = jax.vjp(rms_rows, state_own, ffn_gain)
    grad_state_norm, grad_ffn_gain = norm_pull(grad_second)
    grad_state = (cotangent_own.astype(f32) + grad_state_norm).astype(bf16)
    state_pieces = gather(grad_state)

    grad_own, grad_other, grad_att = back(
        *(state_pieces, normed, w_abs, raw, query, keys, values, stat, mixed, qk_gain),
        *(cosine, sine, bias, norm_gain.reshape(1, width), grad_ffn_gain.reshape(1, width)),
    )
    grad_att = lax.all_to_all(grad_att, plane, 0, 0)
    parts = split(grad_own, grad_other, down_own, down_got)
    got = [from_z(parts[k], -k) for k in (1, 2, 3)]
    grad_att, grad_ffn, *got = tie(grad_att, grad_ffn, *got)
    total = parts[0] + sum(piece.astype(f32) for piece in got)
    _, first_pull = jax.vjp(rms_rows, x_own.astype(f32), norm_gain)
    grad_resid_norm, _ = first_pull(total[:micro])
    input_grad = grad_state.astype(f32) + grad_resid_norm
    results = swap(jnp.concatenate([state_own + total[micro:], input_grad]).astype(bf16))
    grad_att = jnp.sum(grad_att.astype(f32), axis=0)
    gains = group_sum(grad_att[64:70].reshape(-1))
    grad_att = swap(grad_att[:64])
    grad_ffn = swap(grad_ffn.astype(bf16)).astype(f32)
    both = nq + nk
    q_gains = gains[2 * width :]
    return (
        results[:micro],
        results[micro:],
        grad_att[:, :nq],
        grad_att[:, nq:both],
        grad_att[:, both : both + nk],
        grad_att[:, both + nk :].T,
        grad_ffn[:, :hidden],
        grad_ffn[:, hidden : 2 * hidden],
        grad_ffn[:, 2 * hidden :].T,
        gains[:width],
        gains[width : 2 * width],
        q_gains[:head_size] + q_gains[head_size : 2 * head_size],
        q_gains[2 * head_size : 3 * head_size],
    )


def solution(mesh):
    inner = Mesh(mesh.devices.reshape(4, 2, 2, 4, 2), axes)
    dp, mp = ("y", "xh", "core"), ("z", "xl")
    rows = P(None, dp + mp, None)
    weight_in = [P(dp, mp)] * 3 + [P(mp, dp)] + [P(dp, mp)] * 2 + [P(mp, dp)]
    return jax.shard_map(
        local,
        mesh=inner,
        in_specs=tuple([rows, P(None, dp), rows] + weight_in + [P()] * 4),
        out_specs=tuple([rows, rows] + weight_in + [P()] * 4),
        check_vma=False,
    )
```

```python
import jax
import jax.numpy as jnp
from jax import lax
from jax.experimental import pallas as pl
from jax.experimental.pallas import tpu as pltpu
from jax.sharding import Mesh, PartitionSpec as P

eps = 1e-05
rope_base = 1000000.0
axes = ("y", "xh", "core", "z", "xl")
plane = ("y", "xh", "xl")
CORE = [(0, 1), (1, 0)]
bf16 = jnp.bfloat16
f32 = jnp.float32
VMEM = 60 * 2**20


def product(left, right):
    return jnp.dot(left, right, preferred_element_type=jnp.float32)


def product_nt(left, right):
    return lax.dot_general(
        left, right, (((1,), (1,)), ((), ())), preferred_element_type=jnp.float32
    )


def product_tn(left, right):
    return lax.dot_general(
        left, right, (((0,), (0,)), ((), ())), preferred_element_type=jnp.float32
    )


def rms_scale(value):
    return lax.rsqrt(jnp.mean(value * value, axis=-1, keepdims=True) + eps)


def rms_rows(value, gain):
    return value * rms_scale(value) * gain


def swap(value):
    return lax.ppermute(
        value, ("core", "xl"), [(a * 2 + b, b * 2 + a) for a in range(2) for b in range(2)]
    )


def from_z(value, k):
    return lax.ppermute(value, "z", [(z, (z - k) % 4) for z in range(4)])


def swap_from_x(value, k):
    perm = []
    for xh in range(2):
        for a in range(2):
            for b in range(2):
                x = (xh * 2 + a - k) % 4
                perm.append((xh * 4 + a * 2 + b, (x // 2) * 4 + b * 2 + x % 2))
    return lax.ppermute(value, ("xh", "core", "xl"), perm)


def from_y(value, k):
    return lax.ppermute(value, "y", [(y, (y - k) % 4) for y in range(4)])


def other_core(value):
    return lax.ppermute(value, "core", CORE)


def from_chain(value):
    return [value] + [from_z(value, k) for k in (1, 2, 3)]


def gather_chains(pieces):
    chain = jnp.stack(pieces)
    return chain, other_core(chain)


def gather(value):
    chain = tie(*from_chain(value))
    return chain + [other_core(v) for v in chain]


def ordered(value, z, core, axis):
    shape = value.shape
    block = shape[axis] // 8
    v = value.reshape(shape[:axis] + (4, 2, block) + shape[axis + 1 :])
    v = lax.dynamic_slice_in_dim(jnp.concatenate([v, v], axis), z, 4, axis)
    v = lax.dynamic_slice_in_dim(jnp.concatenate([v, v], axis + 1), core, 2, axis + 1)
    return jnp.swapaxes(v, axis, axis + 1).reshape(shape)


def tie(*values):
    return list(lax.optimization_barrier(values))


def halves(value):
    lane = lax.broadcasted_iota(jnp.int32, value.shape, value.ndim - 1)
    return lane < 64


def quarter(value):
    lane = lax.broadcasted_iota(jnp.int32, value.shape, value.ndim - 1)
    return (lane & 32) == 0


def turn(value):
    return jnp.where(quarter(value), -pltpu.roll(value, 96, 1), pltpu.roll(value, 32, 1))


def turn_back(value):
    return jnp.where(quarter(value), pltpu.roll(value, 96, 1), -pltpu.roll(value, 32, 1))


def head_mean(value):
    low = halves(value)
    first = jnp.sum(jnp.where(low, value, 0.0), axis=-1, keepdims=True)
    second = jnp.sum(jnp.where(low, 0.0, value), axis=-1, keepdims=True)
    return jnp.where(low, first, second) * (1.0 / 64)


def attend_kernel(at_ref, *refs):
    x_refs, w_refs = refs[:2], refs[2:6]
    gain_ref, qk_gain_ref, cos_ref, sin_ref, bias_ref = refs[6:11]
    mixed_ref, x_ref, normed_ref, w_ref, raw_ref, q_ref, kk_ref, vv_ref, stat_ref = refs[11:]

    @pl.when(pl.program_id(0) == 0)
    def _():
        for ky in range(4):
            for kx in range(4):
                row = lax.rem(at_ref[0] + ky, 4) * 256 + lax.rem(at_ref[1] + kx, 4) * 64
                row = pl.multiple_of(row, 64)
                w_ref[pl.ds(row, 64), :] = w_refs[ky][kx * 64 : kx * 64 + 64, :]

    for i in range(8):
        block = x_refs[i // 4][i % 4, 0]
        x_ref[i * 64 : i * 64 + 64, :] = block
        block = block.astype(f32)
        normed_ref[i * 64 : i * 64 + 64, :] = (
            block * rms_scale(block) * gain_ref[0:1, :]
        ).astype(bf16)
    raw = product(normed_ref[...], w_ref[:, :256])
    raw_ref[...] = raw
    cosine, sine = cos_ref[0], sin_ref[0]
    query, kv = raw[:, :128], raw[:, 128:]
    low = halves(kv)
    query = query * lax.rsqrt(head_mean(query * query) + eps) * qk_gain_ref[0:1, :]
    q_ref[...] = (query * cosine + turn(query) * sine).astype(bf16)
    key = kv * lax.rsqrt(head_mean(kv * kv) + eps) * qk_gain_ref[1:2, :]
    key = key * cosine + turn(key) * sine
    kk_ref[...] = jnp.where(low, key, pltpu.roll(key, 64, 1)).astype(bf16)
    vv_ref[...] = jnp.where(low, pltpu.roll(kv, 64, 1), kv).astype(bf16)
    keys, values = kk_ref[...], vv_ref[...]
    for rows in (slice(0, 256), slice(256, 512)):
        queries = q_ref[rows, :]
        low = halves(queries)
        bias = bias_ref[0, rows, :].astype(f32)
        parts = []
        for head in range(2):
            one = jnp.where(low == (head == 0), queries, jnp.zeros_like(queries))
            scores = product_nt(one, keys) * 0.125 + bias
            top = jnp.max(scores, axis=-1, keepdims=True)
            expo = jnp.exp(scores - top)
            total = jnp.sum(expo, axis=-1, keepdims=True)
            weights = (expo * (1.0 / total)).astype(bf16)
            parts.append((product(weights, values), top + jnp.log(total)))
        first = halves(parts[0][0])
        mixed_ref[rows, :] = jnp.where(first, parts[0][0], parts[1][0]).astype(bf16)
        stat_ref[rows, :] = jnp.where(first, parts[0][1], parts[1][1])


def attend(at, pieces, weights, gain, qk_gain, cosine, sine, bias):
    width = pieces[0].shape[3]
    micro = pieces[0].shape[1]
    group = 512
    chain = pl.BlockSpec((4, 1, 64, width), lambda m, at: (0, m, 0, 0))
    whole = lambda a: pl.BlockSpec(a.shape, lambda m, at: (0,) * a.ndim)
    part = lambda a: pl.BlockSpec((1,) + a.shape[1:], lambda m, at: (m, 0, 0))
    rows = lambda cols: pl.BlockSpec((group, cols), lambda m, at: (m, 0))
    out = lambda cols, kind: jax.ShapeDtypeStruct((micro * group, cols), kind)
    return pl.pallas_call(
        attend_kernel,
        grid_spec=pltpu.PrefetchScalarGridSpec(
            num_scalar_prefetch=1,
            grid=(micro,),
            in_specs=[chain, chain]
            + [whole(w) for w in weights]
            + [whole(gain), whole(qk_gain), part(cosine), part(sine), part(bias)],
            out_specs=[
                rows(128),
                rows(width),
                rows(width),
                pl.BlockSpec((width, 384), lambda m, at: (0, 0)),
                rows(256),
                rows(128),
                rows(128),
                rows(128),
                rows(128),
            ],
        ),
        out_shape=[
            out(128, bf16),
            out(width, bf16),
            out(width, bf16),
            jax.ShapeDtypeStruct((width, 384), bf16),
            out(256, f32),
            out(128, bf16),
            out(128, bf16),
            out(128, bf16),
            out(128, f32),
        ],
        compiler_params=pltpu.CompilerParams(vmem_limit_bytes=VMEM),
        cost_estimate=pl.CostEstimate(flops=12 * 10**9, bytes_accessed=10**7, transcendentals=10**6),
        name="attend",
    )(at, *pieces, *weights, gain, qk_gain, cosine, sine, bias)


def state_kernel(at_ref, *refs):
    mixed_refs, w_refs = refs[:8], refs[8:10]
    x_ref, gain_ref, state_ref, second_ref, w_out, mixed = refs[10:]
    step = pl.program_id(0)
    micro, side = step // 2, lax.rem(step, 2)

    @pl.when(step == 0)
    def _():
        for i in range(8):
            for ky in range(4):
                for kx in range(4):
                    row = lax.rem(at_ref[0] + ky, 4) * 256 + lax.rem(at_ref[1] + kx, 4) * 64
                    row = pl.multiple_of(row, 64)
                    w_out[pl.ds(row, 64), i * 128 : i * 128 + 128] = w_refs[i // 4][
                        i % 4, ky * 256 + kx * 64 : ky * 256 + kx * 64 + 64, :
                    ]

    for i, ref in enumerate(mixed_refs):
        flip, k = i // 4, i % 4
        base = micro * 512 + lax.rem(side + flip, 2) * 256
        for j in range(4):
            row = pl.multiple_of(base + (j - k) % 4 * 64, 64)
            mixed[j * 64 : j * 64 + 64, i * 128 : i * 128 + 128] = ref[pl.ds(row, 64), :]
    state = x_ref[...].astype(f32) + product_nt(mixed[...], w_out[...])
    state_ref[...] = state[:64]
    second_ref[...] = (state * rms_scale(state) * gain_ref[0:1, :]).astype(bf16)


def second_norm(at, mixed, w_out, x, gain):
    count, width = x.shape
    steps = count // 256
    whole = lambda a: pl.BlockSpec(a.shape, lambda b, at: (0,) * a.ndim)
    rows = lambda block: pl.BlockSpec((block, width), lambda b, at: (b, 0))
    return pl.pallas_call(
        state_kernel,
        grid_spec=pltpu.PrefetchScalarGridSpec(
            num_scalar_prefetch=1,
            grid=(steps,),
            in_specs=[whole(p) for p in mixed]
            + [whole(w) for w in w_out]
            + [rows(256), whole(gain)],
            out_specs=[rows(64), rows(256)],
            scratch_shapes=[pltpu.VMEM((width, 1024), bf16), pltpu.VMEM((256, 1024), bf16)],
        ),
        out_shape=[
            jax.ShapeDtypeStruct((steps * 64, width), f32),
            jax.ShapeDtypeStruct((count, width), bf16),
        ],
        compiler_params=pltpu.CompilerParams(vmem_limit_bytes=VMEM),
        cost_estimate=pl.CostEstimate(flops=3 * 10**9, bytes_accessed=10**7, transcendentals=0),
        name="second_norm",
    )(at, *mixed, *w_out, x, gain)


def feed_kernel(second_ref, wf_ref, *refs):
    up_refs = refs[:2]
    inner_ref, low_ref, own_ref, other_ref = refs[2:6]
    up_ref, down_own_ref, down_other_ref, w_gu = refs[6:]
    step = pl.program_id(0)
    side = lax.rem(step, 2)

    @pl.when(step == 0)
    def _():
        for rows in (slice(i, i + 128) for i in range(0, w_gu.shape[0], 128)):
            w_gu[rows, :512] = wf_ref[rows, :512]
            rest = wf_ref[rows, 512:1152].astype(f32)
            w_gu[rows, 512:] = pltpu.roll(rest, 576, 1).astype(bf16)

    for i, ref in enumerate(up_refs):

        @pl.when(side == i)
        def _():
            for j in range(4):
                up_ref[j * 64 : j * 64 + 64, :] = ref[j, 0]

    both = product(second_ref[...], w_gu[...])
    grad_inner = product(up_ref[...], wf_ref[:, 1152:1728])

    def glu(gate, up, grad):
        sig = 1.0 / (1.0 + jnp.exp(-gate))
        silu = gate * sig
        inner = (silu * up).astype(bf16)
        grad_gate = (grad * up * sig * (1.0 + gate * (1.0 - sig))).astype(bf16)
        return inner, grad_gate, (grad * silu).astype(bf16)

    inner, grad_gate, grad_up = glu(both[:, :512], both[:, 512:1024], grad_inner[:, :512])
    inner_ref[:, :512] = inner
    low_ref[:, :512] = grad_gate
    low_ref[:, 512:1024] = grad_up
    tail = both[:, 1024:]
    gate_tail = pltpu.roll(tail, 64, 1)
    inner, grad_gate, grad_up = glu(gate_tail[:, :64], tail[:, :64], grad_inner[:, 512:])
    inner_ref[:, 512:] = inner
    low_ref[:, 1024:1088] = grad_up
    low_ref[:, 1088:] = grad_gate
    grad = product_nt(low_ref[...], w_gu[...]).astype(bf16)
    down = product_nt(inner_ref[...], wf_ref[:, 1152:]).astype(bf16)

    @pl.when(side == 0)
    def _():
        own_ref[0] = grad
        down_own_ref[0] = down

    @pl.when(side == 1)
    def _():
        other_ref[0] = grad
        down_other_ref[0] = down


def feed(second, w_ffn, cotangent):
    count, width = second.shape
    steps = count // 256
    whole = lambda a: pl.BlockSpec(a.shape, lambda b: (0,) * a.ndim)
    rows = lambda cols: pl.BlockSpec((256, cols), lambda b: (b, 0))
    half = pl.BlockSpec((1, 256, width), lambda b: (b // 2, 0, 0))
    chain = pl.BlockSpec((4, 1, 64, width), lambda b: (0, b // 2, 0, 0))
    out = lambda *shape: jax.ShapeDtypeStruct(shape, bf16)
    halves_out = out(steps // 2, 256, width)
    return pl.pallas_call(
        feed_kernel,
        grid=(steps,),
        in_specs=[rows(width), whole(w_ffn), chain, chain],
        out_specs=[rows(576), rows(1152), half, half, rows(width), half, half],
        scratch_shapes=[pltpu.VMEM((width, 1152), bf16)],
        out_shape=[
            *(out(count, 576), out(count, 1152), halves_out, halves_out),
            *(out(count, width), halves_out, halves_out),
        ],
        compiler_params=pltpu.CompilerParams(vmem_limit_bytes=VMEM),
        cost_estimate=pl.CostEstimate(flops=9 * 10**9, bytes_accessed=10**7, transcendentals=10**6),
        name="feed",
    )(second, w_ffn, *cotangent)


def weights_kernel(second_ref, up_ref, low_ref, inner_ref, grad_ref):
    grad = product_tn(second_ref[...], low_ref[...])
    grad_ref[:, :512] = grad[:, :512].astype(bf16)
    grad_ref[:, 512:1152] = pltpu.roll(grad[:, 512:], 64, 1).astype(bf16)
    grad_ref[:, 1152:] = product_tn(up_ref[...], inner_ref[...]).astype(bf16)


def weights_back(second, upstream, low, inner):
    count, width = second.shape
    whole = lambda a: pl.BlockSpec(a.shape, lambda b: (0,) * a.ndim)
    columns = pl.BlockSpec((count, 256), lambda b: (0, b))
    return pl.pallas_call(
        weights_kernel,
        grid=(width // 256,),
        in_specs=[columns, columns, whole(low), whole(inner)],
        out_specs=pl.BlockSpec((256, 1728), lambda b: (b, 0)),
        out_shape=jax.ShapeDtypeStruct((width, 1728), bf16),
        compiler_params=pltpu.CompilerParams(vmem_limit_bytes=VMEM),
        cost_estimate=pl.CostEstimate(flops=4 * 10**9, bytes_accessed=10**7, transcendentals=0),
        name="weights_back",
    )(second, upstream, low, inner)


def back_kernel(*refs):
    state_refs = refs[:8]
    normed_ref, w_ref, raw_ref, q_ref, kk_ref, vv_ref, stat_ref, mixed_ref = refs[8:16]
    qk_gain_ref, cos_ref, sin_ref, bias_ref, gain_ref, ffn_ref = refs[16:22]
    own_ref, other_ref, grad_ref = refs[22:25]
    state, low_ref, total, norm_ref, qk_grad_ref = refs[25:]
    step = pl.program_id(0)
    for i, ref in enumerate(state_refs):
        state[i * 64 : i * 64 + 64, :] = ref[0]
    grad_mixed = product(state[...], w_ref[:, 256:]).astype(bf16)
    keys, values = kk_ref[...], vv_ref[...]
    grad_key = jnp.zeros((512, 128), f32)
    grad_value = jnp.zeros((512, 128), f32)
    grad_query = []
    for rows in (slice(0, 256), slice(256, 512)):
        queries, grads = q_ref[rows, :], grad_mixed[rows, :]
        low = halves(queries)
        bias = bias_ref[0, rows, :].astype(f32)
        parts = []
        for head in range(2):
            keep = low == (head == 0)
            one = jnp.where(keep, queries, jnp.zeros_like(queries))
            grad_one = jnp.where(keep, grads, jnp.zeros_like(grads))
            scores = product_nt(one, keys) * 0.125 + bias
            soft = jnp.exp(scores - stat_ref[rows, head * 64 : head * 64 + 1])
            grad_weights = product_nt(grad_one, values)
            center = jnp.sum(soft * grad_weights, axis=-1, keepdims=True)
            grad_scores = (soft * (grad_weights - center)).astype(bf16)
            parts.append(product(grad_scores, keys))
            grad_key = grad_key + product_tn(grad_scores, one)
            grad_value = grad_value + product_tn(soft.astype(bf16), grad_one)
        grad_query.append(jnp.where(halves(parts[0]), parts[0], parts[1]))
    cosine, sine = cos_ref[0], sin_ref[0]

    def prepare_back(grad, raw, gain):
        grad = grad * cosine + turn_back(grad * sine)
        scale = lax.rsqrt(head_mean(raw * raw) + eps)
        unit = raw * scale
        grad_gain = jnp.sum(grad * unit, axis=0, keepdims=True)
        scaled = grad * gain
        return scale * (scaled - unit * head_mean(scaled * unit)), grad_gain

    raw = raw_ref[...]
    grad_q = jnp.concatenate(grad_query, axis=0) * 0.125
    grad_q, gain_q = prepare_back(grad_q, raw[:, :128], qk_gain_ref[0:1, :])
    grad_key = (grad_key + pltpu.roll(grad_key, 64, 1)) * 0.125
    grad_value = grad_value + pltpu.roll(grad_value, 64, 1)
    low = halves(grad_value)
    raw_k = jnp.where(low, raw[:, 128:], 0.0)
    grad_k, gain_k = prepare_back(jnp.where(low, grad_key, 0.0), raw_k, qk_gain_ref[1:2, :])
    low_ref[:, :128] = grad_q.astype(bf16)
    low_ref[:, 128:] = jnp.where(low, grad_k, grad_value).astype(bf16)

    @pl.when(step == 0)
    def _():
        total[...] = jnp.zeros_like(total)
        norm_ref[...] = jnp.zeros_like(norm_ref)
        qk_grad_ref[...] = jnp.zeros_like(qk_grad_ref)

    qk_grad_ref[0:1, :] += gain_q
    qk_grad_ref[1:2, :] += gain_k
    for rows, ref in ((slice(0, 256), own_ref), (slice(256, 512), other_ref)):
        grad = product_nt(low_ref[rows, :], w_ref[:, :256])
        ref[0] = grad.astype(bf16)
        norm_ref[0:1, :] += jnp.sum(grad * normed_ref[rows, :].astype(f32), axis=0, keepdims=True)
    total[:, :256] += product_tn(normed_ref[...], low_ref[...])
    total[:, 256:] += product_tn(state[...], mixed_ref[...])

    @pl.when(step == pl.num_programs(0) - 1)
    def _():
        norm = norm_ref[0:1, :] / gain_ref[0:1, :]
        chunks = [norm[:, i : i + 128] for i in range(0, 1024, 128)]
        chunks += [ffn_ref[0:1, i : i + 128] for i in range(0, 1024, 128)]
        chunks += [qk_grad_ref[0:1, :], qk_grad_ref[1:2, :]]
        lines = [jnp.concatenate(chunks[i : i + 3], axis=1) for i in range(0, 18, 3)]
        lines = jnp.concatenate(lines + [jnp.zeros((10, 384), f32)], axis=0).astype(bf16)
        for i in range(16):
            grad_ref[i, :64, :] = total[i * 64 : i * 64 + 64, :].astype(bf16)
            grad_ref[i, 64:, :] = lines


def back(
    state, normed, w_att, raw, query, keys, values, stat, mixed, qk_gain, cosine, sine, bias, gain, ffn
):
    width = state[0].shape[2]
    micro = state[0].shape[0]
    whole = lambda a: pl.BlockSpec(a.shape, lambda m: (0,) * a.ndim)
    part = lambda a: pl.BlockSpec((1,) + a.shape[1:], lambda m: (m, 0, 0))
    rows = lambda a: pl.BlockSpec((512, a.shape[1]), lambda m: (m, 0))
    half = pl.BlockSpec((1, 256, width), lambda m: (m, 0, 0))
    out = jax.ShapeDtypeStruct
    return pl.pallas_call(
        back_kernel,
        grid=(micro,),
        in_specs=[part(p) for p in state]
        + [rows(normed), whole(w_att), rows(raw), rows(query), rows(keys), rows(values)]
        + [rows(stat), rows(mixed), whole(qk_gain), part(cosine), part(sine), part(bias)]
        + [whole(gain), whole(ffn)],
        out_specs=[half, half, pl.BlockSpec((16, 80, 384), lambda m: (0, 0, 0))],
        scratch_shapes=[
            pltpu.VMEM((512, width), bf16),
            pltpu.VMEM((512, 256), bf16),
            pltpu.VMEM((width, 384), f32),
            pltpu.VMEM((8, width), f32),
            pltpu.VMEM((8, 128), f32),
        ],
        out_shape=[
            out((micro, 256, width), bf16),
            out((micro, 256, width), bf16),
            out((16, 80, 384), bf16),
        ],
        compiler_params=pltpu.CompilerParams(vmem_limit_bytes=VMEM),
        cost_estimate=pl.CostEstimate(flops=10**6, bytes_accessed=10**4, transcendentals=0),
        name="back",
    )(
        *(*state, normed, w_att, raw, query, keys, values, stat, mixed),
        *(qk_gain, cosine, sine, bias, gain, ffn),
    )


def split_kernel(*refs):
    count = len(refs) // 2 - 2
    for i in range(count):
        own_ref, got_ref = refs[2 * i], refs[2 * i + 1]
        micro = own_ref.shape[0]
        for k, ref in enumerate(refs[-4:]):
            rows = slice(k * 64, k * 64 + 64)
            value = own_ref[:, rows].astype(f32) + got_ref[:, rows].astype(f32)
            ref[i * micro : (i + 1) * micro] = value.astype(ref.dtype)


def split(own, other, *more):
    micro, _, width = own.shape
    values = (own, other_core(other)) + more
    out = lambda kind: jax.ShapeDtypeStruct((len(values) // 2 * micro, 64, width), kind)
    return pl.pallas_call(
        split_kernel,
        out_shape=[out(f32), out(bf16), out(bf16), out(bf16)],
        compiler_params=pltpu.CompilerParams(vmem_limit_bytes=VMEM),
        name="split",
    )(*values)


def local(
    tokens,
    segment_ids,
    cotangent,
    w_query,
    w_key,
    w_value,
    w_out,
    w_gate,
    w_up,
    w_down,
    norm_gain,
    ffn_gain,
    query_gain,
    key_gain,
):
    micro, own, width = tokens.shape
    head_size = query_gain.shape[0]
    nq = w_query.shape[1]
    nk = w_key.shape[1]
    group = segment_ids.shape[1]
    hidden = w_gate.shape[1]
    z = lax.axis_index("z")
    core = lax.axis_index("core")
    at = jnp.stack([lax.axis_index("y"), lax.axis_index("xh") * 2 + lax.axis_index("xl"), z, core])
    at = at.astype(jnp.int32)

    segment = swap(segment_ids)
    x_own = swap(tokens)
    w_att = jnp.concatenate([w_query, w_key, w_value, w_out.T], axis=1)
    w_att = jnp.concatenate([swap_from_x(w_att, k) for k in range(4)], axis=0)
    w_att, x_own, segment = tie(w_att, x_own, segment)
    x_pieces = from_chain(x_own)
    w_att = [w_att] + [from_y(w_att, k) for k in (1, 2, 3)]
    w_ffn = swap(jnp.concatenate([w_gate, w_up, w_down.T], axis=1))
    cotangent_own = swap(cotangent)

    index = jnp.arange(group, dtype=jnp.int32)
    change = jnp.concatenate(
        [jnp.ones((micro, 1), dtype=bool), segment[:, 1:] != segment[:, :-1]], axis=1
    )
    start = lax.cummax(jnp.where(change, index, 0), axis=1)
    start = ordered(start, z, core, 1)
    index = ordered(index[None], z, core, 1)
    place = (index - start).astype(f32)
    freq = rope_base ** (-(jnp.arange(head_size // 2, dtype=f32) * 2.0 / head_size))
    angle = place[:, :, None] * jnp.tile(freq, 4)
    cosine, sine = jnp.cos(angle), jnp.sin(angle)
    allowed = (start[:, :, None] == start[:, None, :]) & (index[:, :, None] >= index[:, None, :])
    bias = jnp.where(allowed, 0.0, -1e30).astype(bf16)
    qk_gain = jnp.stack([jnp.tile(query_gain, 2), jnp.tile(key_gain, 2)])

    w_ffn, *pieces = tie(w_ffn, *w_att, *x_pieces, cosine, sine, bias, qk_gain, at, cotangent_own)
    w_att, x_pieces = pieces[:4], pieces[4:8]
    cosine, sine, bias, qk_gain, at, cotangent_own = pieces[8:]
    w_ffn = lax.all_gather(w_ffn, plane, axis=0, tiled=True)
    w_out_chain = from_chain(jnp.concatenate([w[:, nq + 2 * nk :] for w in w_att], axis=0))
    x_chain, x_other = gather_chains(x_pieces)

    mixed, x, normed, w_abs, raw, query, keys, values, stat = attend(
        at, (x_chain, x_other), w_att, norm_gain.reshape(1, width), qk_gain, cosine, sine, bias
    )
    mixed, *chains = tie(mixed, *w_out_chain, *from_chain(cotangent_own))
    w_out_all = gather_chains(chains[:4])
    cotangent_all = gather_chains(chains[4:])
    state, second = second_norm(at, gather(mixed), w_out_all, x, ffn_gain.reshape(1, width))
    inner, gu_low, grad_own, grad_other, upstream, down_own, down_other = feed(
        second, w_ffn, cotangent_all
    )
    down_got = other_core(down_other)
    parts = split(grad_own, grad_other)
    got = [from_z(parts[k], -k) for k in (1, 2, 3)]
    grad_ffn = weights_back(second, upstream, gu_low, inner)
    grad_ffn, *got = tie(grad_ffn, *got)
    grad_ffn = lax.psum_scatter(grad_ffn, plane, scatter_dimension=0, tiled=True)
    grad_second = parts[0] + sum(piece.astype(f32) for piece in got)
    state_own = state.reshape(micro, 2, own, width)[:, 0]
    _, norm_pull = jax.vjp(rms_rows, state_own, ffn_gain)
    grad_state_norm, grad_ffn_gain = norm_pull(grad_second)
    grad_state = (cotangent_own.astype(f32) + grad_state_norm).astype(bf16)
    state_pieces = gather(grad_state)

    grad_own, grad_other, grad_att = back(
        *(state_pieces, normed, w_abs, raw, query, keys, values, stat, mixed, qk_gain),
        *(cosine, sine, bias, norm_gain.reshape(1, width), grad_ffn_gain.reshape(1, width)),
    )
    grad_att = lax.all_to_all(grad_att, plane, 0, 0)
    parts = split(grad_own, grad_other, down_own, down_got)
    got = [from_z(parts[k], -k) for k in (1, 2, 3)]
    grad_att = jnp.sum(grad_att.astype(f32), axis=0)
    gains = grad_att[64:70].reshape(-1)
    gains, grad_ffn, *got = tie(gains + other_core(gains), grad_ffn, *got)
    total = parts[0] + sum(piece.astype(f32) for piece in got)
    _, first_pull = jax.vjp(rms_rows, x_own.astype(f32), norm_gain)
    grad_resid_norm, _ = first_pull(total[:micro])
    input_grad = grad_state.astype(f32) + grad_resid_norm
    results = swap(jnp.concatenate([state_own + total[micro:], input_grad]).astype(bf16))
    gains = gains + sum(from_z(gains, k) for k in (1, 2, 3))
    grad_att = swap(grad_att[:64])
    grad_ffn = swap(grad_ffn.astype(bf16)).astype(f32)
    both = nq + nk
    q_gains = gains[2 * width :]
    return (
        results[:micro],
        results[micro:],
        grad_att[:, :nq],
        grad_att[:, nq:both],
        grad_att[:, both : both + nk],
        grad_att[:, both + nk :].T,
        grad_ffn[:, :hidden],
        grad_ffn[:, hidden : 2 * hidden],
        grad_ffn[:, 2 * hidden :].T,
        gains[:width],
        gains[width : 2 * width],
        q_gains[:head_size] + q_gains[head_size : 2 * head_size],
        q_gains[2 * head_size : 3 * head_size],
    )


def solution(mesh):
    inner = Mesh(mesh.devices.reshape(4, 2, 2, 4, 2), axes)
    dp, mp = ("y", "xh", "core"), ("z", "xl")
    rows = P(None, dp + mp, None)
    weight_in = [P(dp, mp)] * 3 + [P(mp, dp)] + [P(dp, mp)] * 2 + [P(mp, dp)]
    return jax.shard_map(
        local,
        mesh=inner,
        in_specs=tuple([rows, P(None, dp), rows] + weight_in + [P()] * 4),
        out_specs=tuple([rows, rows] + weight_in + [P()] * 4),
        check_vma=False,
    )
```

```python
import jax
import jax.numpy as jnp
from jax import lax
from jax.experimental import pallas as pl
from jax.experimental.pallas import tpu as pltpu
from jax.sharding import Mesh, PartitionSpec as P

eps = 1e-05
rope_base = 1000000.0
axes = ("y", "xh", "core", "z", "xl")
plane = ("y", "xh", "xl")
CORE = [(0, 1), (1, 0)]
bf16 = jnp.bfloat16
f32 = jnp.float32
VMEM = 60 * 2**20


def product(left, right):
    return jnp.dot(left, right, preferred_element_type=jnp.float32)


def product_nt(left, right):
    return lax.dot_general(
        left, right, (((1,), (1,)), ((), ())), preferred_element_type=jnp.float32
    )


def product_tn(left, right):
    return lax.dot_general(
        left, right, (((0,), (0,)), ((), ())), preferred_element_type=jnp.float32
    )


def rms_scale(value):
    return lax.rsqrt(jnp.mean(value * value, axis=-1, keepdims=True) + eps)


def rms_rows(value, gain):
    return value * rms_scale(value) * gain


def swap(value):
    return lax.ppermute(
        value, ("core", "xl"), [(a * 2 + b, b * 2 + a) for a in range(2) for b in range(2)]
    )


def from_z(value, k):
    return lax.ppermute(value, "z", [(z, (z - k) % 4) for z in range(4)])


def swap_from_x(value, k):
    perm = []
    for xh in range(2):
        for a in range(2):
            for b in range(2):
                x = (xh * 2 + a - k) % 4
                perm.append((xh * 4 + a * 2 + b, (x // 2) * 4 + b * 2 + x % 2))
    return lax.ppermute(value, ("xh", "core", "xl"), perm)


def from_y(value, k):
    return lax.ppermute(value, "y", [(y, (y - k) % 4) for y in range(4)])


def other_core(value):
    return lax.ppermute(value, "core", CORE)


def from_chain(value):
    return [value] + [from_z(value, k) for k in (1, 2, 3)]


def gather_chains(pieces):
    chain = jnp.stack(pieces)
    return chain, other_core(chain)


def gather(value):
    chain = tie(*from_chain(value))
    return chain + [other_core(v) for v in chain]


def ordered(value, z, core, axis):
    shape = value.shape
    block = shape[axis] // 8
    v = value.reshape(shape[:axis] + (4, 2, block) + shape[axis + 1 :])
    v = lax.dynamic_slice_in_dim(jnp.concatenate([v, v], axis), z, 4, axis)
    v = lax.dynamic_slice_in_dim(jnp.concatenate([v, v], axis + 1), core, 2, axis + 1)
    return jnp.swapaxes(v, axis, axis + 1).reshape(shape)


def group_sum(value):
    value = value + other_core(value)
    return value + sum(from_z(value, k) for k in (1, 2, 3))


def tie(*values):
    return list(lax.optimization_barrier(values))


def halves(value):
    lane = lax.broadcasted_iota(jnp.int32, value.shape, value.ndim - 1)
    return lane < 64


def quarter(value):
    lane = lax.broadcasted_iota(jnp.int32, value.shape, value.ndim - 1)
    return (lane & 32) == 0


def turn(value):
    return jnp.where(quarter(value), -pltpu.roll(value, 96, 1), pltpu.roll(value, 32, 1))


def turn_back(value):
    return jnp.where(quarter(value), pltpu.roll(value, 96, 1), -pltpu.roll(value, 32, 1))


def head_mean(value):
    low = halves(value)
    first = jnp.sum(jnp.where(low, value, 0.0), axis=-1, keepdims=True)
    second = jnp.sum(jnp.where(low, 0.0, value), axis=-1, keepdims=True)
    return jnp.where(low, first, second) * (1.0 / 64)


def attend_kernel(at_ref, *refs):
    x_refs, w_refs = refs[:2], refs[2:6]
    gain_ref, qk_gain_ref, cos_ref, sin_ref, bias_ref = refs[6:11]
    mixed_ref, x_ref, normed_ref, w_ref, raw_ref, q_ref, kk_ref, vv_ref, stat_ref = refs[11:]

    @pl.when(pl.program_id(0) == 0)
    def _():
        for ky in range(4):
            for kx in range(4):
                row = lax.rem(at_ref[0] + ky, 4) * 256 + lax.rem(at_ref[1] + kx, 4) * 64
                row = pl.multiple_of(row, 64)
                w_ref[pl.ds(row, 64), :] = w_refs[ky][kx * 64 : kx * 64 + 64, :]

    for i in range(8):
        block = x_refs[i // 4][i % 4, 0]
        x_ref[i * 64 : i * 64 + 64, :] = block
        block = block.astype(f32)
        normed_ref[i * 64 : i * 64 + 64, :] = (
            block * rms_scale(block) * gain_ref[0:1, :]
        ).astype(bf16)
    raw = product(normed_ref[...], w_ref[:, :256])
    raw_ref[...] = raw
    cosine, sine = cos_ref[0], sin_ref[0]
    query, kv = raw[:, :128], raw[:, 128:]
    low = halves(kv)
    query = query * lax.rsqrt(head_mean(query * query) + eps) * qk_gain_ref[0:1, :]
    q_ref[...] = (query * cosine + turn(query) * sine).astype(bf16)
    key = kv * lax.rsqrt(head_mean(kv * kv) + eps) * qk_gain_ref[1:2, :]
    key = key * cosine + turn(key) * sine
    kk_ref[...] = jnp.where(low, key, pltpu.roll(key, 64, 1)).astype(bf16)
    vv_ref[...] = jnp.where(low, pltpu.roll(kv, 64, 1), kv).astype(bf16)
    keys, values = kk_ref[...], vv_ref[...]
    for rows in (slice(0, 256), slice(256, 512)):
        queries = q_ref[rows, :]
        low = halves(queries)
        bias = bias_ref[0, rows, :].astype(f32)
        parts = []
        for head in range(2):
            one = jnp.where(low == (head == 0), queries, jnp.zeros_like(queries))
            scores = product_nt(one, keys) * 0.125 + bias
            top = jnp.max(scores, axis=-1, keepdims=True)
            expo = jnp.exp(scores - top)
            total = jnp.sum(expo, axis=-1, keepdims=True)
            weights = (expo * (1.0 / total)).astype(bf16)
            parts.append((product(weights, values), top + jnp.log(total)))
        first = halves(parts[0][0])
        mixed_ref[rows, :] = jnp.where(first, parts[0][0], parts[1][0]).astype(bf16)
        stat_ref[rows, :] = jnp.where(first, parts[0][1], parts[1][1])


def attend(at, pieces, weights, gain, qk_gain, cosine, sine, bias):
    width = pieces[0].shape[3]
    micro = pieces[0].shape[1]
    group = 512
    chain = pl.BlockSpec((4, 1, 64, width), lambda m, at: (0, m, 0, 0))
    whole = lambda a: pl.BlockSpec(a.shape, lambda m, at: (0,) * a.ndim)
    part = lambda a: pl.BlockSpec((1,) + a.shape[1:], lambda m, at: (m, 0, 0))
    rows = lambda cols: pl.BlockSpec((group, cols), lambda m, at: (m, 0))
    out = lambda cols, kind: jax.ShapeDtypeStruct((micro * group, cols), kind)
    return pl.pallas_call(
        attend_kernel,
        grid_spec=pltpu.PrefetchScalarGridSpec(
            num_scalar_prefetch=1,
            grid=(micro,),
            in_specs=[chain, chain]
            + [whole(w) for w in weights]
            + [whole(gain), whole(qk_gain), part(cosine), part(sine), part(bias)],
            out_specs=[
                rows(128),
                rows(width),
                rows(width),
                pl.BlockSpec((width, 384), lambda m, at: (0, 0)),
                rows(256),
                rows(128),
                rows(128),
                rows(128),
                rows(128),
            ],
        ),
        out_shape=[
            out(128, bf16),
            out(width, bf16),
            out(width, bf16),
            jax.ShapeDtypeStruct((width, 384), bf16),
            out(256, f32),
            out(128, bf16),
            out(128, bf16),
            out(128, bf16),
            out(128, f32),
        ],
        compiler_params=pltpu.CompilerParams(vmem_limit_bytes=VMEM),
        cost_estimate=pl.CostEstimate(flops=12 * 10**9, bytes_accessed=10**7, transcendentals=10**6),
        name="attend",
    )(at, *pieces, *weights, gain, qk_gain, cosine, sine, bias)


def state_kernel(at_ref, *refs):
    mixed_refs, w_refs = refs[:8], refs[8:10]
    x_ref, gain_ref, state_ref, second_ref, w_out, mixed = refs[10:]
    step = pl.program_id(0)
    micro, side = step // 2, lax.rem(step, 2)

    @pl.when(step == 0)
    def _():
        for i in range(8):
            for ky in range(4):
                for kx in range(4):
                    row = lax.rem(at_ref[0] + ky, 4) * 256 + lax.rem(at_ref[1] + kx, 4) * 64
                    row = pl.multiple_of(row, 64)
                    w_out[pl.ds(row, 64), i * 128 : i * 128 + 128] = w_refs[i // 4][
                        i % 4, ky * 256 + kx * 64 : ky * 256 + kx * 64 + 64, :
                    ]

    for i, ref in enumerate(mixed_refs):
        flip, k = i // 4, i % 4
        base = micro * 512 + lax.rem(side + flip, 2) * 256
        for j in range(4):
            row = pl.multiple_of(base + (j - k) % 4 * 64, 64)
            mixed[j * 64 : j * 64 + 64, i * 128 : i * 128 + 128] = ref[pl.ds(row, 64), :]
    state = x_ref[...].astype(f32) + product_nt(mixed[...], w_out[...])
    state_ref[...] = state[:64]
    second_ref[...] = (state * rms_scale(state) * gain_ref[0:1, :]).astype(bf16)


def second_norm(at, mixed, w_out, x, gain):
    count, width = x.shape
    steps = count // 256
    whole = lambda a: pl.BlockSpec(a.shape, lambda b, at: (0,) * a.ndim)
    rows = lambda block: pl.BlockSpec((block, width), lambda b, at: (b, 0))
    return pl.pallas_call(
        state_kernel,
        grid_spec=pltpu.PrefetchScalarGridSpec(
            num_scalar_prefetch=1,
            grid=(steps,),
            in_specs=[whole(p) for p in mixed]
            + [whole(w) for w in w_out]
            + [rows(256), whole(gain)],
            out_specs=[rows(64), rows(256)],
            scratch_shapes=[pltpu.VMEM((width, 1024), bf16), pltpu.VMEM((256, 1024), bf16)],
        ),
        out_shape=[
            jax.ShapeDtypeStruct((steps * 64, width), f32),
            jax.ShapeDtypeStruct((count, width), bf16),
        ],
        compiler_params=pltpu.CompilerParams(vmem_limit_bytes=VMEM),
        cost_estimate=pl.CostEstimate(flops=3 * 10**9, bytes_accessed=10**7, transcendentals=0),
        name="second_norm",
    )(at, *mixed, *w_out, x, gain)


def feed_kernel(second_ref, wf_ref, *refs):
    up_refs = refs[:2]
    inner_ref, low_ref, own_ref, other_ref = refs[2:6]
    up_ref, down_own_ref, down_other_ref, w_gu = refs[6:]
    step = pl.program_id(0)
    side = lax.rem(step, 2)

    @pl.when(step == 0)
    def _():
        for rows in (slice(i, i + 128) for i in range(0, w_gu.shape[0], 128)):
            w_gu[rows, :512] = wf_ref[rows, :512]
            rest = wf_ref[rows, 512:1152].astype(f32)
            w_gu[rows, 512:] = pltpu.roll(rest, 576, 1).astype(bf16)

    for i, ref in enumerate(up_refs):

        @pl.when(side == i)
        def _():
            for j in range(4):
                up_ref[j * 64 : j * 64 + 64, :] = ref[j, 0]

    both = product(second_ref[...], w_gu[...])
    grad_inner = product(up_ref[...], wf_ref[:, 1152:1728])

    def glu(gate, up, grad):
        sig = 1.0 / (1.0 + jnp.exp(-gate))
        silu = gate * sig
        inner = (silu * up).astype(bf16)
        grad_gate = (grad * up * sig * (1.0 + gate * (1.0 - sig))).astype(bf16)
        return inner, grad_gate, (grad * silu).astype(bf16)

    inner, grad_gate, grad_up = glu(both[:, :512], both[:, 512:1024], grad_inner[:, :512])
    inner_ref[:, :512] = inner
    low_ref[:, :512] = grad_gate
    low_ref[:, 512:1024] = grad_up
    tail = both[:, 1024:]
    gate_tail = pltpu.roll(tail, 64, 1)
    inner, grad_gate, grad_up = glu(gate_tail[:, :64], tail[:, :64], grad_inner[:, 512:])
    inner_ref[:, 512:] = inner
    low_ref[:, 1024:1088] = grad_up
    low_ref[:, 1088:] = grad_gate
    grad = product_nt(low_ref[...], w_gu[...]).astype(bf16)
    down = product_nt(inner_ref[...], wf_ref[:, 1152:]).astype(bf16)

    @pl.when(side == 0)
    def _():
        own_ref[0] = grad
        down_own_ref[0] = down

    @pl.when(side == 1)
    def _():
        other_ref[0] = grad
        down_other_ref[0] = down


def feed(second, w_ffn, cotangent):
    count, width = second.shape
    steps = count // 256
    whole = lambda a: pl.BlockSpec(a.shape, lambda b: (0,) * a.ndim)
    rows = lambda cols: pl.BlockSpec((256, cols), lambda b: (b, 0))
    half = pl.BlockSpec((1, 256, width), lambda b: (b // 2, 0, 0))
    chain = pl.BlockSpec((4, 1, 64, width), lambda b: (0, b // 2, 0, 0))
    out = lambda *shape: jax.ShapeDtypeStruct(shape, bf16)
    halves_out = out(steps // 2, 256, width)
    return pl.pallas_call(
        feed_kernel,
        grid=(steps,),
        in_specs=[rows(width), whole(w_ffn), chain, chain],
        out_specs=[rows(576), rows(1152), half, half, rows(width), half, half],
        scratch_shapes=[pltpu.VMEM((width, 1152), bf16)],
        out_shape=[
            *(out(count, 576), out(count, 1152), halves_out, halves_out),
            *(out(count, width), halves_out, halves_out),
        ],
        compiler_params=pltpu.CompilerParams(vmem_limit_bytes=VMEM),
        cost_estimate=pl.CostEstimate(flops=9 * 10**9, bytes_accessed=10**7, transcendentals=10**6),
        name="feed",
    )(second, w_ffn, *cotangent)


def weights_kernel(second_ref, up_ref, low_ref, inner_ref, grad_ref):
    grad = product_tn(second_ref[...], low_ref[...])
    grad_ref[:, :512] = grad[:, :512].astype(bf16)
    grad_ref[:, 512:1152] = pltpu.roll(grad[:, 512:], 64, 1).astype(bf16)
    grad_ref[:, 1152:] = product_tn(up_ref[...], inner_ref[...]).astype(bf16)


def weights_back(second, upstream, low, inner):
    count, width = second.shape
    whole = lambda a: pl.BlockSpec(a.shape, lambda b: (0,) * a.ndim)
    columns = pl.BlockSpec((count, 256), lambda b: (0, b))
    return pl.pallas_call(
        weights_kernel,
        grid=(width // 256,),
        in_specs=[columns, columns, whole(low), whole(inner)],
        out_specs=pl.BlockSpec((256, 1728), lambda b: (b, 0)),
        out_shape=jax.ShapeDtypeStruct((width, 1728), bf16),
        compiler_params=pltpu.CompilerParams(vmem_limit_bytes=VMEM),
        cost_estimate=pl.CostEstimate(flops=4 * 10**9, bytes_accessed=10**7, transcendentals=0),
        name="weights_back",
    )(second, upstream, low, inner)


def back_kernel(*refs):
    state_refs = refs[:8]
    normed_ref, w_ref, raw_ref, q_ref, kk_ref, vv_ref, stat_ref, mixed_ref = refs[8:16]
    qk_gain_ref, cos_ref, sin_ref, bias_ref, gain_ref, ffn_ref = refs[16:22]
    own_ref, other_ref, grad_ref = refs[22:25]
    state, low_ref, total, norm_ref, qk_grad_ref = refs[25:]
    step = pl.program_id(0)
    for i, ref in enumerate(state_refs):
        state[i * 64 : i * 64 + 64, :] = ref[0]
    grad_mixed = product(state[...], w_ref[:, 256:]).astype(bf16)
    keys, values = kk_ref[...], vv_ref[...]
    grad_key = jnp.zeros((512, 128), f32)
    grad_value = jnp.zeros((512, 128), f32)
    grad_query = []
    for rows in (slice(0, 256), slice(256, 512)):
        queries, grads = q_ref[rows, :], grad_mixed[rows, :]
        low = halves(queries)
        bias = bias_ref[0, rows, :].astype(f32)
        parts = []
        for head in range(2):
            keep = low == (head == 0)
            one = jnp.where(keep, queries, jnp.zeros_like(queries))
            grad_one = jnp.where(keep, grads, jnp.zeros_like(grads))
            scores = product_nt(one, keys) * 0.125 + bias
            soft = jnp.exp(scores - stat_ref[rows, head * 64 : head * 64 + 1])
            grad_weights = product_nt(grad_one, values)
            center = jnp.sum(soft * grad_weights, axis=-1, keepdims=True)
            grad_scores = (soft * (grad_weights - center)).astype(bf16)
            parts.append(product(grad_scores, keys))
            grad_key = grad_key + product_tn(grad_scores, one)
            grad_value = grad_value + product_tn(soft.astype(bf16), grad_one)
        grad_query.append(jnp.where(halves(parts[0]), parts[0], parts[1]))
    cosine, sine = cos_ref[0], sin_ref[0]

    def prepare_back(grad, raw, gain):
        grad = grad * cosine + turn_back(grad * sine)
        scale = lax.rsqrt(head_mean(raw * raw) + eps)
        unit = raw * scale
        grad_gain = jnp.sum(grad * unit, axis=0, keepdims=True)
        scaled = grad * gain
        return scale * (scaled - unit * head_mean(scaled * unit)), grad_gain

    raw = raw_ref[...]
    grad_q = jnp.concatenate(grad_query, axis=0) * 0.125
    grad_q, gain_q = prepare_back(grad_q, raw[:, :128], qk_gain_ref[0:1, :])
    grad_key = (grad_key + pltpu.roll(grad_key, 64, 1)) * 0.125
    grad_value = grad_value + pltpu.roll(grad_value, 64, 1)
    low = halves(grad_value)
    raw_k = jnp.where(low, raw[:, 128:], 0.0)
    grad_k, gain_k = prepare_back(jnp.where(low, grad_key, 0.0), raw_k, qk_gain_ref[1:2, :])
    low_ref[:, :128] = grad_q.astype(bf16)
    low_ref[:, 128:] = jnp.where(low, grad_k, grad_value).astype(bf16)

    @pl.when(step == 0)
    def _():
        total[...] = jnp.zeros_like(total)
        norm_ref[...] = jnp.zeros_like(norm_ref)
        qk_grad_ref[...] = jnp.zeros_like(qk_grad_ref)

    qk_grad_ref[0:1, :] += gain_q
    qk_grad_ref[1:2, :] += gain_k
    for rows, ref in ((slice(0, 256), own_ref), (slice(256, 512), other_ref)):
        grad = product_nt(low_ref[rows, :], w_ref[:, :256])
        ref[0] = grad.astype(bf16)
        norm_ref[0:1, :] += jnp.sum(grad * normed_ref[rows, :].astype(f32), axis=0, keepdims=True)
    total[:, :256] += product_tn(normed_ref[...], low_ref[...])
    total[:, 256:] += product_tn(state[...], mixed_ref[...])

    @pl.when(step == pl.num_programs(0) - 1)
    def _():
        norm = norm_ref[0:1, :] / gain_ref[0:1, :]
        chunks = [norm[:, i : i + 128] for i in range(0, 1024, 128)]
        chunks += [ffn_ref[0:1, i : i + 128] for i in range(0, 1024, 128)]
        chunks += [qk_grad_ref[0:1, :], qk_grad_ref[1:2, :]]
        lines = [jnp.concatenate(chunks[i : i + 3], axis=1) for i in range(0, 18, 3)]
        lines = jnp.concatenate(lines + [jnp.zeros((10, 384), f32)], axis=0).astype(bf16)
        for i in range(16):
            grad_ref[i, :64, :] = total[i * 64 : i * 64 + 64, :].astype(bf16)
            grad_ref[i, 64:, :] = lines


def back(
    state, normed, w_att, raw, query, keys, values, stat, mixed, qk_gain, cosine, sine, bias, gain, ffn
):
    width = state[0].shape[2]
    micro = state[0].shape[0]
    whole = lambda a: pl.BlockSpec(a.shape, lambda m: (0,) * a.ndim)
    part = lambda a: pl.BlockSpec((1,) + a.shape[1:], lambda m: (m, 0, 0))
    rows = lambda a: pl.BlockSpec((512, a.shape[1]), lambda m: (m, 0))
    half = pl.BlockSpec((1, 256, width), lambda m: (m, 0, 0))
    out = jax.ShapeDtypeStruct
    return pl.pallas_call(
        back_kernel,
        grid=(micro,),
        in_specs=[part(p) for p in state]
        + [rows(normed), whole(w_att), rows(raw), rows(query), rows(keys), rows(values)]
        + [rows(stat), rows(mixed), whole(qk_gain), part(cosine), part(sine), part(bias)]
        + [whole(gain), whole(ffn)],
        out_specs=[half, half, pl.BlockSpec((16, 80, 384), lambda m: (0, 0, 0))],
        scratch_shapes=[
            pltpu.VMEM((512, width), bf16),
            pltpu.VMEM((512, 256), bf16),
            pltpu.VMEM((width, 384), f32),
            pltpu.VMEM((8, width), f32),
            pltpu.VMEM((8, 128), f32),
        ],
        out_shape=[
            out((micro, 256, width), bf16),
            out((micro, 256, width), bf16),
            out((16, 80, 384), bf16),
        ],
        compiler_params=pltpu.CompilerParams(vmem_limit_bytes=VMEM),
        cost_estimate=pl.CostEstimate(flops=10**6, bytes_accessed=10**4, transcendentals=0),
        name="back",
    )(
        *(*state, normed, w_att, raw, query, keys, values, stat, mixed),
        *(qk_gain, cosine, sine, bias, gain, ffn),
    )


def split_kernel(*refs):
    count = len(refs) // 2 - 2
    for i in range(count):
        own_ref, got_ref = refs[2 * i], refs[2 * i + 1]
        micro = own_ref.shape[0]
        for k, ref in enumerate(refs[-4:]):
            rows = slice(k * 64, k * 64 + 64)
            value = own_ref[:, rows].astype(f32) + got_ref[:, rows].astype(f32)
            ref[i * micro : (i + 1) * micro] = value.astype(ref.dtype)


def split(own, other, *more):
    micro, _, width = own.shape
    values = (own, other_core(other)) + more
    out = lambda kind: jax.ShapeDtypeStruct((len(values) // 2 * micro, 64, width), kind)
    return pl.pallas_call(
        split_kernel,
        out_shape=[out(f32), out(bf16), out(bf16), out(bf16)],
        compiler_params=pltpu.CompilerParams(vmem_limit_bytes=VMEM),
        name="split",
    )(*values)


def local(
    tokens,
    segment_ids,
    cotangent,
    w_query,
    w_key,
    w_value,
    w_out,
    w_gate,
    w_up,
    w_down,
    norm_gain,
    ffn_gain,
    query_gain,
    key_gain,
):
    micro, own, width = tokens.shape
    head_size = query_gain.shape[0]
    nq = w_query.shape[1]
    nk = w_key.shape[1]
    group = segment_ids.shape[1]
    hidden = w_gate.shape[1]
    z = lax.axis_index("z")
    core = lax.axis_index("core")
    at = jnp.stack([lax.axis_index("y"), lax.axis_index("xh") * 2 + lax.axis_index("xl"), z, core])
    at = at.astype(jnp.int32)

    segment = swap(segment_ids)
    x_own = swap(tokens)
    w_att = jnp.concatenate([w_query, w_key, w_value, w_out.T], axis=1)
    w_att = jnp.concatenate([swap_from_x(w_att, k) for k in range(4)], axis=0)
    w_att, x_own, segment = tie(w_att, x_own, segment)
    x_pieces = from_chain(x_own)
    w_att = [w_att] + [from_y(w_att, k) for k in (1, 2, 3)]
    w_ffn = swap(jnp.concatenate([w_gate, w_up, w_down.T], axis=1))
    cotangent_own = swap(cotangent)

    index = jnp.arange(group, dtype=jnp.int32)
    change = jnp.concatenate(
        [jnp.ones((micro, 1), dtype=bool), segment[:, 1:] != segment[:, :-1]], axis=1
    )
    start = lax.cummax(jnp.where(change, index, 0), axis=1)
    start = ordered(start, z, core, 1)
    index = ordered(index[None], z, core, 1)
    place = (index - start).astype(f32)
    freq = rope_base ** (-(jnp.arange(head_size // 2, dtype=f32) * 2.0 / head_size))
    angle = place[:, :, None] * jnp.tile(freq, 4)
    cosine, sine = jnp.cos(angle), jnp.sin(angle)
    allowed = (start[:, :, None] == start[:, None, :]) & (index[:, :, None] >= index[:, None, :])
    bias = jnp.where(allowed, 0.0, -1e30).astype(bf16)
    qk_gain = jnp.stack([jnp.tile(query_gain, 2), jnp.tile(key_gain, 2)])

    w_ffn, *pieces = tie(w_ffn, *w_att, *x_pieces, cosine, sine, bias, qk_gain, at, cotangent_own)
    w_att, x_pieces = pieces[:4], pieces[4:8]
    cosine, sine, bias, qk_gain, at, cotangent_own = pieces[8:]
    w_ffn = lax.all_gather(w_ffn, plane, axis=0, tiled=True)
    w_out_chain = from_chain(jnp.concatenate([w[:, nq + 2 * nk :] for w in w_att], axis=0))
    x_chain, x_other = gather_chains(x_pieces)

    mixed, x, normed, w_abs, raw, query, keys, values, stat = attend(
        at, (x_chain, x_other), w_att, norm_gain.reshape(1, width), qk_gain, cosine, sine, bias
    )
    mixed, *chains = tie(mixed, *w_out_chain, *from_chain(cotangent_own))
    w_out_all = gather_chains(chains[:4])
    cotangent_all = gather_chains(chains[4:])
    state, second = second_norm(at, gather(mixed), w_out_all, x, ffn_gain.reshape(1, width))
    inner, gu_low, grad_own, grad_other, upstream, down_own, down_other = feed(
        second, w_ffn, cotangent_all
    )
    down_got = other_core(down_other)
    parts = split(grad_own, grad_other)
    got = [from_z(parts[k], -k) for k in (1, 2, 3)]
    grad_ffn = weights_back(second, upstream, gu_low, inner)
    grad_ffn, *got = tie(grad_ffn, *got)
    grad_ffn = lax.psum_scatter(grad_ffn, plane, scatter_dimension=0, tiled=True)
    grad_second = parts[0] + sum(piece.astype(f32) for piece in got)
    state_own = state.reshape(micro, 2, own, width)[:, 0]
    _, norm_pull = jax.vjp(rms_rows, state_own, ffn_gain)
    grad_state_norm, grad_ffn_gain = norm_pull(grad_second)
    grad_state = (cotangent_own.astype(f32) + grad_state_norm).astype(bf16)
    state_pieces = gather(grad_state)

    grad_own, grad_other, grad_att = back(
        *(state_pieces, normed, w_abs, raw, query, keys, values, stat, mixed, qk_gain),
        *(cosine, sine, bias, norm_gain.reshape(1, width), grad_ffn_gain.reshape(1, width)),
    )
    grad_att = lax.all_to_all(grad_att, plane, 0, 0)
    parts = split(grad_own, grad_other, down_own, down_got)
    got = [from_z(parts[k], -k) for k in (1, 2, 3)]
    grad_att, grad_ffn, *got = tie(grad_att, grad_ffn, *got)
    total = parts[0] + sum(piece.astype(f32) for piece in got)
    _, first_pull = jax.vjp(rms_rows, x_own.astype(f32), norm_gain)
    grad_resid_norm, _ = first_pull(total[:micro])
    input_grad = grad_state.astype(f32) + grad_resid_norm
    results = swap(jnp.concatenate([state_own + total[micro:], input_grad]).astype(bf16))
    grad_att = jnp.sum(grad_att.astype(f32), axis=0)
    gains = group_sum(grad_att[64:70].reshape(-1))
    grad_att = swap(grad_att[:64])
    grad_ffn = swap(grad_ffn.astype(bf16)).astype(f32)
    both = nq + nk
    q_gains = gains[2 * width :]
    return (
        results[:micro],
        results[micro:],
        grad_att[:, :nq],
        grad_att[:, nq:both],
        grad_att[:, both : both + nk],
        grad_att[:, both + nk :].T,
        grad_ffn[:, :hidden],
        grad_ffn[:, hidden : 2 * hidden],
        grad_ffn[:, 2 * hidden :].T,
        gains[:width],
        gains[width : 2 * width],
        q_gains[:head_size] + q_gains[head_size : 2 * head_size],
        q_gains[2 * head_size : 3 * head_size],
    )


def solution(mesh):
    inner = Mesh(mesh.devices.reshape(4, 2, 2, 4, 2), axes)
    dp, mp = ("y", "xh", "core"), ("z", "xl")
    rows = P(None, dp + mp, None)
    weight_in = [P(dp, mp)] * 3 + [P(mp, dp)] + [P(dp, mp)] * 2 + [P(mp, dp)]
    return jax.shard_map(
        local,
        mesh=inner,
        in_specs=tuple([rows, P(None, dp), rows] + weight_in + [P()] * 4),
        out_specs=tuple([rows, rows] + weight_in + [P()] * 4),
        check_vma=False,
    )
```
